256 devices in a mesh: dom: 32 (over z_lo, y, core), rows: 8 (over x, z_hi).
Axes of the slice: x: 4, y: 4, z: 8 (z_hi: 2, z_lo: 4; z = z_hi * 4 + z_lo), core: 2. Of those that a mesh axis runs over, the one named last changes fastest.
Arguments:
- depth: float32 [64, 128, 1536], P('dom', 'rows'), may hold values from 0.05 to 1.5
- x_flow: float32 [64, 128, 1536], P('dom', 'rows'), may hold values from -2 to 2
- y_flow: float32 [64, 128, 1536], P('dom', 'rows'), may hold values from -2 to 2
- elevation: float32 [128, 1536], P('rows'), may hold values from 0 to 0.5
- roughness: int32 [128, 1536], P('rows'), may hold values from 0 to 7
- wet: int32 [64, 128, 1536], P('dom', 'rows'), may hold values 0 or 1
- ancestors: int32 [64], P('dom'), may hold values from 0 to 63, as said below
Outputs:
- depth_out: float32 [64, 128, 1536], P('dom', 'rows')
- x_out: float32 [64, 128, 1536], P('dom', 'rows')
- y_out: float32 [64, 128, 1536], P('dom', 'rows')
The draws below stay inside these ranges and needn't reach their ends.
Inputs may be any that keep to these rules, and one draw needn't show every extreme that they name: `ancestors`: duplicates allowed; some particle names ancestor 0 and some ancestor 64 - 1.
All inputs are finite; a program needn't handle non-finite values. No bound on the sum of `wet` on one device may be relied on, other than what follows from the above.
Results may differ from the reference program's by a relative error of at most 0.00002.
Values sent between devices are 32-bit elements; how exact they have to be, the bound alone decides.
No kernel may reach another device: no remote copies, remote signals or barrier semaphores. Data moves between devices by JAX's collectives and lax.ppermute only.
A program may use at most 128 MiB of HBM per device.

```python
import jax
import jax.numpy as jnp

COLS = 1536
STEPS = 2
P_SIZE = 64
NR = 128


def draw_ancestors(key, part):
    key = jax.random.fold_in(key, 7)
    first, second, third = jax.random.split(key, 3)
    chosen = jax.random.randint(first, (P_SIZE,), 0, P_SIZE).astype(jnp.int32)
    top_slot = jax.random.randint(second, (), 0, P_SIZE)
    low_slot = (top_slot + 1 + jax.random.randint(third, (), 0, P_SIZE - 1)) % P_SIZE
    chosen = chosen.at[top_slot].set(P_SIZE - 1)
    chosen = chosen.at[low_slot].set(0)
    return chosen.astype(jnp.int32)


def touch_ends(array, key, least, top_value):
    shape = array.shape
    place = [jax.random.randint(jax.random.fold_in(key, axis), (), 0, shape[axis]) for axis in range(len(shape))]
    array = array.at[tuple(place)].set(least)
    longest = shape.index(max(shape))
    place[longest] = (place[longest] + 1) % shape[longest]
    return array.at[tuple(place)].set(top_value)


def shard_levels(rng, dims, cuts, least, high):
    loudness, own = 1.0, jax.random.fold_in(rng, 6)
    for axis_at, shards_of in cuts:
        heights = jnp.exp(jax.random.uniform(jax.random.fold_in(own, axis_at), (shards_of,), jnp.float32, least / len(cuts), high / len(cuts)))
        loudness = loudness * jnp.repeat(heights, dims[axis_at] // shards_of).reshape([-1 if axis == axis_at else 1 for axis in range(len(dims))])
    return loudness


def noise(rng, extent, spread, bound, pieces=(), dtype=jnp.bfloat16):
    factor_of = shard_levels(rng, extent, pieces, -0.22, 0.18) if pieces else 1.0
    entries = jax.random.normal(rng, extent, jnp.float32) * spread * factor_of
    return jnp.minimum(jnp.maximum(entries, -bound), bound).astype(dtype)


def setup_inputs(seed: int = 0) -> dict:
    streams_of = jax.random.split(jax.random.key(seed), 8)
    return {
        "depth": jnp.clip(0.05 + 1.45 * jax.random.uniform(streams_of[0], (P_SIZE, NR, COLS), jnp.float32) ** shard_levels(streams_of[0], (P_SIZE, NR, COLS), ((0, 32), (1, 8)), -0.2, 0.2), 0.05, 1.5),
        "x_flow": noise(streams_of[1], (P_SIZE, NR, COLS), 0.3, 2.0, ((0, 32), (1, 8)), jnp.float32),
        "y_flow": noise(streams_of[2], (P_SIZE, NR, COLS), 0.3, 2.0, ((0, 32), (1, 8)), jnp.float32),
        "elevation": jnp.clip(0.5 * jax.random.uniform(streams_of[3], (NR, COLS), jnp.float32) ** shard_levels(streams_of[3], (NR, COLS), ((0, 8),), -0.2, 0.2), 0.0, 0.5),
        "roughness": touch_ends(jax.random.randint(streams_of[4], (NR, COLS), 0, 8), jax.random.fold_in(streams_of[4], 1), 0, 7).astype(jnp.int32),
        "wet": touch_ends((jax.random.randint(streams_of[5], (P_SIZE, NR, COLS), 0, 4) < 3).astype(jnp.int32), jax.random.fold_in(streams_of[5], 1), 0, 1),
        "ancestors": draw_ancestors(jax.random.fold_in(streams_of[7], 71), 0),
    }


gravity = 9.81
time_step = 1.0
spacing = 10.0
min_depth = 0.05
manning_values = (0.02, 0.025, 0.03, 0.035, 0.045, 0.06, 0.08, 0.1)


def manning_square(roughness):
    total = jnp.zeros(roughness.shape, jnp.float32)
    for klass in range(8):
        value = manning_values[klass] * manning_values[klass]
        total = total + jnp.where(roughness == klass, jnp.float32(value), jnp.float32(0.0))
    return total


def face_flux(old_flux, level_a, level_b, bed_a, bed_b, rough_sq):
    flow_depth = jnp.maximum(level_a, level_b) - jnp.maximum(bed_a, bed_b)
    eff_depth = jnp.maximum(flow_depth, min_depth)
    slope = (level_b - level_a) / spacing
    numer = old_flux - gravity * time_step * eff_depth * slope
    denom = 1.0 + gravity * time_step * rough_sq * jnp.abs(old_flux) / jnp.power(eff_depth, 7.0 / 3.0)
    return numer / denom


def reference(depth, x_flow, y_flow, elevation, roughness, wet, ancestors):
    masked = depth * wet.astype(jnp.float32)
    water = masked[ancestors]
    flow_x = x_flow[ancestors]
    flow_y = y_flow[ancestors]
    rough_sq = manning_square(roughness)
    total_rows = water.shape[1]
    zero_col = jnp.zeros((water.shape[0], water.shape[1], 1), jnp.float32)
    zero_row = jnp.zeros((water.shape[0], 1, water.shape[2]), jnp.float32)
    bed_next = jnp.concatenate([elevation[1:], jnp.zeros((1, elevation.shape[1]), jnp.float32)], axis=0)
    row_valid = (jnp.arange(total_rows) < total_rows - 1)[None, :, None]
    for step in range(STEPS):
        level = elevation[None] + water
        faces_x = face_flux(flow_x[..., :-1], level[..., :-1], level[..., 1:],
                            elevation[None, :, :-1], elevation[None, :, 1:], rough_sq[None, :, :-1])
        new_x = jnp.concatenate([faces_x, zero_col], axis=2)
        level_next = jnp.concatenate([level[:, 1:], zero_row], axis=1)
        faces_y = face_flux(flow_y, level, level_next, elevation[None], bed_next[None], rough_sq[None])
        new_y = jnp.where(row_valid, faces_y, jnp.float32(0.0))
        x_left = jnp.concatenate([zero_col, new_x[..., :-1]], axis=2)
        y_above = jnp.concatenate([zero_row, new_y[:, :-1]], axis=1)
        water = water + (time_step / spacing) * ((x_left - new_x) + (y_above - new_y))
        flow_x = new_x
        flow_y = new_y
    return water, flow_x, flow_y
```

```python
import functools

import jax
import jax.numpy as jnp
from jax import lax
from jax.experimental import pallas as pl
from jax.experimental.pallas import tpu as pltpu
from jax.sharding import PartitionSpec as P

GDT = 9.81 * 1.0
SPACING = 10.0
RATIO = 1.0 / 10.0
MIN_DEPTH = 0.05
MANNING = (0.02, 0.025, 0.03, 0.035, 0.045, 0.06, 0.08, 0.1)
ROWS, COLS = 16, 1536
NT = COLS // 128
F32 = jnp.float32

ITEMS_A = [(q, f, c) for q in (1, 2) for f in range(3) for c in range(NT) if f < 2 or c < 8]
ITEMS_B = [(q, f, c) for q in (0, 3) for f in range(3) for c in range(NT)] + [
    (q, 2, c) for q in (1, 2) for c in range(8, NT)
]
TA, TB = 4, 5
VMEM = pl.BlockSpec(memory_space=pltpu.VMEM)
SMEM = pl.BlockSpec(memory_space=pltpu.SMEM)


def place():
    dom = lax.axis_index("dom")
    return dom >> 3, (dom >> 1) & 3, dom & 1


def flux(q, eta_a, eta_b, bed, fric):
    he = jnp.maximum(jnp.maximum(eta_a, eta_b) - bed, MIN_DEPTH)
    numer = q - (GDT / SPACING) * he * (eta_b - eta_a)
    denom = 1.0 + fric * jnp.abs(q) * jnp.exp2((-7.0 / 3.0) * jnp.log2(he))
    return numer / denom


def friction(rough):
    total = jnp.zeros(rough.shape, F32)
    for klass, n in enumerate(MANNING):
        total = jnp.where(rough == klass, F32(GDT * (n * n)), total)
    return total


def row_iota():
    return lax.broadcasted_iota(jnp.int32, (ROWS, COLS), 0)


def right_of(v):
    return pltpu.roll(v, COLS - 1, 1)


def left_of(v):
    return pltpu.roll(v, 1, 1)


def below(v):
    return pltpu.roll(v, ROWS - 1, 0)


def above(v):
    return pltpu.roll(v, 1, 0)


def last_col():
    return lax.broadcasted_iota(jnp.int32, (ROWS, COLS), 1) == COLS - 1


def x_faces(q, eta, bed_x, fric):
    return jnp.where(last_col(), 0.0, flux(q, eta, right_of(eta), bed_x, fric))


def pack(items, fields, out, per):
    low = lax.broadcasted_iota(jnp.int32, (8, 128), 0) < 4
    for n, (q, f, c) in enumerate(items):
        r, s = q // 2, q % 2
        a = fields[0][f][8 * r : 8 * r + 8, 128 * c : 128 * c + 128]
        b = fields[1][f][8 * r : 8 * r + 8, 128 * c : 128 * c + 128]
        tile = jnp.where(low, a, pltpu.roll(b, 4, 0)) if s == 0 else jnp.where(low, pltpu.roll(a, 4, 0), b)
        out[n // per, n % per] = tile


def first_kernel(anc, depth, xf, yf, wet, elev, rough, a0, a1, a2, a3, down, up, h1o, x1o, y1o, frico, packed):
    z, y, _ = place()
    bed = elev[...]
    fric = friction(rough[...])
    frico[...] = fric
    bed_x = jnp.maximum(bed, right_of(bed))
    bed_y = jnp.maximum(bed, below(bed))
    row = row_iota()
    last_row = row == ROWS - 1
    down[6:7, :] = bed[ROWS - 1 :]
    down[7:8, :] = fric[ROWS - 1 :]
    up[...] = jnp.zeros_like(up)
    up[4:5, :] = bed[:1]
    fields = []
    for p in range(2):
        h0 = depth[p] * wet[p].astype(F32)
        qx, qy = xf[p], yf[p]
        down[3 * p : 3 * p + 1, :] = h0[ROWS - 1 :]
        down[3 * p + 1 : 3 * p + 2, :] = qy[ROWS - 1 :]
        up[2 * p : 2 * p + 1, :] = h0[:1]
        eta = bed + h0
        qx = x_faces(qx, eta, bed_x, fric)
        qy = jnp.where(last_row, 0.0, flux(qy, eta, below(eta), bed_y, fric))
        h1 = h0 + RATIO * ((left_of(qx) - qx) + (above(qy) - qy))
        down[3 * p + 2 : 3 * p + 3, :] = h1[ROWS - 1 :]
        up[2 * p + 1 : 2 * p + 2, :] = h1[:1]
        h1o[p] = h1
        x1o[p] = qx
        y1o[p] = qy
        eta = bed + h1
        qx = x_faces(qx, eta, bed_x, fric)
        qy = flux(qy, eta, below(eta), bed_y, fric)
        h2 = h1 + RATIO * ((left_of(qx) - qx) + (above(qy) - qy))
        fields.append((h2, qx, qy))
    pack(ITEMS_A, fields, packed, TA)
    sub = lax.broadcasted_iota(jnp.int32, (8, 128), 0)
    lane = lax.broadcasted_iota(jnp.int32, (8, 128), 1)
    at = 2 * lax.axis_index("dom")
    names = jnp.where(
        sub == 0,
        jnp.where(lane == at, anc[0].astype(F32), 0.0) + jnp.where(lane == at + 1, anc[1].astype(F32), 0.0),
        0.0,
    )
    for k, out in enumerate((a0, a1, a2, a3)):
        for j in range(4):
            out[TA * j : TA * j + TA] = packed[(z ^ k) * 4 + (y ^ j)]
        out[4 * TA] = names


def second_kernel(depth, wet, yf, elev, fric_in, h1i, x1i, y1i, down, up, b0, b1, b2, b3, packed, sq, sa, sb, sz, sf):
    z, y, _ = place()
    slab = lax.axis_index("rows")
    bed = elev[...]
    fric = fric_in[...]
    bed_x = jnp.maximum(bed, right_of(bed))
    row = row_iota()
    first_row, last_row = row == 0, row == ROWS - 1
    bed_up, fric_up = down[6:7, :], down[7:8, :]
    bed_dn = up[4:5, :]
    bed_y = jnp.maximum(bed, jnp.where(last_row, bed_dn, below(bed)))
    zero = jnp.zeros((8, COLS), F32)
    for s in (sq, sa, sb, sf):
        s[...] = zero
    sz[...] = zero
    for p in range(2):
        t, b = 2 * p, 2 * p + 1
        top0 = depth[p, 0:1, :] * wet[p, 0:1, :].astype(F32)
        bot0 = depth[p, ROWS - 1 : ROWS, :] * wet[p, ROWS - 1 : ROWS, :].astype(F32)
        sq[t : t + 1, :] = down[3 * p + 1 : 3 * p + 2, :]
        sa[t : t + 1, :] = bed_up + down[3 * p : 3 * p + 1, :]
        sb[t : t + 1, :] = bed[:1] + top0
        sz[t : t + 1, :] = jnp.maximum(bed_up, bed[:1])
        sf[t : t + 1, :] = fric_up
        sq[b : b + 1, :] = yf[p, ROWS - 1 : ROWS, :]
        sa[b : b + 1, :] = bed[ROWS - 1 :] + bot0
        sb[b : b + 1, :] = bed_dn + up[2 * p : 2 * p + 1, :]
        sz[b : b + 1, :] = jnp.maximum(bed[ROWS - 1 :], bed_dn)
        sf[b : b + 1, :] = fric[ROWS - 1 :]
    edge = lax.broadcasted_iota(jnp.int32, (8, COLS), 0) & 1
    dead = ((edge == 0) & (slab == 0)) | ((edge == 1) & (slab == 7))
    q1 = jnp.where(dead, 0.0, flux(sq[...], sa[...], sb[...], sz[...], sf[...]))
    sq[...] = q1
    levels = []
    for p in range(2):
        t, b = 2 * p, 2 * p + 1
        q_top, q_bot = q1[t : t + 1], q1[b : b + 1]
        h1 = h1i[p] + RATIO * jnp.where(first_row, q_top, jnp.where(last_row, -q_bot, 0.0))
        qy1 = jnp.where(last_row, q_bot, y1i[p])
        over = down[3 * p + 2 : 3 * p + 3, :] - RATIO * q_top
        under = up[2 * p + 1 : 2 * p + 2, :] + RATIO * q_bot
        sa[t : t + 1, :] = bed_up + over
        sb[t : t + 1, :] = bed[:1] + h1[:1]
        levels.append((h1, qy1, bed_dn + under))
    q2 = jnp.where(dead, 0.0, flux(q1, sa[...], sb[...], sz[...], sf[...]))
    fields = []
    for p in range(2):
        h1, qy1, eta_dn = levels[p]
        eta = bed + h1
        qx = x_faces(x1i[p], eta, bed_x, fric)
        qy = flux(qy1, eta, jnp.where(last_row, eta_dn, below(eta)), bed_y, fric)
        qy = jnp.where(last_row & (slab == 7), 0.0, qy)
        over = jnp.where(first_row, q2[2 * p : 2 * p + 1], above(qy))
        h2 = h1 + RATIO * ((left_of(qx) - qx) + (over - qy))
        fields.append((h2, qx, qy))
    pack(ITEMS_B, fields, packed, TB)
    for k, out in enumerate((b0, b1, b2, b3)):
        for j in range(4):
            out[TB * j : TB * j + TB] = packed[(z ^ j) * 4 + (y ^ k)]


def select_kernel(per, z_outer, anc, own, other, o0, o1, o2, o3):
    z, y, c = place()
    low = lax.broadcasted_iota(jnp.int32, (per, 8, 128), 1) < 4
    for outer, out in enumerate((o0, o1, o2, o3)):
        for inner in range(4):
            kz, ky = (outer, inner) if z_outer else (inner, outer)
            dest = ((z ^ kz) << 3) | ((y ^ ky) << 1) | c
            halves = []
            for p in range(2):
                name = anc[2 * dest + p]
                sz, sy, sc, slot = name >> 4, (name >> 2) & 3, (name >> 1) & 1, name & 1
                hi, lo = (sz ^ z, sy ^ y) if z_outer else (sy ^ y, sz ^ z)
                base = (hi * 4 + lo) * per
                got = jnp.where(sc == c, own[pl.ds(base, per)], other[pl.ds(base, per)])
                halves.append(jnp.where(slot == p, got, pltpu.roll(got, 4, 1)))
            out[per * inner : per * inner + per] = jnp.where(low, halves[0], halves[1])


def last_kernel(f0, f1, f2, f3, g0, g1, g2, g3, ho, xo, yo, pa, pb):
    z, y, _ = place()
    for kz, ref in enumerate((f0, f1, f2, f3)):
        for ky in range(4):
            pa[(z ^ kz) * 4 + (y ^ ky)] = ref[TA * ky : TA * ky + TA]
    for ky, ref in enumerate((g0, g1, g2, g3)):
        for kz in range(4):
            pb[(z ^ kz) * 4 + (y ^ ky)] = ref[TB * kz : TB * kz + TB]
    low = lax.broadcasted_iota(jnp.int32, (8, 128), 0) < 4
    where = {item: (pa, n // TA, n % TA) for n, item in enumerate(ITEMS_A)}
    where.update({item: (pb, n // TB, n % TB) for n, item in enumerate(ITEMS_B)})
    for f, out in enumerate((ho, xo, yo)):
        for r in range(2):
            for c in range(NT):
                ref, i, t = where[(2 * r, f, c)]
                upper = ref[i, t]
                ref, i, t = where[(2 * r + 1, f, c)]
                lower = ref[i, t]
                out[0, 8 * r : 8 * r + 8, 128 * c : 128 * c + 128] = jnp.where(low, upper, pltpu.roll(lower, 4, 0))
                out[1, 8 * r : 8 * r + 8, 128 * c : 128 * c + 128] = jnp.where(low, pltpu.roll(upper, 4, 0), lower)


def tiles(n):
    return jax.ShapeDtypeStruct((n, 8, 128), F32)


def params():
    return pltpu.CompilerParams(vmem_limit_bytes=32 * 1024 * 1024)


def shift_z(v, k):
    return v if k == 0 else lax.ppermute(v, "dom", [(i, i ^ (k << 3)) for i in range(32)])


def shift_y(v, k):
    return v if k == 0 else lax.ppermute(v, "dom", [(i, i ^ (k << 1)) for i in range(32)])


def other_core(v):
    return lax.ppermute(v, "dom", [(i, i ^ 1) for i in range(32)])


def regroup(parts, per):
    return [jnp.concatenate([p[per * j : per * j + per] for p in parts]) for j in range(4)]


def select(per, z_outer, anc, own, other):
    return pl.pallas_call(
        functools.partial(select_kernel, per, z_outer),
        out_shape=[tiles(4 * per)] * 4,
        in_specs=[SMEM, VMEM, VMEM],
        out_specs=[VMEM] * 4,
        compiler_params=params(),
    )(anc, own, other)


def shards(depth, x_flow, y_flow, elevation, roughness, wet, ancestors):
    state = jax.ShapeDtypeStruct((2, ROWS, COLS), F32)
    strip = jax.ShapeDtypeStruct((8, COLS), F32)
    plane = jax.ShapeDtypeStruct((ROWS, COLS), F32)
    *a, down, up, h1, x1, y1, fric = pl.pallas_call(
        first_kernel,
        out_shape=[tiles(4 * TA + 1)] * 4 + [strip, strip, state, state, state, plane],
        in_specs=[SMEM] + [VMEM] * 6,
        out_specs=[VMEM] * 10,
        scratch_shapes=[pltpu.VMEM((16, TA, 8, 128), F32)],
        compiler_params=params(),
    )(ancestors, depth, x_flow, y_flow, wet, elevation, roughness)
    a = [shift_z(v, k) for k, v in enumerate(a)]
    down = lax.ppermute(down, "rows", [(i, i + 1) for i in range(7)])
    up = lax.ppermute(up, "rows", [(i + 1, i) for i in range(7)])
    names = a[0][4 * TA] + a[1][4 * TA] + a[2][4 * TA] + a[3][4 * TA]
    a = [jnp.concatenate([v, names[None]]) for v in regroup(a, TA)]
    a = [shift_y(v, k) for k, v in enumerate(a)]
    names = a[0][4 * TA] + a[1][4 * TA] + a[2][4 * TA] + a[3][4 * TA]
    held_a = jnp.concatenate([v[: 4 * TA] for v in a] + [names[None]])
    other_a = other_core(held_a)
    anc = (held_a[16 * TA, 0, :64] + other_a[16 * TA, 0, :64]).astype(jnp.int32)
    b = pl.pallas_call(
        second_kernel,
        out_shape=[tiles(4 * TB)] * 4,
        in_specs=[VMEM] * 10,
        out_specs=[VMEM] * 4,
        scratch_shapes=[pltpu.VMEM((16, TB, 8, 128), F32)] + [pltpu.VMEM((8, COLS), F32)] * 5,
        compiler_params=params(),
    )(depth, wet, y_flow, elevation, fric, h1, x1, y1, down, up)
    b = [shift_y(v, k) for k, v in enumerate(b)]
    b = [shift_z(v, k) for k, v in enumerate(regroup(b, TB))]
    held_b = jnp.concatenate(b)
    other_b = other_core(held_b)
    a = select(TA, False, anc, held_a, other_a)
    a = [shift_y(v, k) for k, v in enumerate(a)]
    a = [shift_z(v, k) for k, v in enumerate(regroup(a, TA))]
    b = select(TB, True, anc, held_b, other_b)
    b = [shift_z(v, k) for k, v in enumerate(b)]
    b = [shift_y(v, k) for k, v in enumerate(regroup(b, TB))]
    return tuple(
        pl.pallas_call(
            last_kernel,
            out_shape=[state] * 3,
            in_specs=[VMEM] * 8,
            out_specs=[VMEM] * 3,
            scratch_shapes=[pltpu.VMEM((16, TA, 8, 128), F32), pltpu.VMEM((16, TB, 8, 128), F32)],
            compiler_params=params(),
        )(*a, *b)
    )


def solution(mesh):
    wide = P("dom", "rows", None)
    in_specs = (wide, wide, wide, P("rows", None), P("rows", None), wide, P("dom"))
    return jax.shard_map(shards, mesh=mesh, in_specs=in_specs, out_specs=(wide, wide, wide), check_vma=False)
```

```python
import jax
import jax.numpy as jnp
from jax import lax
from jax.experimental import pallas as pl
from jax.experimental.pallas import tpu as pltpu
from jax.sharding import PartitionSpec as P

GDT = 9.81 * 1.0
SPACING = 10.0
RATIO = 1.0 / 10.0
MIN_DEPTH = 0.05
MANNING = (0.02, 0.025, 0.03, 0.035, 0.045, 0.06, 0.08, 0.1)
ROWS, COLS = 16, 1536
NT = COLS // 128
F32 = jnp.float32

PER = 9
ITEMS = [(q, f, 3 * z + c) for z in range(4) for q in range(4) for f in range(3) for c in range(3)]
VMEM = pl.BlockSpec(memory_space=pltpu.VMEM)
SMEM = pl.BlockSpec(memory_space=pltpu.SMEM)
HBM = pl.BlockSpec(memory_space=pltpu.HBM)


def place():
    dom = lax.axis_index("dom")
    return dom >> 3, (dom >> 1) & 3, dom & 1


def flux(q, eta_a, eta_b, bed, fric):
    he = jnp.maximum(jnp.maximum(eta_a, eta_b) - bed, MIN_DEPTH)
    numer = q - (GDT / SPACING) * he * (eta_b - eta_a)
    denom = 1.0 + fric * jnp.abs(q) * jnp.exp2((-7.0 / 3.0) * jnp.log2(he))
    return numer / denom


def friction(rough):
    total = jnp.zeros(rough.shape, F32)
    for klass, n in enumerate(MANNING):
        total = jnp.where(rough == klass, F32(GDT * (n * n)), total)
    return total


def row_iota():
    return lax.broadcasted_iota(jnp.int32, (ROWS, COLS), 0)


def right_of(v):
    return pltpu.roll(v, COLS - 1, 1)


def left_of(v):
    return pltpu.roll(v, 1, 1)


def below(v):
    return pltpu.roll(v, ROWS - 1, 0)


def above(v):
    return pltpu.roll(v, 1, 0)


def last_col():
    return lax.broadcasted_iota(jnp.int32, (ROWS, COLS), 1) == COLS - 1


def x_faces(q, eta, bed_x, fric):
    return jnp.where(last_col(), 0.0, flux(q, eta, right_of(eta), bed_x, fric))


def chunk_at(z, y, c, outer, inner):
    return jnp.where(c == 0, (z ^ outer) * 4 + (y ^ inner), (z ^ inner) * 4 + (y ^ outer))


def first_kernel(
    depth_in, xf_in, yf_in, wet_in, elev_in, rough_in, keep, give, up, down, h1o, x1o, y1o, frico, bedo,
    depth, xf, yf, wet, elev, rough, sems,
):
    pairs = zip((elev_in, rough_in, depth_in, wet_in, xf_in, yf_in), (elev, rough, depth, wet, xf, yf))
    copies = [pltpu.make_async_copy(src, dst, sems.at[n]) for n, (src, dst) in enumerate(pairs)]
    for copy in copies:
        copy.start()
    for copy in copies:
        copy.wait()
    _, _, c = place()
    bed = elev[...]
    bedo[...] = bed
    fric = friction(rough[...])
    frico[...] = fric
    bed_x = jnp.maximum(bed, right_of(bed))
    bed_y = jnp.maximum(bed, below(bed))
    last_row = row_iota() == ROWS - 1
    down[6:7, :] = bed[ROWS - 1 :]
    down[7:8, :] = fric[ROWS - 1 :]
    up[...] = jnp.zeros_like(up)
    up[4:5, :] = bed[:1]
    for p in range(2):
        h0 = depth[p] * wet[p].astype(F32)
        qx, qy = xf[p], yf[p]
        down[3 * p : 3 * p + 1, :] = h0[ROWS - 1 :]
        down[3 * p + 1 : 3 * p + 2, :] = qy[ROWS - 1 :]
        up[2 * p : 2 * p + 1, :] = h0[:1]
        eta = bed + h0
        qx = x_faces(qx, eta, bed_x, fric)
        qy = jnp.where(last_row, 0.0, flux(qy, eta, below(eta), bed_y, fric))
        h1 = h0 + RATIO * ((left_of(qx) - qx) + (above(qy) - qy))
        down[3 * p + 2 : 3 * p + 3, :] = h1[ROWS - 1 :]
        up[2 * p + 1 : 2 * p + 2, :] = h1[:1]
        h1o[p] = h1
        x1o[p] = qx
        y1o[p] = qy
    keep[...] = jnp.where(c == 0, down[...], up[...])
    give[...] = jnp.where(c == 0, up[...], down[...])


def second_kernel(
    anc, h1i, x1i, y1i, fric_in, elev, own_up, own_down, mine, theirs, o0, o1, o2, o3, packed, sq, sa, sb, sz, sf
):
    z, y, c = place()
    slab = lax.axis_index("rows")
    bed = elev[...]
    fric = fric_in[...]
    down = jnp.where(c == 0, mine[...], theirs[...])
    up = jnp.where(c == 0, theirs[...], mine[...])
    bed_x = jnp.maximum(bed, right_of(bed))
    row = row_iota()
    first_row, last_row = row == 0, row == ROWS - 1
    bed_up, fric_up = down[6:7], down[7:8]
    bed_dn = up[4:5]
    bed_y = jnp.maximum(bed, jnp.where(last_row, bed_dn, below(bed)))
    for s in (sq, sa, sb, sz, sf):
        s[...] = jnp.zeros((8, COLS), F32)
    for p in range(2):
        t, b = 2 * p, 2 * p + 1
        sq[t : t + 1, :] = down[3 * p + 1 : 3 * p + 2]
        sa[t : t + 1, :] = bed_up + down[3 * p : 3 * p + 1]
        sb[t : t + 1, :] = bed[:1] + own_up[2 * p : 2 * p + 1, :]
        sz[t : t + 1, :] = jnp.maximum(bed_up, bed[:1])
        sf[t : t + 1, :] = fric_up
        sq[b : b + 1, :] = own_down[3 * p + 1 : 3 * p + 2, :]
        sa[b : b + 1, :] = bed[ROWS - 1 :] + own_down[3 * p : 3 * p + 1, :]
        sb[b : b + 1, :] = bed_dn + up[2 * p : 2 * p + 1]
        sz[b : b + 1, :] = jnp.maximum(bed[ROWS - 1 :], bed_dn)
        sf[b : b + 1, :] = fric[ROWS - 1 :]
    edge = lax.broadcasted_iota(jnp.int32, (8, COLS), 0) & 1
    dead = ((edge == 0) & (slab == 0)) | ((edge == 1) & (slab == 7))
    q1 = jnp.where(dead, 0.0, flux(sq[...], sa[...], sb[...], sz[...], sf[...]))
    levels = []
    for p in range(2):
        t, b = 2 * p, 2 * p + 1
        q_top, q_bot = q1[t : t + 1], q1[b : b + 1]
        h1 = h1i[p] + RATIO * jnp.where(first_row, q_top, jnp.where(last_row, -q_bot, 0.0))
        qy1 = jnp.where(last_row, q_bot, y1i[p])
        over = down[3 * p + 2 : 3 * p + 3] - RATIO * q_top
        under = up[2 * p + 1 : 2 * p + 2] + RATIO * q_bot
        sa[t : t + 1, :] = bed_up + over
        sb[t : t + 1, :] = bed[:1] + h1[:1]
        levels.append((h1, qy1, bed_dn + under))
    q2 = jnp.where(dead, 0.0, flux(q1, sa[...], sb[...], sz[...], sf[...]))
    fields = []
    for p in range(2):
        h1, qy1, eta_dn = levels[p]
        eta = bed + h1
        qx = x_faces(x1i[p], eta, bed_x, fric)
        qy = flux(qy1, eta, jnp.where(last_row, eta_dn, below(eta)), bed_y, fric)
        qy = jnp.where(last_row & (slab == 7), 0.0, qy)
        over = jnp.where(first_row, q2[2 * p : 2 * p + 1], above(qy))
        h2 = h1 + RATIO * ((left_of(qx) - qx) + (over - qy))
        fields.append((h2, qx, qy))
    low = lax.broadcasted_iota(jnp.int32, (8, 128), 0) < 4
    for n, (q, f, col) in enumerate(ITEMS):
        r, s = q // 2, q % 2
        a = fields[0][f][8 * r : 8 * r + 8, 128 * col : 128 * col + 128]
        b = fields[1][f][8 * r : 8 * r + 8, 128 * col : 128 * col + 128]
        tile = jnp.where(low, a, pltpu.roll(b, 4, 0)) if s == 0 else jnp.where(low, pltpu.roll(a, 4, 0), b)
        packed[n // PER, n % PER] = tile
    sub = lax.broadcasted_iota(jnp.int32, (8, 128), 0)
    lane = lax.broadcasted_iota(jnp.int32, (8, 128), 1)
    at = 2 * lax.axis_index("dom")
    names = jnp.where(lane == at, anc[0].astype(F32), 0.0) + jnp.where(lane == at + 1, anc[1].astype(F32), 0.0)
    names = jnp.where(sub == 0, names, 0.0)
    for k, out in enumerate((o0, o1, o2, o3)):
        for j in range(4):
            out[PER * j : PER * j + PER] = packed[chunk_at(z, y, c, k, j)]
        out[4 * PER] = names


def select_kernel(anc, m0, m1, m2, m3, t0, t1, t2, t3, o0, o1, o2, o3, held):
    z, y, c = place()
    for n, refs in enumerate(((m0, m1, m2, m3), (t0, t1, t2, t3))):
        for j, ref in enumerate(refs):
            held[n, 4 * PER * j : 4 * PER * j + 4 * PER] = ref[: 4 * PER]
    low = lax.broadcasted_iota(jnp.int32, (PER, 8, 128), 1) < 4
    for k, out in enumerate((o0, o1, o2, o3)):
        for j in range(4):
            at = chunk_at(z, y, c, k, j)
            dest = ((at >> 2) << 3) | ((at & 3) << 1) | c
            halves = []
            for p in range(2):
                name = anc[2 * dest + p]
                dz, dy, sc, slot = (name >> 4) ^ z, ((name >> 2) & 3) ^ y, (name >> 1) & 1, name & 1
                base = jnp.where(sc == 0, dy * 4 + dz, dz * 4 + dy) * PER
                got = held[sc ^ c, pl.ds(base, PER)]
                halves.append(jnp.where(slot == p, got, pltpu.roll(got, 4, 1)))
            out[PER * j : PER * j + PER] = jnp.where(low, halves[0], halves[1])


def last_kernel(f0, f1, f2, f3, ho, xo, yo, packed):
    z, y, c = place()
    for j, ref in enumerate((f0, f1, f2, f3)):
        for k in range(4):
            packed[chunk_at(z, y, c, k, j)] = ref[PER * k : PER * k + PER]
    low = lax.broadcasted_iota(jnp.int32, (8, 128), 0) < 4
    where = {item: (n // PER, n % PER) for n, item in enumerate(ITEMS)}
    for f, out in enumerate((ho, xo, yo)):
        for r in range(2):
            for col in range(NT):
                upper = packed[where[(2 * r, f, col)]]
                lower = packed[where[(2 * r + 1, f, col)]]
                at = (slice(8 * r, 8 * r + 8), slice(128 * col, 128 * col + 128))
                out[(0,) + at] = jnp.where(low, upper, pltpu.roll(lower, 4, 0))
                out[(1,) + at] = jnp.where(low, pltpu.roll(upper, 4, 0), lower)


def tiles(n):
    return jax.ShapeDtypeStruct((n, 8, 128), F32)


def params():
    return pltpu.CompilerParams(vmem_limit_bytes=32 * 1024 * 1024)


def outer_step(v, k):
    return v if k == 0 else lax.ppermute(v, "dom", [(i, i ^ (k << (3 if i % 2 == 0 else 1))) for i in range(32)])


def inner_step(v, k):
    return v if k == 0 else lax.ppermute(v, "dom", [(i, i ^ (k << (1 if i % 2 == 0 else 3))) for i in range(32)])


def other_core(v):
    return lax.ppermute(v, "dom", [(i, i ^ 1) for i in range(32)])


def to_slabs(v):
    pairs = [(d * 8 + r, d * 8 + r + (1 if d % 2 == 0 else -1)) for d in range(32) for r in range(8)]
    return lax.ppermute(v, ("dom", "rows"), [(a, b) for a, b in pairs if a // 8 == b // 8 and b >= 0])


def regroup(parts, count=PER):
    return [jnp.concatenate([p[count * j : count * j + count] for p in parts]) for j in range(4)]


def shards(depth, x_flow, y_flow, elevation, roughness, wet, ancestors):
    state = jax.ShapeDtypeStruct((2, ROWS, COLS), F32)
    strip = jax.ShapeDtypeStruct((8, COLS), F32)
    plane = jax.ShapeDtypeStruct((ROWS, COLS), F32)
    vm = lambda s: pltpu.VMEM(s.shape, s.dtype)
    ints = lambda s: pltpu.VMEM(s.shape, jnp.int32)
    keep, give, up, down, h1, x1, y1, fric, bed = pl.pallas_call(
        first_kernel,
        out_shape=[strip] * 4 + [state] * 3 + [plane] * 2,
        in_specs=[HBM] * 6,
        out_specs=[VMEM] * 9,
        scratch_shapes=[vm(state)] * 3 + [ints(state), vm(plane), ints(plane), pltpu.SemaphoreType.DMA((6,))],
        compiler_params=params(),
    )(depth, x_flow, y_flow, wet, elevation, roughness)
    arrived = to_slabs(jnp.concatenate([keep, other_core(give)]))
    mine = arrived[:8]
    theirs = other_core(arrived[8:])
    parts = pl.pallas_call(
        second_kernel,
        out_shape=[tiles(4 * PER + 1)] * 4,
        in_specs=[SMEM] + [VMEM] * 9,
        out_specs=[VMEM] * 4,
        scratch_shapes=[pltpu.VMEM((16, PER, 8, 128), F32)] + [vm(strip)] * 5,
        compiler_params=params(),
    )(ancestors, h1, x1, y1, fric, bed, up, down, mine, theirs)
    parts = [outer_step(v, k) for k, v in enumerate(parts)]
    names = (parts[0][4 * PER] + parts[1][4 * PER]) + (parts[2][4 * PER] + parts[3][4 * PER])
    parts = [jnp.concatenate([v, names[None]]) for v in regroup(parts)]
    parts = [inner_step(v, k) for k, v in enumerate(parts)]
    others = [other_core(v) for v in parts]
    names = sum(v[4 * PER, 0, :64] for v in parts + others).astype(jnp.int32)
    parts = pl.pallas_call(
        select_kernel,
        out_shape=[tiles(4 * PER)] * 4,
        in_specs=[SMEM] + [VMEM] * 8,
        out_specs=[VMEM] * 4,
        scratch_shapes=[pltpu.VMEM((2, 16 * PER, 8, 128), F32)],
        compiler_params=params(),
    )(names, *parts, *others)
    parts = [outer_step(v, k) for k, v in enumerate(parts)]
    parts = [inner_step(v, k) for k, v in enumerate(regroup(parts))]
    return tuple(
        pl.pallas_call(
            last_kernel,
            out_shape=[state] * 3,
            in_specs=[VMEM] * 4,
            out_specs=[VMEM] * 3,
            scratch_shapes=[pltpu.VMEM((16, PER, 8, 128), F32)],
            compiler_params=params(),
        )(*parts)
    )


def solution(mesh):
    wide = P("dom", "rows", None)
    in_specs = (wide, wide, wide, P("rows", None), P("rows", None), wide, P("dom"))
    return jax.shard_map(shards, mesh=mesh, in_specs=in_specs, out_specs=(wide, wide, wide), check_vma=False)
```

```python
import jax
import jax.numpy as jnp
from jax import lax
from jax.experimental import pallas as pl
from jax.experimental.pallas import tpu as pltpu
from jax.sharding import PartitionSpec as P

GDT = 9.81 * 1.0
SPACING = 10.0
RATIO = 1.0 / 10.0
MIN_DEPTH = 0.05
MANNING = (0.02, 0.025, 0.03, 0.035, 0.045, 0.06, 0.08, 0.1)
ROWS, COLS = 16, 1536
NT = COLS // 128
F32 = jnp.float32

PER = 9
STEP_Z = (0, 2, 3, 1)
STEP_Y = (0, 2, 1, 3)
ITEMS = [(q, f, 3 * z + c) for z in range(4) for q in range(4) for f in range(3) for c in range(3)]
VMEM = pl.BlockSpec(memory_space=pltpu.VMEM)
SMEM = pl.BlockSpec(memory_space=pltpu.SMEM)
HBM = pl.BlockSpec(memory_space=pltpu.HBM)


def place():
    dom = lax.axis_index("dom")
    return dom >> 3, (dom >> 1) & 3, dom & 1


def flux(q, eta_a, eta_b, bed, fric):
    he = jnp.maximum(jnp.maximum(eta_a, eta_b) - bed, MIN_DEPTH)
    numer = q - (GDT / SPACING) * he * (eta_b - eta_a)
    denom = 1.0 + fric * jnp.abs(q) * jnp.exp2((-7.0 / 3.0) * jnp.log2(he))
    return numer / denom


def friction(rough):
    total = jnp.zeros(rough.shape, F32)
    for klass, n in enumerate(MANNING):
        total = jnp.where(rough == klass, F32(GDT * (n * n)), total)
    return total


def row_iota():
    return lax.broadcasted_iota(jnp.int32, (ROWS, COLS), 0)


def right_of(v):
    return pltpu.roll(v, COLS - 1, 1)


def left_of(v):
    return pltpu.roll(v, 1, 1)


def below(v):
    return pltpu.roll(v, ROWS - 1, 0)


def above(v):
    return pltpu.roll(v, 1, 0)


def last_col():
    return lax.broadcasted_iota(jnp.int32, (ROWS, COLS), 1) == COLS - 1


def x_faces(q, eta, bed_x, fric):
    return jnp.where(last_col(), 0.0, flux(q, eta, right_of(eta), bed_x, fric))


def chunk_at(z, y, c, outer, inner):
    return jnp.where(
        c == 0,
        (z ^ STEP_Z[outer]) * 4 + (y ^ STEP_Y[inner]),
        (z ^ STEP_Z[inner]) * 4 + (y ^ STEP_Y[outer]),
    )


def step_of(steps, distance):
    found = jnp.int32(0)
    for k in range(1, 4):
        found = jnp.where(distance == steps[k], k, found)
    return found


def first_kernel(
    depth_in, xf_in, yf_in, wet_in, elev_in, rough_in, keep, give, up, down, h1o, x1o, y1o, frico, bedo,
    depth, xf, yf, wet, elev, rough, sems,
):
    pairs = zip((elev_in, rough_in, depth_in, wet_in, xf_in, yf_in), (elev, rough, depth, wet, xf, yf))
    copies = [pltpu.make_async_copy(src, dst, sems.at[n]) for n, (src, dst) in enumerate(pairs)]
    for copy in copies:
        copy.start()
    for copy in copies:
        copy.wait()
    _, _, c = place()
    bed = elev[...]
    bedo[...] = bed
    fric = friction(rough[...])
    frico[...] = fric
    bed_x = jnp.maximum(bed, right_of(bed))
    bed_y = jnp.maximum(bed, below(bed))
    last_row = row_iota() == ROWS - 1
    down[6:7, :] = bed[ROWS - 1 :]
    down[7:8, :] = fric[ROWS - 1 :]
    up[...] = jnp.zeros_like(up)
    up[4:5, :] = bed[:1]
    for p in range(2):
        h0 = depth[p] * wet[p].astype(F32)
        qx, qy = xf[p], yf[p]
        down[3 * p : 3 * p + 1, :] = h0[ROWS - 1 :]
        down[3 * p + 1 : 3 * p + 2, :] = qy[ROWS - 1 :]
        up[2 * p : 2 * p + 1, :] = h0[:1]
        eta = bed + h0
        qx = x_faces(qx, eta, bed_x, fric)
        qy = jnp.where(last_row, 0.0, flux(qy, eta, below(eta), bed_y, fric))
        h1 = h0 + RATIO * ((left_of(qx) - qx) + (above(qy) - qy))
        down[3 * p + 2 : 3 * p + 3, :] = h1[ROWS - 1 :]
        up[2 * p + 1 : 2 * p + 2, :] = h1[:1]
        h1o[p] = h1
        x1o[p] = qx
        y1o[p] = qy
    keep[...] = jnp.where(c == 0, down[...], up[...])
    give[...] = jnp.where(c == 0, up[...], down[...])


def second_kernel(
    anc, h1i, x1i, y1i, fric_in, elev, own_up, own_down, mine, theirs, o0, o1, o2, o3, packed, sq, sa, sb, sz, sf
):
    z, y, c = place()
    slab = lax.axis_index("rows")
    bed = elev[...]
    fric = fric_in[...]
    down = jnp.where(c == 0, mine[...], theirs[...])
    up = jnp.where(c == 0, theirs[...], mine[...])
    bed_x = jnp.maximum(bed, right_of(bed))
    row = row_iota()
    first_row, last_row = row == 0, row == ROWS - 1
    bed_up, fric_up = down[6:7], down[7:8]
    bed_dn = up[4:5]
    bed_y = jnp.maximum(bed, jnp.where(last_row, bed_dn, below(bed)))
    for s in (sq, sa, sb, sz, sf):
        s[...] = jnp.zeros((8, COLS), F32)
    for p in range(2):
        t, b = 2 * p, 2 * p + 1
        sq[t : t + 1, :] = down[3 * p + 1 : 3 * p + 2]
        sa[t : t + 1, :] = bed_up + down[3 * p : 3 * p + 1]
        sb[t : t + 1, :] = bed[:1] + own_up[2 * p : 2 * p + 1, :]
        sz[t : t + 1, :] = jnp.maximum(bed_up, bed[:1])
        sf[t : t + 1, :] = fric_up
        sq[b : b + 1, :] = own_down[3 * p + 1 : 3 * p + 2, :]
        sa[b : b + 1, :] = bed[ROWS - 1 :] + own_down[3 * p : 3 * p + 1, :]
        sb[b : b + 1, :] = bed_dn + up[2 * p : 2 * p + 1]
        sz[b : b + 1, :] = jnp.maximum(bed[ROWS - 1 :], bed_dn)
        sf[b : b + 1, :] = fric[ROWS - 1 :]
    edge = lax.broadcasted_iota(jnp.int32, (8, COLS), 0) & 1
    dead = ((edge == 0) & (slab == 0)) | ((edge == 1) & (slab == 7))
    q1 = jnp.where(dead, 0.0, flux(sq[...], sa[...], sb[...], sz[...], sf[...]))
    levels = []
    for p in range(2):
        t, b = 2 * p, 2 * p + 1
        q_top, q_bot = q1[t : t + 1], q1[b : b + 1]
        h1 = h1i[p] + RATIO * jnp.where(first_row, q_top, jnp.where(last_row, -q_bot, 0.0))
        qy1 = jnp.where(last_row, q_bot, y1i[p])
        over = down[3 * p + 2 : 3 * p + 3] - RATIO * q_top
        under = up[2 * p + 1 : 2 * p + 2] + RATIO * q_bot
        sa[t : t + 1, :] = bed_up + over
        sb[t : t + 1, :] = bed[:1] + h1[:1]
        levels.append((h1, qy1, bed_dn + under))
    q2 = jnp.where(dead, 0.0, flux(q1, sa[...], sb[...], sz[...], sf[...]))
    fields = []
    for p in range(2):
        h1, qy1, eta_dn = levels[p]
        eta = bed + h1
        qx = x_faces(x1i[p], eta, bed_x, fric)
        qy = flux(qy1, eta, jnp.where(last_row, eta_dn, below(eta)), bed_y, fric)
        qy = jnp.where(last_row & (slab == 7), 0.0, qy)
        over = jnp.where(first_row, q2[2 * p : 2 * p + 1], above(qy))
        h2 = h1 + RATIO * ((left_of(qx) - qx) + (over - qy))
        fields.append((h2, qx, qy))
    low = lax.broadcasted_iota(jnp.int32, (8, 128), 0) < 4
    for n, (q, f, col) in enumerate(ITEMS):
        r, s = q // 2, q % 2
        a = fields[0][f][8 * r : 8 * r + 8, 128 * col : 128 * col + 128]
        b = fields[1][f][8 * r : 8 * r + 8, 128 * col : 128 * col + 128]
        tile = jnp.where(low, a, pltpu.roll(b, 4, 0)) if s == 0 else jnp.where(low, pltpu.roll(a, 4, 0), b)
        packed[n // PER, n % PER] = tile
    sub = lax.broadcasted_iota(jnp.int32, (8, 128), 0)
    lane = lax.broadcasted_iota(jnp.int32, (8, 128), 1)
    at = 2 * lax.axis_index("dom")
    names = jnp.where(lane == at, anc[0].astype(F32), 0.0) + jnp.where(lane == at + 1, anc[1].astype(F32), 0.0)
    names = jnp.where(sub == 0, names, 0.0)
    for k, out in enumerate((o0, o1, o2, o3)):
        for j in range(4):
            out[PER * j : PER * j + PER] = packed[chunk_at(z, y, c, k, j)]
        out[4 * PER] = names


def select_kernel(anc, m0, m1, m2, m3, t0, t1, t2, t3, o0, o1, o2, o3, held):
    z, y, c = place()
    for n, refs in enumerate(((m0, m1, m2, m3), (t0, t1, t2, t3))):
        for j, ref in enumerate(refs):
            held[n, 4 * PER * j : 4 * PER * j + 4 * PER] = ref[: 4 * PER]
    low = lax.broadcasted_iota(jnp.int32, (PER, 8, 128), 1) < 4
    for k, out in enumerate((o0, o1, o2, o3)):
        for j in range(4):
            at = chunk_at(z, y, c, k, j)
            dest = ((at >> 2) << 3) | ((at & 3) << 1) | c
            halves = []
            for p in range(2):
                name = anc[2 * dest + p]
                dz, dy, sc, slot = (name >> 4) ^ z, ((name >> 2) & 3) ^ y, (name >> 1) & 1, name & 1
                dz, dy = step_of(STEP_Z, dz), step_of(STEP_Y, dy)
                base = jnp.where(sc == 0, dy * 4 + dz, dz * 4 + dy) * PER
                got = held[sc ^ c, pl.ds(base, PER)]
                halves.append(jnp.where(slot == p, got, pltpu.roll(got, 4, 1)))
            out[PER * j : PER * j + PER] = jnp.where(low, halves[0], halves[1])


def last_kernel(f0, f1, f2, f3, ho, xo, yo, packed):
    z, y, c = place()
    for j, ref in enumerate((f0, f1, f2, f3)):
        for k in range(4):
            packed[chunk_at(z, y, c, k, j)] = ref[PER * k : PER * k + PER]
    low = lax.broadcasted_iota(jnp.int32, (8, 128), 0) < 4
    where = {item: (n // PER, n % PER) for n, item in enumerate(ITEMS)}
    for f, out in enumerate((ho, xo, yo)):
        for r in range(2):
            for col in range(NT):
                upper = packed[where[(2 * r, f, col)]]
                lower = packed[where[(2 * r + 1, f, col)]]
                at = (slice(8 * r, 8 * r + 8), slice(128 * col, 128 * col + 128))
                out[(0,) + at] = jnp.where(low, upper, pltpu.roll(lower, 4, 0))
                out[(1,) + at] = jnp.where(low, pltpu.roll(upper, 4, 0), lower)


def tiles(n):
    return jax.ShapeDtypeStruct((n, 8, 128), F32)


def params():
    return pltpu.CompilerParams(vmem_limit_bytes=32 * 1024 * 1024)


def outer_step(v, k):
    return v if k == 0 else lax.ppermute(v, "dom", [(i, i ^ (STEP_Z[k] << 3 if i % 2 == 0 else STEP_Y[k] << 1)) for i in range(32)])


def inner_step(v, k):
    return v if k == 0 else lax.ppermute(v, "dom", [(i, i ^ (STEP_Y[k] << 1 if i % 2 == 0 else STEP_Z[k] << 3)) for i in range(32)])


def other_core(v):
    return lax.ppermute(v, "dom", [(i, i ^ 1) for i in range(32)])


def to_slabs(v):
    pairs = [(d * 8 + r, d * 8 + r + (1 if d % 2 == 0 else -1)) for d in range(32) for r in range(8)]
    return lax.ppermute(v, ("dom", "rows"), [(a, b) for a, b in pairs if a // 8 == b // 8 and b >= 0])


def regroup(parts, count=PER):
    return [jnp.concatenate([p[count * j : count * j + count] for p in parts]) for j in range(4)]


def shards(depth, x_flow, y_flow, elevation, roughness, wet, ancestors):
    state = jax.ShapeDtypeStruct((2, ROWS, COLS), F32)
    strip = jax.ShapeDtypeStruct((8, COLS), F32)
    plane = jax.ShapeDtypeStruct((ROWS, COLS), F32)
    vm = lambda s: pltpu.VMEM(s.shape, s.dtype)
    ints = lambda s: pltpu.VMEM(s.shape, jnp.int32)
    keep, give, up, down, h1, x1, y1, fric, bed = pl.pallas_call(
        first_kernel,
        out_shape=[strip] * 4 + [state] * 3 + [plane] * 2,
        in_specs=[HBM] * 6,
        out_specs=[VMEM] * 9,
        scratch_shapes=[vm(state)] * 3 + [ints(state), vm(plane), ints(plane), pltpu.SemaphoreType.DMA((6,))],
        compiler_params=params(),
    )(*[pltpu.with_memory_space_constraint(v, pltpu.HBM) for v in (depth, x_flow, y_flow, wet, elevation, roughness)])
    arrived = to_slabs(jnp.concatenate([keep, other_core(give)]))
    mine = arrived[:8]
    theirs = other_core(arrived[8:])
    parts = pl.pallas_call(
        second_kernel,
        out_shape=[tiles(4 * PER + 1)] * 4,
        in_specs=[SMEM] + [VMEM] * 9,
        out_specs=[VMEM] * 4,
        scratch_shapes=[pltpu.VMEM((16, PER, 8, 128), F32)] + [vm(strip)] * 5,
        compiler_params=params(),
    )(ancestors, h1, x1, y1, fric, bed, up, down, mine, theirs)
    parts = [outer_step(v, k) for k, v in enumerate(parts)]
    names = (parts[0][4 * PER] + parts[1][4 * PER]) + (parts[2][4 * PER] + parts[3][4 * PER])
    parts = [jnp.concatenate([v, names[None]]) for v in regroup(parts)]
    parts = [inner_step(v, k) for k, v in enumerate(parts)]
    others = [other_core(v) for v in parts]
    names = sum(v[4 * PER, 0, :64] for v in parts + others).astype(jnp.int32)
    parts = pl.pallas_call(
        select_kernel,
        out_shape=[tiles(4 * PER)] * 4,
        in_specs=[SMEM] + [VMEM] * 8,
        out_specs=[VMEM] * 4,
        scratch_shapes=[pltpu.VMEM((2, 16 * PER, 8, 128), F32)],
        compiler_params=params(),
    )(names, *parts, *others)
    parts = [outer_step(v, k) for k, v in enumerate(parts)]
    parts = [inner_step(v, k) for k, v in enumerate(regroup(parts))]
    return tuple(
        pl.pallas_call(
            last_kernel,
            out_shape=[state] * 3,
            in_specs=[VMEM] * 4,
            out_specs=[VMEM] * 3,
            scratch_shapes=[pltpu.VMEM((16, PER, 8, 128), F32)],
            compiler_params=params(),
        )(*parts)
    )


def solution(mesh):
    wide = P("dom", "rows", None)
    in_specs = (wide, wide, wide, P("rows", None), P("rows", None), wide, P("dom"))
    return jax.shard_map(shards, mesh=mesh, in_specs=in_specs, out_specs=(wide, wide, wide), check_vma=False)
```

```python
import jax
import jax.numpy as jnp
from jax import lax
from jax.experimental import pallas as pl
from jax.experimental.pallas import tpu as pltpu
from jax.sharding import PartitionSpec as P

GDT = 9.81 * 1.0
SPACING = 10.0
RATIO = 1.0 / 10.0
MIN_DEPTH = 0.05
MANNING = (0.02, 0.025, 0.03, 0.035, 0.045, 0.06, 0.08, 0.1)
ROWS, COLS, HALF = 16, 1536, 8
NT = COLS // 128
F32 = jnp.float32

ITEMS_A = [(e, f, t) for e in (1, 2, 3) for f in range(3) for t in range(NT) if (e, f) != (1, 2)]
ITEMS_B = [(0, f, t) for f in range(3) for t in range(NT)] + [(1, 2, t) for t in range(NT)]
PA, PB = 6, 3
PER = PA + PB
AT = {item: (n // PA) * PER + n % PA for n, item in enumerate(ITEMS_A)}
AT.update({item: (n // PB) * PER + PA + n % PB for n, item in enumerate(ITEMS_B)})
STEP_Z = (0, 2, 3, 1)
STEP_Y = (0, 2, 1, 3)
VMEM = pl.BlockSpec(memory_space=pltpu.VMEM)
SMEM = pl.BlockSpec(memory_space=pltpu.SMEM)
HBM = pl.BlockSpec(memory_space=pltpu.HBM)


def place():
    dom = lax.axis_index("dom")
    return dom >> 3, (dom >> 1) & 3, dom & 1


def flux(q, eta_a, eta_b, bed, fric):
    he = jnp.maximum(jnp.maximum(eta_a, eta_b) - bed, MIN_DEPTH)
    numer = q - (GDT / SPACING) * he * (eta_b - eta_a)
    denom = 1.0 + fric * jnp.abs(q) * jnp.exp2((-7.0 / 3.0) * jnp.log2(he))
    return numer / denom


def friction(rough):
    total = jnp.zeros(rough.shape, F32)
    for klass, n in enumerate(MANNING):
        total = jnp.where(rough == klass, F32(GDT * (n * n)), total)
    return total


def right_of(v):
    return pltpu.roll(v, COLS - 1, 1)


def left_of(v):
    return pltpu.roll(v, 1, 1)


def below(v):
    return pltpu.roll(v, v.shape[0] - 1, 0)


def above(v):
    return pltpu.roll(v, 1, 0)


def x_faces(q, eta, bed_x, fric):
    last = lax.broadcasted_iota(jnp.int32, q.shape, 1) == COLS - 1
    return jnp.where(last, 0.0, flux(q, eta, right_of(eta), bed_x, fric))


def chunk_at(z, y, c, outer, inner):
    return jnp.where(
        c == 0,
        (z ^ STEP_Z[outer]) * 4 + (y ^ STEP_Y[inner]),
        (z ^ STEP_Z[inner]) * 4 + (y ^ STEP_Y[outer]),
    )


def step_of(steps, distance):
    found = jnp.int32(0)
    for k in range(1, 4):
        found = jnp.where(distance == steps[k], k, found)
    return found


def first_kernel(
    depth_in, xf_in, yf_in, wet_in, elev_in, rough_in, anc_in, keep, give, kept, given, terrain,
    depth, xf, yf, wet, elev, rough, anc, sems,
):
    pairs = zip(
        (elev_in, rough_in, depth_in, wet_in, xf_in, yf_in, anc_in), (elev, rough, depth, wet, xf, yf, anc)
    )
    copies = [pltpu.make_async_copy(src, dst, sems.at[n]) for n, (src, dst) in enumerate(pairs)]
    for copy in copies:
        copy.start()
    for copy in copies:
        copy.wait()
    _, _, c = place()
    top = c == 0
    bed = elev[...]
    fric = friction(rough[...])
    bed_x = jnp.maximum(bed, right_of(bed))
    bed_y = jnp.maximum(bed, below(bed))
    end = ROWS - 1
    last_row = lax.broadcasted_iota(jnp.int32, (ROWS, COLS), 0) == end
    terrain[0] = jnp.where(top, bed[:HALF], bed[HALF:])
    terrain[1] = jnp.where(top, fric[:HALF], fric[HALF:])
    terrain[2] = jnp.zeros((HALF, COLS), F32)
    terrain[2, 0:1, :] = jnp.where(top, bed[HALF : HALF + 1], bed[HALF - 1 : HALF])
    terrain[2, 1:2, :] = jnp.where(top, fric[HALF : HALF + 1], fric[HALF - 1 : HALF])
    lane = lax.broadcasted_iota(jnp.int32, (1, COLS), 1)
    at = 2 * lax.axis_index("dom")
    names = jnp.where(lane == at, anc[0].astype(F32), 0.0) + jnp.where(lane == at + 1, anc[1].astype(F32), 0.0)
    kept[6] = jnp.zeros((HALF, COLS), F32)
    given[6] = jnp.zeros((HALF, COLS), F32)
    kept[6, 4:5, :] = names
    given[6, 4:5, :] = names

    def edge(row, upper, lower):
        keep[row : row + 1, :] = jnp.where(top, upper, lower)
        give[row : row + 1, :] = jnp.where(top, lower, upper)

    zero = jnp.zeros((1, COLS), F32)
    edge(6, bed[:1], bed[end:])
    edge(7, fric[:1], fric[end:])
    for p in range(2):
        h0 = depth[p] * wet[p].astype(F32)
        qx, qy = xf[p], yf[p]
        edge(p, h0[:1], h0[end:])
        edge(4 + p, zero, qy[end:])
        eta = bed + h0
        qx = x_faces(qx, eta, bed_x, fric)
        qy = jnp.where(last_row, 0.0, flux(qy, eta, below(eta), bed_y, fric))
        h1 = h0 + RATIO * ((left_of(qx) - qx) + (above(qy) - qy))
        edge(2 + p, h1[:1], h1[end:])
        for f, v in enumerate((h1, qx, qy)):
            kept[3 * p + f] = jnp.where(top, v[:HALF], v[HALF:])
            given[3 * p + f] = jnp.where(top, v[HALF:], v[:HALF])
        kept[6, p : p + 1, :] = jnp.where(top, h1[HALF : HALF + 1], h1[HALF - 1 : HALF])
        given[6, p : p + 1, :] = jnp.where(top, h1[HALF - 1 : HALF], h1[HALF : HALF + 1])
        kept[6, 2 + p : 3 + p, :] = jnp.where(top, zero, qy[HALF - 1 : HALF])
        given[6, 2 + p : 3 + p, :] = jnp.where(top, qy[HALF - 1 : HALF], zero)


def advance(own, far, terrain, rows, edges):
    _, _, c = place()
    top = c == 0
    slab = lax.axis_index("rows")
    bed, fric = terrain[0], terrain[1]
    bed_in, fric_in = terrain[2, 0:1, :], terrain[2, 1:2, :]
    row = lax.broadcasted_iota(jnp.int32, (HALF, COLS), 0)
    first, last = row == 0, row == HALF - 1
    at_edge = jnp.where(top, 0, HALF - 1)
    lower_edge = jnp.where(top, -1, HALF - 1)
    grid_end = jnp.where(slab == 7, lower_edge, -1)

    def rows_of(n, a, b):
        rows[n] = jnp.zeros((HALF, COLS), F32)
        rows[n, 0:2, :] = a
        rows[n, 2:4, :] = b
        return rows[n]

    in_h = rows_of(0, own[6, 0:2, :], far[6, 0:2, :])
    in_q = rows_of(1, own[6, 2:4, :], far[6, 2:4, :])
    if edges is None:
        bed_out, fric_out = jnp.zeros((1, COLS), F32), jnp.zeros((1, COLS), F32)
        q1 = jnp.zeros((HALF, COLS), F32)
        out_h = q1
    else:
        mine, next_slab = edges
        out_h0 = rows_of(2, next_slab[8:10, :], next_slab[0:2, :])
        out_h1 = rows_of(3, next_slab[10:12, :], next_slab[2:4, :])
        out_q = rows_of(4, next_slab[12:14, :], next_slab[4:6, :])
        my_h = rows_of(5, mine[0:2, :], mine[8:10, :])
        my_q = rows_of(6, mine[4:6, :], mine[12:14, :])
        bed_out, fric_out = next_slab[6:7, :], next_slab[7:8, :]
        bed_mine = jnp.where(top, bed[:1], bed[HALF - 1 :])
        eta_mine, eta_out = bed_mine + my_h, bed_out + out_h0
        q1 = flux(
            jnp.where(top, out_q, my_q),
            jnp.where(top, eta_out, eta_mine),
            jnp.where(top, eta_mine, eta_out),
            jnp.maximum(bed_mine, bed_out),
            jnp.where(top, fric_out, fric[HALF - 1 :]),
        )
        q1 = jnp.where(jnp.where(top, slab, 7 - slab) == 0, 0.0, q1)
        out_h = out_h1 + jnp.where(top, -RATIO, RATIO) * q1
    bed_up, fric_up = jnp.where(top, bed_out, bed_in), jnp.where(top, fric_out, fric_in)
    bed_dn = jnp.where(top, bed_in, bed_out)
    eta_up = bed_up + jnp.where(top, out_h, in_h)
    eta_dn = bed_dn + jnp.where(top, in_h, out_h)
    q_up = jnp.where(top, q1, in_q)
    levels = []
    rows[7] = jnp.zeros((HALF, COLS), F32)
    for p in range(4):
        ref, n = (own, 3 * p) if p < 2 else (far, 3 * p - 6)
        q = q1[p : p + 1]
        h1 = ref[n] + jnp.where(row == at_edge, jnp.where(top, RATIO, -RATIO) * q, 0.0)
        qy1 = jnp.where(row == lower_edge, q, ref[n + 2])
        rows[7, p : p + 1, :] = bed[:1] + h1[:1]
        levels.append((h1, ref[n + 1], qy1))
    q2 = flux(q_up, eta_up, rows[7], jnp.maximum(bed_up, bed[:1]), fric_up)
    q2 = jnp.where(2 * slab + c == 0, 0.0, q2)
    bed_x = jnp.maximum(bed, right_of(bed))
    bed_y = jnp.maximum(bed, jnp.where(last, bed_dn, below(bed)))
    fields = []
    for p, (h1, qx, qy) in enumerate(levels):
        eta = bed + h1
        qx = x_faces(qx, eta, bed_x, fric)
        qy = flux(qy, eta, jnp.where(last, eta_dn[p : p + 1], below(eta)), bed_y, fric)
        qy = jnp.where(row == grid_end, 0.0, qy)
        over = jnp.where(first, q2[p : p + 1], above(qy))
        fields.append((h1 + RATIO * ((left_of(qx) - qx) + (over - qy)), qx, qy))
    return fields


def masks():
    sub = lax.broadcasted_iota(jnp.int32, (8, 128), 0)
    return sub < 4, (sub & 2) == 0


def put_items(items, per, fields, packed, outs):
    z, y, c = place()
    low, even = masks()
    number = {item: n for n, item in enumerate(items)}
    for f in range(3):
        for t in range(NT):
            wanted = [(e, number[(e, f, t)]) for e in range(4) if (e, f, t) in number]
            if not wanted:
                continue
            a = [fields[p][f][:, 128 * t : 128 * t + 128] for p in range(4)]
            b0, b2 = jnp.where(low, a[0], pltpu.roll(a[2], 4, 0)), jnp.where(low, pltpu.roll(a[0], 4, 0), a[2])
            b1, b3 = jnp.where(low, a[1], pltpu.roll(a[3], 4, 0)), jnp.where(low, pltpu.roll(a[1], 4, 0), a[3])
            pair = [
                jnp.where(even, b0, pltpu.roll(b1, 2, 0)),
                jnp.where(even, pltpu.roll(b0, 6, 0), b1),
                jnp.where(even, b2, pltpu.roll(b3, 2, 0)),
                jnp.where(even, pltpu.roll(b2, 6, 0), b3),
            ]
            for e, n in wanted:
                packed[n // per, n % per] = jnp.where(c == 0, pair[e], pair[3 - e])
    for k, out in enumerate(outs):
        for j in range(4):
            out[per * j : per * j + per] = packed[chunk_at(z, y, c, k, j)]


def inner_kernel(own, far, terrain, o0, o1, o2, o3, rows, packed):
    outs = (o0, o1, o2, o3)
    put_items(ITEMS_A, PA, advance(own, far, terrain, rows, None), packed, outs)
    names = own[6, 4:5, 0:128] + far[6, 4:5, 0:128]
    for out in outs:
        out[4 * PA] = jnp.zeros((8, 128), F32)
        out[4 * PA, 0:1, :] = names


def edge_kernel(own, far, terrain, mine, next_slab, o0, o1, o2, o3, rows, packed):
    fields = advance(own, far, terrain, rows, (mine, next_slab))
    put_items(ITEMS_B, PB, fields, packed, (o0, o1, o2, o3))


def select_kernel(anc, a0, a1, a2, a3, b0, b1, b2, b3, o0, o1, o2, o3, held_a, held_b):
    z, y, c = place()
    for j, (a, b) in enumerate(((a0, b0), (a1, b1), (a2, b2), (a3, b3))):
        held_a[4 * PA * j : 4 * PA * j + 4 * PA] = a[: 4 * PA]
        held_b[4 * PB * j : 4 * PB * j + 4 * PB] = b[...]
    for k, out in enumerate((o0, o1, o2, o3)):
        for j in range(4):
            at = chunk_at(z, y, c, k, j)
            chip = ((at >> 2) << 3) | ((at & 3) << 1)
            for u in range(4):
                name = anc[2 * (chip | (c ^ (u >> 1))) + (u & 1)]
                dz = step_of(STEP_Z, (name >> 4) ^ z)
                dy = step_of(STEP_Y, ((name >> 2) & 3) ^ y)
                base = jnp.where(c == 0, dy * 4 + dz, dz * 4 + dy)
                v = pl.multiple_of((((name >> 1) & 1) ^ c) * 4 + (name & 1) * 2, 2)
                out[PER * j : PER * j + PA, 2 * u : 2 * u + 2, :] = held_a[pl.ds(base * PA, PA), pl.ds(v, 2), :]
                out[PER * j + PA : PER * j + PER, 2 * u : 2 * u + 2, :] = held_b[
                    pl.ds(base * PB, PB), pl.ds(v, 2), :
                ]


def last_kernel(f0, f1, f2, f3, g0, g1, g2, g3, ho, xo, yo, packed):
    z, y, c = place()
    low, even = masks()
    for s, refs in enumerate(((f0, f1, f2, f3), (g0, g1, g2, g3))):
        core = c ^ s
        for j, ref in enumerate(refs):
            for k in range(4):
                at = s * 16 * PER + chunk_at(z, y, core, k, j) * PER
                packed[pl.ds(at, PER)] = ref[PER * k : PER * k + PER]
    for s in range(2):
        core = c ^ s
        rows = pl.ds(pl.multiple_of(core * HALF, HALF), HALF)
        for f, out in enumerate((ho, xo, yo)):
            for t in range(NT):
                cols = slice(128 * t, 128 * t + 128)
                pair = [
                    packed[s * 16 * PER + jnp.where(core == 0, AT[(d, f, t)], AT[(3 - d, f, t)])] for d in range(4)
                ]
                if s == 0:
                    b0 = jnp.where(low, pair[0], pltpu.roll(pair[2], 4, 0))
                    b1 = jnp.where(low, pair[1], pltpu.roll(pair[3], 4, 0))
                else:
                    b0 = jnp.where(low, pltpu.roll(pair[0], 4, 0), pair[2])
                    b1 = jnp.where(low, pltpu.roll(pair[1], 4, 0), pair[3])
                out[0, rows, cols] = jnp.where(even, b0, pltpu.roll(b1, 2, 0))
                out[1, rows, cols] = jnp.where(even, pltpu.roll(b0, 6, 0), b1)


def tiles(n):
    return jax.ShapeDtypeStruct((n, 8, 128), F32)


def params():
    return pltpu.CompilerParams(vmem_limit_bytes=32 * 1024 * 1024)


def outer_step(v, k):
    pairs = [(i, i ^ (STEP_Z[k] << 3 if i % 2 == 0 else STEP_Y[k] << 1)) for i in range(32)]
    return v if k == 0 else lax.ppermute(v, "dom", pairs)


def inner_step(v, k):
    pairs = [(i, i ^ (STEP_Y[k] << 1 if i % 2 == 0 else STEP_Z[k] << 3)) for i in range(32)]
    return v if k == 0 else lax.ppermute(v, "dom", pairs)


def other_core(v):
    return lax.ppermute(v, "dom", [(i, i ^ 1) for i in range(32)])


def next_slab(v):
    low = [((2 * chip + 1) * 8 + r, 2 * chip * 8 + r + 1) for chip in range(16) for r in range(7)]
    return lax.ppermute(v, ("dom", "rows"), low + [(b, a) for a, b in low])


def regroup(parts, count):
    return [jnp.concatenate([p[count * j : count * j + count] for p in parts]) for j in range(4)]


def shards(depth, x_flow, y_flow, elevation, roughness, wet, ancestors):
    state = jax.ShapeDtypeStruct((2, ROWS, COLS), F32)
    strip = jax.ShapeDtypeStruct((HALF, COLS), F32)
    halves = jax.ShapeDtypeStruct((7, HALF, COLS), F32)
    ground = jax.ShapeDtypeStruct((3, HALF, COLS), F32)
    args = (depth, x_flow, y_flow, wet, elevation, roughness, ancestors)
    keep, give, kept, given, terrain = pl.pallas_call(
        first_kernel,
        out_shape=[strip, strip, halves, halves, ground],
        in_specs=[HBM] * 7,
        out_specs=[VMEM] * 5,
        scratch_shapes=[pltpu.VMEM(v.shape, v.dtype) for v in args[:6]]
        + [pltpu.SMEM((2,), jnp.int32), pltpu.SemaphoreType.DMA((7,))],
        compiler_params=params(),
    )(*[pltpu.with_memory_space_constraint(v, pltpu.HBM) for v in args])
    mine = jnp.concatenate([keep, other_core(give)])
    far = other_core(given)
    arrived = next_slab(mine)
    a = pl.pallas_call(
        inner_kernel,
        out_shape=[tiles(4 * PA + 1)] * 4,
        in_specs=[VMEM] * 3,
        out_specs=[VMEM] * 4,
        scratch_shapes=[pltpu.VMEM((8, HALF, COLS), F32), pltpu.VMEM((16, PA, 8, 128), F32)],
        compiler_params=params(),
    )(kept, far, terrain)
    b = pl.pallas_call(
        edge_kernel,
        out_shape=[tiles(4 * PB)] * 4,
        in_specs=[VMEM] * 5,
        out_specs=[VMEM] * 4,
        scratch_shapes=[pltpu.VMEM((8, HALF, COLS), F32), pltpu.VMEM((16, PB, 8, 128), F32)],
        compiler_params=params(),
    )(kept, far, terrain, mine, arrived)
    a = [outer_step(v, k) for k, v in enumerate(a)]
    names = (a[0][4 * PA] + a[1][4 * PA]) + (a[2][4 * PA] + a[3][4 * PA])
    a = [jnp.concatenate([v, names[None]]) for v in regroup(a, PA)]
    a = [inner_step(v, k) for k, v in enumerate(a)]
    names = sum(v[4 * PA, 0, :64] for v in a).astype(jnp.int32)
    b = [outer_step(v, k) for k, v in enumerate(b)]
    b = [inner_step(v, k) for k, v in enumerate(regroup(b, PB))]
    parts = pl.pallas_call(
        select_kernel,
        out_shape=[tiles(4 * PER)] * 4,
        in_specs=[SMEM] + [VMEM] * 8,
        out_specs=[VMEM] * 4,
        scratch_shapes=[pltpu.VMEM((16 * PA, 8, 128), F32), pltpu.VMEM((16 * PB, 8, 128), F32)],
        compiler_params=params(),
    )(names, *a, *b)
    parts = [outer_step(v, k) for k, v in enumerate(parts)]
    parts = [inner_step(v, k) for k, v in enumerate(regroup(parts, PER))]
    others = [other_core(v) for v in parts]
    return tuple(
        pl.pallas_call(
            last_kernel,
            out_shape=[state] * 3,
            in_specs=[VMEM] * 8,
            out_specs=[VMEM] * 3,
            scratch_shapes=[pltpu.VMEM((2 * 16 * PER, 8, 128), F32)],
            compiler_params=params(),
        )(*parts, *others)
    )


def solution(mesh):
    wide = P("dom", "rows", None)
    in_specs = (wide, wide, wide, P("rows", None), P("rows", None), wide, P("dom"))
    return jax.shard_map(shards, mesh=mesh, in_specs=in_specs, out_specs=(wide, wide, wide), check_vma=False)
```

```python
import jax
import jax.numpy as jnp
from jax import lax
from jax.experimental import pallas as pl
from jax.experimental.pallas import tpu as pltpu
from jax.sharding import PartitionSpec as P

GDT = 9.81 * 1.0
SPACING = 10.0
RATIO = 1.0 / 10.0
MIN_DEPTH = 0.05
MANNING = (0.02, 0.025, 0.03, 0.035, 0.045, 0.06, 0.08, 0.1)
ROWS, COLS, HALF = 16, 1536, 8
NT = COLS // 128
F32 = jnp.float32

PER = 9
ITEMS = [(d, f, 3 * z + t) for z in range(4) for d in range(4) for f in range(3) for t in range(3)]
AT = {item: n for n, item in enumerate(ITEMS)}
STEP_Z = (0, 2, 3, 1)
STEP_Y = (0, 2, 1, 3)
VMEM = pl.BlockSpec(memory_space=pltpu.VMEM)
SMEM = pl.BlockSpec(memory_space=pltpu.SMEM)
HBM = pl.BlockSpec(memory_space=pltpu.HBM)


def place():
    dom = lax.axis_index("dom")
    return dom >> 3, (dom >> 1) & 3, dom & 1


def flux(q, eta_a, eta_b, bed, fric):
    he = jnp.maximum(jnp.maximum(eta_a, eta_b) - bed, MIN_DEPTH)
    numer = q - (GDT / SPACING) * he * (eta_b - eta_a)
    denom = 1.0 + fric * jnp.abs(q) * jnp.exp2((-7.0 / 3.0) * jnp.log2(he))
    return numer / denom


def friction(rough):
    total = jnp.zeros(rough.shape, F32)
    for klass, n in enumerate(MANNING):
        total = jnp.where(rough == klass, F32(GDT * (n * n)), total)
    return total


def right_of(v):
    return pltpu.roll(v, COLS - 1, 1)


def left_of(v):
    return pltpu.roll(v, 1, 1)


def below(v):
    return pltpu.roll(v, v.shape[0] - 1, 0)


def above(v):
    return pltpu.roll(v, 1, 0)


def x_faces(q, eta, bed_x, fric):
    last = lax.broadcasted_iota(jnp.int32, q.shape, 1) == COLS - 1
    return jnp.where(last, 0.0, flux(q, eta, right_of(eta), bed_x, fric))


def chunk_at(z, y, c, outer, inner):
    return jnp.where(
        c == 0,
        (z ^ STEP_Z[outer]) * 4 + (y ^ STEP_Y[inner]),
        (z ^ STEP_Z[inner]) * 4 + (y ^ STEP_Y[outer]),
    )


def step_of(steps, distance):
    found = jnp.int32(0)
    for k in range(1, 4):
        found = jnp.where(distance == steps[k], k, found)
    return found


def first_kernel(
    depth_in, xf_in, yf_in, wet_in, elev_in, rough_in, anc_in, keep, give, kept, given, terrain,
    depth, xf, yf, wet, elev, rough, anc, sems,
):
    pairs = zip(
        (elev_in, rough_in, depth_in, wet_in, xf_in, yf_in, anc_in), (elev, rough, depth, wet, xf, yf, anc)
    )
    copies = [pltpu.make_async_copy(src, dst, sems.at[n]) for n, (src, dst) in enumerate(pairs)]
    for copy in copies:
        copy.start()
    for copy in copies:
        copy.wait()
    _, _, c = place()
    top = c == 0
    bed = elev[...]
    fric = friction(rough[...])
    bed_x = jnp.maximum(bed, right_of(bed))
    bed_y = jnp.maximum(bed, below(bed))
    end = ROWS - 1
    last_row = lax.broadcasted_iota(jnp.int32, (ROWS, COLS), 0) == end
    terrain[0] = jnp.where(top, bed[:HALF], bed[HALF:])
    terrain[1] = jnp.where(top, fric[:HALF], fric[HALF:])
    terrain[2] = jnp.zeros((HALF, COLS), F32)
    terrain[2, 0:1, :] = jnp.where(top, bed[HALF : HALF + 1], bed[HALF - 1 : HALF])
    terrain[2, 1:2, :] = jnp.where(top, fric[HALF : HALF + 1], fric[HALF - 1 : HALF])
    lane = lax.broadcasted_iota(jnp.int32, (1, COLS), 1)
    at = 2 * lax.axis_index("dom")
    names = jnp.where(lane == at, anc[0].astype(F32), 0.0) + jnp.where(lane == at + 1, anc[1].astype(F32), 0.0)
    kept[6] = jnp.zeros((HALF, COLS), F32)
    given[6] = jnp.zeros((HALF, COLS), F32)
    kept[6, 4:5, :] = names
    given[6, 4:5, :] = names

    def edge(row, upper, lower):
        keep[row : row + 1, :] = jnp.where(top, upper, lower)
        give[row : row + 1, :] = jnp.where(top, lower, upper)

    zero = jnp.zeros((1, COLS), F32)
    edge(6, bed[:1], bed[end:])
    edge(7, fric[:1], fric[end:])
    for p in range(2):
        h0 = depth[p] * wet[p].astype(F32)
        qx, qy = xf[p], yf[p]
        edge(p, h0[:1], h0[end:])
        edge(4 + p, zero, qy[end:])
        eta = bed + h0
        qx = x_faces(qx, eta, bed_x, fric)
        qy = jnp.where(last_row, 0.0, flux(qy, eta, below(eta), bed_y, fric))
        h1 = h0 + RATIO * ((left_of(qx) - qx) + (above(qy) - qy))
        edge(2 + p, h1[:1], h1[end:])
        for f, v in enumerate((h1, qx, qy)):
            kept[3 * p + f] = jnp.where(top, v[:HALF], v[HALF:])
            given[3 * p + f] = jnp.where(top, v[HALF:], v[:HALF])
        kept[6, p : p + 1, :] = jnp.where(top, h1[HALF : HALF + 1], h1[HALF - 1 : HALF])
        given[6, p : p + 1, :] = jnp.where(top, h1[HALF - 1 : HALF], h1[HALF : HALF + 1])
        kept[6, 2 + p : 3 + p, :] = jnp.where(top, zero, qy[HALF - 1 : HALF])
        given[6, 2 + p : 3 + p, :] = jnp.where(top, qy[HALF - 1 : HALF], zero)


def second_kernel(own, far, terrain, mine, next_slab, o0, o1, o2, o3, rows, packed):
    z, y, c = place()
    top = c == 0
    slab = lax.axis_index("rows")
    bed, fric = terrain[0], terrain[1]
    bed_in, fric_in = terrain[2, 0:1, :], terrain[2, 1:2, :]
    row = lax.broadcasted_iota(jnp.int32, (HALF, COLS), 0)
    first, last = row == 0, row == HALF - 1
    at_edge = jnp.where(top, 0, HALF - 1)
    lower_edge = jnp.where(top, -1, HALF - 1)
    grid_end = jnp.where(slab == 7, lower_edge, -1)

    def rows_of(n, a, b):
        rows[n] = jnp.zeros((HALF, COLS), F32)
        rows[n, 0:2, :] = a
        rows[n, 2:4, :] = b
        return rows[n]

    in_h = rows_of(0, own[6, 0:2, :], far[6, 0:2, :])
    in_q = rows_of(1, own[6, 2:4, :], far[6, 2:4, :])
    out_h0 = rows_of(2, next_slab[8:10, :], next_slab[0:2, :])
    out_h1 = rows_of(3, next_slab[10:12, :], next_slab[2:4, :])
    out_q = rows_of(4, next_slab[12:14, :], next_slab[4:6, :])
    my_h = rows_of(5, mine[0:2, :], mine[8:10, :])
    my_q = rows_of(6, mine[4:6, :], mine[12:14, :])
    bed_out, fric_out = next_slab[6:7, :], next_slab[7:8, :]
    bed_mine = jnp.where(top, bed[:1], bed[HALF - 1 :])
    eta_mine, eta_out = bed_mine + my_h, bed_out + out_h0
    q1 = flux(
        jnp.where(top, out_q, my_q),
        jnp.where(top, eta_out, eta_mine),
        jnp.where(top, eta_mine, eta_out),
        jnp.maximum(bed_mine, bed_out),
        jnp.where(top, fric_out, fric[HALF - 1 :]),
    )
    q1 = jnp.where(jnp.where(top, slab, 7 - slab) == 0, 0.0, q1)
    out_h = out_h1 + jnp.where(top, -RATIO, RATIO) * q1
    bed_up, fric_up = jnp.where(top, bed_out, bed_in), jnp.where(top, fric_out, fric_in)
    bed_dn = jnp.where(top, bed_in, bed_out)
    eta_up = bed_up + jnp.where(top, out_h, in_h)
    eta_dn = bed_dn + jnp.where(top, in_h, out_h)
    q_up = jnp.where(top, q1, in_q)
    levels = []
    rows[7] = jnp.zeros((HALF, COLS), F32)
    for p in range(4):
        ref, n = (own, 3 * p) if p < 2 else (far, 3 * p - 6)
        q = q1[p : p + 1]
        h1 = ref[n] + jnp.where(row == at_edge, jnp.where(top, RATIO, -RATIO) * q, 0.0)
        qy1 = jnp.where(row == lower_edge, q, ref[n + 2])
        rows[7, p : p + 1, :] = bed[:1] + h1[:1]
        levels.append((h1, ref[n + 1], qy1))
    q2 = flux(q_up, eta_up, rows[7], jnp.maximum(bed_up, bed[:1]), fric_up)
    q2 = jnp.where(2 * slab + c == 0, 0.0, q2)
    bed_x = jnp.maximum(bed, right_of(bed))
    bed_y = jnp.maximum(bed, jnp.where(last, bed_dn, below(bed)))
    fields = []
    for p, (h1, qx, qy) in enumerate(levels):
        eta = bed + h1
        qx = x_faces(qx, eta, bed_x, fric)
        qy = flux(qy, eta, jnp.where(last, eta_dn[p : p + 1], below(eta)), bed_y, fric)
        qy = jnp.where(row == grid_end, 0.0, qy)
        over = jnp.where(first, q2[p : p + 1], above(qy))
        fields.append((h1 + RATIO * ((left_of(qx) - qx) + (over - qy)), qx, qy))
    low, even = masks()
    for f in range(3):
        for t in range(NT):
            a = [fields[p][f][:, 128 * t : 128 * t + 128] for p in range(4)]
            b0, b2 = jnp.where(low, a[0], pltpu.roll(a[2], 4, 0)), jnp.where(low, pltpu.roll(a[0], 4, 0), a[2])
            b1, b3 = jnp.where(low, a[1], pltpu.roll(a[3], 4, 0)), jnp.where(low, pltpu.roll(a[1], 4, 0), a[3])
            pair = [
                jnp.where(even, b0, pltpu.roll(b1, 2, 0)),
                jnp.where(even, pltpu.roll(b0, 6, 0), b1),
                jnp.where(even, b2, pltpu.roll(b3, 2, 0)),
                jnp.where(even, pltpu.roll(b2, 6, 0), b3),
            ]
            for d in range(4):
                n = AT[(d, f, t)]
                packed[n // PER, n % PER] = pair[d]
    names = own[6, 4:5, 0:128] + far[6, 4:5, 0:128]
    for k, out in enumerate((o0, o1, o2, o3)):
        for j in range(4):
            out[PER * j : PER * j + PER] = packed[chunk_at(z, y, c, k, j)]
        out[4 * PER] = jnp.zeros((8, 128), F32)
        out[4 * PER, 0:1, :] = names


def masks():
    sub = lax.broadcasted_iota(jnp.int32, (8, 128), 0)
    return sub < 4, (sub & 2) == 0


def select_kernel(anc, a0, a1, a2, a3, o0, o1, o2, o3, held):
    z, y, c = place()
    for j, a in enumerate((a0, a1, a2, a3)):
        held[4 * PER * j : 4 * PER * j + 4 * PER] = a[: 4 * PER]
    for k, out in enumerate((o0, o1, o2, o3)):
        for j in range(4):
            at = chunk_at(z, y, c, j, k)
            chip = ((at >> 2) << 3) | ((at & 3) << 1)
            for u in range(4):
                name = anc[2 * (chip | (c ^ (u >> 1))) + (u & 1)]
                dz = step_of(STEP_Z, (name >> 4) ^ z)
                dy = step_of(STEP_Y, ((name >> 2) & 3) ^ y)
                base = jnp.where(c == 0, dy * 4 + dz, dz * 4 + dy) * PER
                v = pl.multiple_of((((name >> 1) & 1) ^ c) * 4 + (name & 1) * 2, 2)
                out[PER * j : PER * j + PER, 2 * u : 2 * u + 2, :] = held[pl.ds(base, PER), pl.ds(v, 2), :]


def last_kernel(f0, f1, f2, f3, g0, g1, g2, g3, ho, xo, yo, packed):
    z, y, c = place()
    low, even = masks()
    for s, refs in enumerate(((f0, f1, f2, f3), (g0, g1, g2, g3))):
        core = c ^ s
        for j, ref in enumerate(refs):
            for k in range(4):
                at = s * 16 * PER + chunk_at(z, y, core, j, k) * PER
                packed[pl.ds(at, PER)] = ref[PER * k : PER * k + PER]
    for s in range(2):
        core = c ^ s
        rows = pl.ds(pl.multiple_of(core * HALF, HALF), HALF)
        for f, out in enumerate((ho, xo, yo)):
            for t in range(NT):
                cols = slice(128 * t, 128 * t + 128)
                pair = [packed[s * 16 * PER + AT[(d, f, t)]] for d in range(4)]
                if s == 0:
                    b0 = jnp.where(low, pair[0], pltpu.roll(pair[2], 4, 0))
                    b1 = jnp.where(low, pair[1], pltpu.roll(pair[3], 4, 0))
                else:
                    b0 = jnp.where(low, pltpu.roll(pair[0], 4, 0), pair[2])
                    b1 = jnp.where(low, pltpu.roll(pair[1], 4, 0), pair[3])
                out[0, rows, cols] = jnp.where(even, b0, pltpu.roll(b1, 2, 0))
                out[1, rows, cols] = jnp.where(even, pltpu.roll(b0, 6, 0), b1)


def tiles(n):
    return jax.ShapeDtypeStruct((n, 8, 128), F32)


def params():
    return pltpu.CompilerParams(vmem_limit_bytes=32 * 1024 * 1024)


def outer_step(v, k):
    pairs = [(i, i ^ (STEP_Z[k] << 3 if i % 2 == 0 else STEP_Y[k] << 1)) for i in range(32)]
    return v if k == 0 else lax.ppermute(v, "dom", pairs)


def inner_step(v, k):
    pairs = [(i, i ^ (STEP_Y[k] << 1 if i % 2 == 0 else STEP_Z[k] << 3)) for i in range(32)]
    return v if k == 0 else lax.ppermute(v, "dom", pairs)


def other_core(v):
    return lax.ppermute(v, "dom", [(i, i ^ 1) for i in range(32)])


def next_slab(v):
    low = [((2 * chip + 1) * 8 + r, 2 * chip * 8 + r + 1) for chip in range(16) for r in range(7)]
    return lax.ppermute(v, ("dom", "rows"), low + [(b, a) for a, b in low])


def regroup(parts, count):
    return [jnp.concatenate([p[count * j : count * j + count] for p in parts]) for j in range(4)]


def shards(depth, x_flow, y_flow, elevation, roughness, wet, ancestors):
    state = jax.ShapeDtypeStruct((2, ROWS, COLS), F32)
    strip = jax.ShapeDtypeStruct((HALF, COLS), F32)
    halves = jax.ShapeDtypeStruct((7, HALF, COLS), F32)
    ground = jax.ShapeDtypeStruct((3, HALF, COLS), F32)
    args = (depth, x_flow, y_flow, wet, elevation, roughness, ancestors)
    keep, give, kept, given, terrain = pl.pallas_call(
        first_kernel,
        out_shape=[strip, strip, halves, halves, ground],
        in_specs=[HBM] * 7,
        out_specs=[VMEM] * 5,
        scratch_shapes=[pltpu.VMEM(v.shape, v.dtype) for v in args[:6]]
        + [pltpu.SMEM((2,), jnp.int32), pltpu.SemaphoreType.DMA((7,))],
        compiler_params=params(),
    )(*[pltpu.with_memory_space_constraint(v, pltpu.HBM) for v in args])
    mine = jnp.concatenate([keep, other_core(give)])
    far = other_core(given)
    arrived = next_slab(mine)
    parts = pl.pallas_call(
        second_kernel,
        out_shape=[tiles(4 * PER + 1)] * 4,
        in_specs=[VMEM] * 5,
        out_specs=[VMEM] * 4,
        scratch_shapes=[pltpu.VMEM((8, HALF, COLS), F32), pltpu.VMEM((16, PER, 8, 128), F32)],
        compiler_params=params(),
    )(kept, far, terrain, mine, arrived)
    parts = [outer_step(v, k) for k, v in enumerate(parts)]
    names = (parts[0][4 * PER] + parts[1][4 * PER]) + (parts[2][4 * PER] + parts[3][4 * PER])
    parts = [jnp.concatenate([v, names[None]]) for v in regroup(parts, PER)]
    parts = [inner_step(v, k) for k, v in enumerate(parts)]
    names = sum(v[4 * PER, 0, :64] for v in parts).astype(jnp.int32)
    parts = pl.pallas_call(
        select_kernel,
        out_shape=[tiles(4 * PER)] * 4,
        in_specs=[SMEM] + [VMEM] * 4,
        out_specs=[VMEM] * 4,
        scratch_shapes=[pltpu.VMEM((16 * PER, 8, 128), F32)],
        compiler_params=params(),
    )(names, *parts)
    parts = [inner_step(v, k) for k, v in enumerate(parts)]
    parts = [outer_step(v, k) for k, v in enumerate(regroup(parts, PER))]
    others = [other_core(v) for v in parts]
    return tuple(
        pl.pallas_call(
            last_kernel,
            out_shape=[state] * 3,
            in_specs=[VMEM] * 8,
            out_specs=[VMEM] * 3,
            scratch_shapes=[pltpu.VMEM((2 * 16 * PER, 8, 128), F32)],
            compiler_params=params(),
        )(*parts, *others)
    )


def solution(mesh):
    wide = P("dom", "rows", None)
    in_specs = (wide, wide, wide, P("rows", None), P("rows", None), wide, P("dom"))
    return jax.shard_map(shards, mesh=mesh, in_specs=in_specs, out_specs=(wide, wide, wide), check_vma=False)
```

```python
import jax
import jax.numpy as jnp
from jax import lax
from jax.experimental import pallas as pl
from jax.experimental.pallas import tpu as pltpu
from jax.sharding import PartitionSpec as P

GDT = 9.81 * 1.0
SPACING = 10.0
RATIO = 1.0 / 10.0
MIN_DEPTH = 0.05
MANNING = (0.02, 0.025, 0.03, 0.035, 0.045, 0.06, 0.08, 0.1)
ROWS, COLS, HALF = 16, 1536, 8
NT = COLS // 128
F32 = jnp.float32

ITEMS_A = [(e, f, t) for e in (1, 2, 3) for f in range(3) for t in range(NT) if (e, f) != (1, 2)]
ITEMS_B = [(0, f, t) for f in range(3) for t in range(NT)] + [(1, 2, t) for t in range(NT)]
PA, PB = 6, 3
PER = PA + PB
AT = {item: (n // PA) * PER + n % PA for n, item in enumerate(ITEMS_A)}
AT.update({item: (n // PB) * PER + PA + n % PB for n, item in enumerate(ITEMS_B)})
STEP_Z = (0, 2, 3, 1)
STEP_Y = (0, 2, 1, 3)
VMEM = pl.BlockSpec(memory_space=pltpu.VMEM)
SMEM = pl.BlockSpec(memory_space=pltpu.SMEM)
HBM = pl.BlockSpec(memory_space=pltpu.HBM)


def place():
    dom = lax.axis_index("dom")
    return dom >> 3, (dom >> 1) & 3, dom & 1


def flux(q, eta_a, eta_b, bed, fric):
    he = jnp.maximum(jnp.maximum(eta_a, eta_b) - bed, MIN_DEPTH)
    numer = q - (GDT / SPACING) * he * (eta_b - eta_a)
    denom = 1.0 + fric * jnp.abs(q) * jnp.exp2((-7.0 / 3.0) * jnp.log2(he))
    return numer / denom


def friction(rough):
    total = jnp.zeros(rough.shape, F32)
    for klass, n in enumerate(MANNING):
        total = jnp.where(rough == klass, F32(GDT * (n * n)), total)
    return total


def right_of(v):
    return pltpu.roll(v, COLS - 1, 1)


def left_of(v):
    return pltpu.roll(v, 1, 1)


def below(v):
    return pltpu.roll(v, v.shape[0] - 1, 0)


def above(v):
    return pltpu.roll(v, 1, 0)


def x_faces(q, eta, bed_x, fric):
    last = lax.broadcasted_iota(jnp.int32, q.shape, 1) == COLS - 1
    return jnp.where(last, 0.0, flux(q, eta, right_of(eta), bed_x, fric))


def chunk_at(z, y, c, outer, inner):
    return jnp.where(
        c == 0,
        (z ^ STEP_Z[outer]) * 4 + (y ^ STEP_Y[inner]),
        (z ^ STEP_Z[inner]) * 4 + (y ^ STEP_Y[outer]),
    )


def step_of(steps, distance):
    found = jnp.int32(0)
    for k in range(1, 4):
        found = jnp.where(distance == steps[k], k, found)
    return found


def first_kernel(
    depth_in, xf_in, yf_in, wet_in, elev_in, rough_in, anc_in, keep, give, kept, given, terrain,
    depth, xf, yf, wet, elev, rough, anc, sems,
):
    pairs = zip(
        (elev_in, rough_in, depth_in, wet_in, xf_in, yf_in, anc_in), (elev, rough, depth, wet, xf, yf, anc)
    )
    copies = [pltpu.make_async_copy(src, dst, sems.at[n]) for n, (src, dst) in enumerate(pairs)]
    for copy in copies:
        copy.start()
    for copy in copies:
        copy.wait()
    _, _, c = place()
    top = c == 0
    bed = elev[...]
    fric = friction(rough[...])
    bed_x = jnp.maximum(bed, right_of(bed))
    bed_y = jnp.maximum(bed, below(bed))
    end = ROWS - 1
    last_row = lax.broadcasted_iota(jnp.int32, (ROWS, COLS), 0) == end
    terrain[0] = jnp.where(top, bed[:HALF], bed[HALF:])
    terrain[1] = jnp.where(top, fric[:HALF], fric[HALF:])
    terrain[2] = jnp.zeros((HALF, COLS), F32)
    terrain[2, 0:1, :] = jnp.where(top, bed[HALF : HALF + 1], bed[HALF - 1 : HALF])
    terrain[2, 1:2, :] = jnp.where(top, fric[HALF : HALF + 1], fric[HALF - 1 : HALF])
    lane = lax.broadcasted_iota(jnp.int32, (1, COLS), 1)
    at = 2 * lax.axis_index("dom")
    names = jnp.where(lane == at, anc[0].astype(F32), 0.0) + jnp.where(lane == at + 1, anc[1].astype(F32), 0.0)
    kept[6] = jnp.zeros((HALF, COLS), F32)
    given[6] = jnp.zeros((HALF, COLS), F32)
    kept[6, 4:5, :] = names
    given[6, 4:5, :] = names

    def edge(row, upper, lower):
        keep[row : row + 1, :] = jnp.where(top, upper, lower)
        give[row : row + 1, :] = jnp.where(top, lower, upper)

    zero = jnp.zeros((1, COLS), F32)
    edge(6, bed[:1], bed[end:])
    edge(7, fric[:1], fric[end:])
    for p in range(2):
        h0 = depth[p] * wet[p].astype(F32)
        qx, qy = xf[p], yf[p]
        edge(p, h0[:1], h0[end:])
        edge(4 + p, zero, qy[end:])
        eta = bed + h0
        qx = x_faces(qx, eta, bed_x, fric)
        qy = jnp.where(last_row, 0.0, flux(qy, eta, below(eta), bed_y, fric))
        h1 = h0 + RATIO * ((left_of(qx) - qx) + (above(qy) - qy))
        edge(2 + p, h1[:1], h1[end:])
        for f, v in enumerate((h1, qx, qy)):
            kept[3 * p + f] = jnp.where(top, v[:HALF], v[HALF:])
            given[3 * p + f] = jnp.where(top, v[HALF:], v[:HALF])
        kept[6, p : p + 1, :] = jnp.where(top, h1[HALF : HALF + 1], h1[HALF - 1 : HALF])
        given[6, p : p + 1, :] = jnp.where(top, h1[HALF - 1 : HALF], h1[HALF : HALF + 1])
        kept[6, 2 + p : 3 + p, :] = jnp.where(top, zero, qy[HALF - 1 : HALF])
        given[6, 2 + p : 3 + p, :] = jnp.where(top, qy[HALF - 1 : HALF], zero)


def advance(own, far, terrain, rows, edges):
    _, _, c = place()
    top = c == 0
    slab = lax.axis_index("rows")
    bed, fric = terrain[0], terrain[1]
    bed_in, fric_in = terrain[2, 0:1, :], terrain[2, 1:2, :]
    row = lax.broadcasted_iota(jnp.int32, (HALF, COLS), 0)
    first, last = row == 0, row == HALF - 1
    at_edge = jnp.where(top, 0, HALF - 1)
    lower_edge = jnp.where(top, -1, HALF - 1)
    grid_end = jnp.where(slab == 7, lower_edge, -1)

    def rows_of(n, a, b):
        rows[n] = jnp.zeros((HALF, COLS), F32)
        rows[n, 0:2, :] = a
        rows[n, 2:4, :] = b
        return rows[n]

    in_h = rows_of(0, own[6, 0:2, :], far[6, 0:2, :])
    in_q = rows_of(1, own[6, 2:4, :], far[6, 2:4, :])
    if edges is None:
        bed_out, fric_out = jnp.zeros((1, COLS), F32), jnp.zeros((1, COLS), F32)
        q1 = jnp.zeros((HALF, COLS), F32)
        out_h = q1
    else:
        mine, next_slab = edges
        out_h0 = rows_of(2, next_slab[8:10, :], next_slab[0:2, :])
        out_h1 = rows_of(3, next_slab[10:12, :], next_slab[2:4, :])
        out_q = rows_of(4, next_slab[12:14, :], next_slab[4:6, :])
        my_h = rows_of(5, mine[0:2, :], mine[8:10, :])
        my_q = rows_of(6, mine[4:6, :], mine[12:14, :])
        bed_out, fric_out = next_slab[6:7, :], next_slab[7:8, :]
        bed_mine = jnp.where(top, bed[:1], bed[HALF - 1 :])
        eta_mine, eta_out = bed_mine + my_h, bed_out + out_h0
        q1 = flux(
            jnp.where(top, out_q, my_q),
            jnp.where(top, eta_out, eta_mine),
            jnp.where(top, eta_mine, eta_out),
            jnp.maximum(bed_mine, bed_out),
            jnp.where(top, fric_out, fric[HALF - 1 :]),
        )
        q1 = jnp.where(jnp.where(top, slab, 7 - slab) == 0, 0.0, q1)
        out_h = out_h1 + jnp.where(top, -RATIO, RATIO) * q1
    bed_up, fric_up = jnp.where(top, bed_out, bed_in), jnp.where(top, fric_out, fric_in)
    bed_dn = jnp.where(top, bed_in, bed_out)
    eta_up = bed_up + jnp.where(top, out_h, in_h)
    eta_dn = bed_dn + jnp.where(top, in_h, out_h)
    q_up = jnp.where(top, q1, in_q)
    levels = []
    rows[7] = jnp.zeros((HALF, COLS), F32)
    for p in range(4):
        ref, n = (own, 3 * p) if p < 2 else (far, 3 * p - 6)
        q = q1[p : p + 1]
        h1 = ref[n] + jnp.where(row == at_edge, jnp.where(top, RATIO, -RATIO) * q, 0.0)
        qy1 = jnp.where(row == lower_edge, q, ref[n + 2])
        rows[7, p : p + 1, :] = bed[:1] + h1[:1]
        levels.append((h1, ref[n + 1], qy1))
    q2 = flux(q_up, eta_up, rows[7], jnp.maximum(bed_up, bed[:1]), fric_up)
    q2 = jnp.where(2 * slab + c == 0, 0.0, q2)
    bed_x = jnp.maximum(bed, right_of(bed))
    bed_y = jnp.maximum(bed, jnp.where(last, bed_dn, below(bed)))
    fields = []
    for p, (h1, qx, qy) in enumerate(levels):
        eta = bed + h1
        qx = x_faces(qx, eta, bed_x, fric)
        qy = flux(qy, eta, jnp.where(last, eta_dn[p : p + 1], below(eta)), bed_y, fric)
        qy = jnp.where(row == grid_end, 0.0, qy)
        over = jnp.where(first, q2[p : p + 1], above(qy))
        fields.append((h1 + RATIO * ((left_of(qx) - qx) + (over - qy)), qx, qy))
    return fields


def masks():
    sub = lax.broadcasted_iota(jnp.int32, (8, 128), 0)
    return sub < 4, (sub & 2) == 0


def put_items(items, per, fields, packed, outs):
    z, y, c = place()
    low, even = masks()
    number = {item: n for n, item in enumerate(items)}
    for f in range(3):
        for t in range(NT):
            wanted = [(e, number[(e, f, t)]) for e in range(4) if (e, f, t) in number]
            if not wanted:
                continue
            a = [fields[p][f][:, 128 * t : 128 * t + 128] for p in range(4)]
            b0, b2 = jnp.where(low, a[0], pltpu.roll(a[2], 4, 0)), jnp.where(low, pltpu.roll(a[0], 4, 0), a[2])
            b1, b3 = jnp.where(low, a[1], pltpu.roll(a[3], 4, 0)), jnp.where(low, pltpu.roll(a[1], 4, 0), a[3])
            pair = [
                jnp.where(even, b0, pltpu.roll(b1, 2, 0)),
                jnp.where(even, pltpu.roll(b0, 6, 0), b1),
                jnp.where(even, b2, pltpu.roll(b3, 2, 0)),
                jnp.where(even, pltpu.roll(b2, 6, 0), b3),
            ]
            for e, n in wanted:
                packed[n // per, n % per] = jnp.where(c == 0, pair[e], pair[3 - e])
    for k, out in enumerate(outs):
        for j in range(4):
            out[per * j : per * j + per] = packed[chunk_at(z, y, c, k, j)]


def inner_kernel(own, far, terrain, o0, o1, o2, o3, rows, packed):
    outs = (o0, o1, o2, o3)
    put_items(ITEMS_A, PA, advance(own, far, terrain, rows, None), packed, outs)
    names = own[6, 4:5, 0:128] + far[6, 4:5, 0:128]
    for out in outs:
        out[4 * PA] = jnp.zeros((8, 128), F32)
        out[4 * PA, 0:1, :] = names


def edge_kernel(own, far, terrain, mine, next_slab, names, o0, o1, o2, o3, named, rows, packed):
    named[...] = names[...]
    fields = advance(own, far, terrain, rows, (mine, next_slab))
    put_items(ITEMS_B, PB, fields, packed, (o0, o1, o2, o3))


def select_kernel(anc, a0, a1, a2, a3, o0, o1, o2, o3, held):
    z, y, c = place()
    for j, a in enumerate((a0, a1, a2, a3)):
        held[4 * PER * j : 4 * PER * j + 4 * PER] = a[: 4 * PER]
    for k, out in enumerate((o0, o1, o2, o3)):
        for j in range(4):
            at = chunk_at(z, y, c, j, k)
            chip = ((at >> 2) << 3) | ((at & 3) << 1)
            for u in range(4):
                name = anc[2 * (chip | (c ^ (u >> 1))) + (u & 1)]
                dz = step_of(STEP_Z, (name >> 4) ^ z)
                dy = step_of(STEP_Y, ((name >> 2) & 3) ^ y)
                base = jnp.where(c == 0, dy * 4 + dz, dz * 4 + dy) * PER
                v = pl.multiple_of((((name >> 1) & 1) ^ c) * 4 + (name & 1) * 2, 2)
                out[PER * j : PER * j + PER, 2 * u : 2 * u + 2, :] = held[pl.ds(base, PER), pl.ds(v, 2), :]


def last_kernel(f0, f1, f2, f3, g0, g1, g2, g3, ho, xo, yo, packed):
    z, y, c = place()
    _, even = masks()
    for s, refs in enumerate(((f0, f1, f2, f3), (g0, g1, g2, g3))):
        core = c ^ s
        for j, ref in enumerate(refs):
            for k in range(4):
                at = s * 16 * PER + chunk_at(z, y, core, j, k) * PER
                packed[pl.ds(at, PER)] = ref[PER * k : PER * k + PER]
    for s in range(2):
        core = c ^ s
        rows = pl.ds(pl.multiple_of(core * HALF, HALF), HALF)
        for f, out in enumerate((ho, xo, yo)):
            for t in range(NT):
                cols = slice(128 * t, 128 * t + 128)
                pair = [
                    packed[s * 16 * PER + jnp.where(core == 0, AT[(d, f, t)], AT[(3 - d, f, t)])] for d in range(4)
                ]
                b0 = jnp.concatenate([pair[0], pair[2]], axis=0)
                b1 = jnp.concatenate([pair[1], pair[3]], axis=0)
                out[0, rows, cols] = jnp.where(even, b0, pltpu.roll(b1, 2, 0))
                out[1, rows, cols] = jnp.where(even, pltpu.roll(b0, 6, 0), b1)


def tiles(n):
    return jax.ShapeDtypeStruct((n, 8, 128), F32)


def params():
    return pltpu.CompilerParams(vmem_limit_bytes=32 * 1024 * 1024)


def outer_step(v, k):
    pairs = [(i, i ^ (STEP_Z[k] << 3 if i % 2 == 0 else STEP_Y[k] << 1)) for i in range(32)]
    return v if k == 0 else lax.ppermute(v, "dom", pairs)


def inner_step(v, k):
    pairs = [(i, i ^ (STEP_Y[k] << 1 if i % 2 == 0 else STEP_Z[k] << 3)) for i in range(32)]
    return v if k == 0 else lax.ppermute(v, "dom", pairs)


def outer_cross(v, k):
    pairs = [(i, i ^ (STEP_Z[k] << 3 if i % 2 == 0 else STEP_Y[k] << 1) ^ 1) for i in range(32)]
    return lax.ppermute(v, "dom", pairs)


def other_core(v):
    return lax.ppermute(v, "dom", [(i, i ^ 1) for i in range(32)])


def next_slab(v):
    low = [((2 * chip + 1) * 8 + r, 2 * chip * 8 + r + 1) for chip in range(16) for r in range(7)]
    return lax.ppermute(v, ("dom", "rows"), low + [(b, a) for a, b in low])


def regroup(parts, count):
    return [jnp.concatenate([p[count * j : count * j + count] for p in parts]) for j in range(4)]


def shards(depth, x_flow, y_flow, elevation, roughness, wet, ancestors):
    state = jax.ShapeDtypeStruct((2, ROWS, COLS), F32)
    strip = jax.ShapeDtypeStruct((HALF, COLS), F32)
    halves = jax.ShapeDtypeStruct((7, HALF, COLS), F32)
    ground = jax.ShapeDtypeStruct((3, HALF, COLS), F32)
    args = (depth, x_flow, y_flow, wet, elevation, roughness, ancestors)
    keep, give, kept, given, terrain = pl.pallas_call(
        first_kernel,
        out_shape=[strip, strip, halves, halves, ground],
        in_specs=[HBM] * 7,
        out_specs=[VMEM] * 5,
        scratch_shapes=[pltpu.VMEM(v.shape, v.dtype) for v in args[:6]]
        + [pltpu.SMEM((2,), jnp.int32), pltpu.SemaphoreType.DMA((7,))],
        compiler_params=params(),
    )(*[pltpu.with_memory_space_constraint(v, pltpu.HBM) for v in args])
    mine = jnp.concatenate([keep, other_core(give)])
    far = other_core(given)
    arrived = next_slab(mine)
    a = pl.pallas_call(
        inner_kernel,
        out_shape=[tiles(4 * PA + 1)] * 4,
        in_specs=[VMEM] * 3,
        out_specs=[VMEM] * 4,
        scratch_shapes=[pltpu.VMEM((8, HALF, COLS), F32), pltpu.VMEM((16, PA, 8, 128), F32)],
        compiler_params=params(),
    )(kept, far, terrain)
    a = [outer_step(v, k) for k, v in enumerate(a)]
    names = (a[0][4 * PA :] + a[1][4 * PA :]) + (a[2][4 * PA :] + a[3][4 * PA :])
    *b, names = pl.pallas_call(
        edge_kernel,
        out_shape=[tiles(4 * PB)] * 4 + [tiles(1)],
        in_specs=[VMEM] * 6,
        out_specs=[VMEM] * 5,
        scratch_shapes=[pltpu.VMEM((8, HALF, COLS), F32), pltpu.VMEM((16, PB, 8, 128), F32)],
        compiler_params=params(),
    )(kept, far, terrain, mine, arrived, names)
    b = [outer_step(v, k) for k, v in enumerate(b)]
    both = zip(regroup(a, PA), regroup(b, PB))
    parts = [
        jnp.concatenate(
            [v.reshape(4, PA, 8, 128), w.reshape(4, PB, 8, 128)], axis=1
        ).reshape(4 * PER, 8, 128)
        for v, w in both
    ]
    parts = [jnp.concatenate([v, names]) for v in parts]
    parts = [inner_step(v, k) for k, v in enumerate(parts)]
    names = sum(v[4 * PER, 0, :64] for v in parts).astype(jnp.int32)
    parts = pl.pallas_call(
        select_kernel,
        out_shape=[tiles(4 * PER)] * 4,
        in_specs=[SMEM] + [VMEM] * 4,
        out_specs=[VMEM] * 4,
        scratch_shapes=[pltpu.VMEM((16 * PER, 8, 128), F32)],
        compiler_params=params(),
    )(names, *parts)
    parts = [inner_step(v, k) for k, v in enumerate(parts)]
    parts = regroup(parts, PER)
    others = [outer_cross(v[:, 4:], k) for k, v in enumerate(parts)]
    parts = [outer_step(v[:, :4], k) for k, v in enumerate(parts)]
    return tuple(
        pl.pallas_call(
            last_kernel,
            out_shape=[state] * 3,
            in_specs=[VMEM] * 8,
            out_specs=[VMEM] * 3,
            scratch_shapes=[pltpu.VMEM((2 * 16 * PER, 4, 128), F32)],
            compiler_params=params(),
        )(*parts, *others)
    )


def solution(mesh):
    wide = P("dom", "rows", None)
    in_specs = (wide, wide, wide, P("rows", None), P("rows", None), wide, P("dom"))
    return jax.shard_map(shards, mesh=mesh, in_specs=in_specs, out_specs=(wide, wide, wide), check_vma=False)
```

```python
import jax
import jax.numpy as jnp
from jax import lax
from jax.experimental import pallas as pl
from jax.experimental.pallas import tpu as pltpu
from jax.sharding import PartitionSpec as P

GDT = 9.81 * 1.0
SPACING = 10.0
RATIO = 1.0 / 10.0
MIN_DEPTH = 0.05
MANNING = (0.02, 0.025, 0.03, 0.035, 0.045, 0.06, 0.08, 0.1)
ROWS, COLS, HALF = 16, 1536, 8
NT = COLS // 128
F32 = jnp.float32

PER = 9
ITEMS = [(d, f, 3 * z + t) for z in range(4) for d in range(4) for f in range(3) for t in range(3)]
AT = {item: n for n, item in enumerate(ITEMS)}
STEP_Z = (0, 2, 3, 1)
STEP_Y = (0, 2, 1, 3)
VMEM = pl.BlockSpec(memory_space=pltpu.VMEM)
SMEM = pl.BlockSpec(memory_space=pltpu.SMEM)
HBM = pl.BlockSpec(memory_space=pltpu.HBM)


def place():
    dom = lax.axis_index("dom")
    return dom >> 3, (dom >> 1) & 3, dom & 1


def flux(q, eta_a, eta_b, bed, fric):
    he = jnp.maximum(jnp.maximum(eta_a, eta_b) - bed, MIN_DEPTH)
    numer = q - (GDT / SPACING) * he * (eta_b - eta_a)
    denom = 1.0 + fric * jnp.abs(q) * jnp.exp2((-7.0 / 3.0) * jnp.log2(he))
    return numer / denom


def friction(rough):
    total = jnp.zeros(rough.shape, F32)
    for klass, n in enumerate(MANNING):
        total = jnp.where(rough == klass, F32(GDT * (n * n)), total)
    return total


def right_of(v):
    return pltpu.roll(v, COLS - 1, 1)


def left_of(v):
    return pltpu.roll(v, 1, 1)


def below(v):
    return pltpu.roll(v, v.shape[0] - 1, 0)


def above(v):
    return pltpu.roll(v, 1, 0)


def x_faces(q, eta, bed_x, fric):
    last = lax.broadcasted_iota(jnp.int32, q.shape, 1) == COLS - 1
    return jnp.where(last, 0.0, flux(q, eta, right_of(eta), bed_x, fric))


def chunk_at(z, y, c, outer, inner):
    return jnp.where(
        c == 0,
        (z ^ STEP_Z[outer]) * 4 + (y ^ STEP_Y[inner]),
        (z ^ STEP_Z[inner]) * 4 + (y ^ STEP_Y[outer]),
    )


def step_of(steps, distance):
    found = jnp.int32(0)
    for k in range(1, 4):
        found = jnp.where(distance == steps[k], k, found)
    return found


def first_kernel(
    depth_in, xf_in, yf_in, wet_in, elev_in, rough_in, anc_in, keep, give, kept, given, terrain,
    depth, xf, yf, wet, elev, rough, anc, sems,
):
    pairs = zip(
        (elev_in, rough_in, depth_in, wet_in, xf_in, yf_in, anc_in), (elev, rough, depth, wet, xf, yf, anc)
    )
    copies = [pltpu.make_async_copy(src, dst, sems.at[n]) for n, (src, dst) in enumerate(pairs)]
    for copy in copies:
        copy.start()
    for copy in copies:
        copy.wait()
    _, _, c = place()
    top = c == 0
    bed = elev[...]
    fric = friction(rough[...])
    bed_x = jnp.maximum(bed, right_of(bed))
    bed_y = jnp.maximum(bed, below(bed))
    end = ROWS - 1
    last_row = lax.broadcasted_iota(jnp.int32, (ROWS, COLS), 0) == end
    terrain[0] = jnp.where(top, bed[:HALF], bed[HALF:])
    terrain[1] = jnp.where(top, fric[:HALF], fric[HALF:])
    terrain[2] = jnp.zeros((HALF, COLS), F32)
    terrain[2, 0:1, :] = jnp.where(top, bed[HALF : HALF + 1], bed[HALF - 1 : HALF])
    terrain[2, 1:2, :] = jnp.where(top, fric[HALF : HALF + 1], fric[HALF - 1 : HALF])
    lane = lax.broadcasted_iota(jnp.int32, (1, COLS), 1)
    at = 2 * lax.axis_index("dom")
    names = jnp.where(lane == at, anc[0].astype(F32), 0.0) + jnp.where(lane == at + 1, anc[1].astype(F32), 0.0)
    kept[6] = jnp.zeros((HALF, COLS), F32)
    given[6] = jnp.zeros((HALF, COLS), F32)
    kept[6, 4:5, :] = names
    given[6, 4:5, :] = names

    def edge(row, upper, lower):
        keep[row : row + 1, :] = jnp.where(top, upper, lower)
        give[row : row + 1, :] = jnp.where(top, lower, upper)

    zero = jnp.zeros((1, COLS), F32)
    edge(6, bed[:1], bed[end:])
    edge(7, fric[:1], fric[end:])
    for p in range(2):
        h0 = depth[p] * wet[p].astype(F32)
        qx, qy = xf[p], yf[p]
        edge(p, h0[:1], h0[end:])
        edge(4 + p, zero, qy[end:])
        eta = bed + h0
        qx = x_faces(qx, eta, bed_x, fric)
        qy = jnp.where(last_row, 0.0, flux(qy, eta, below(eta), bed_y, fric))
        h1 = h0 + RATIO * ((left_of(qx) - qx) + (above(qy) - qy))
        edge(2 + p, h1[:1], h1[end:])
        for f, v in enumerate((h1, qx, qy)):
            kept[3 * p + f] = jnp.where(top, v[:HALF], v[HALF:])
            given[3 * p + f] = jnp.where(top, v[HALF:], v[:HALF])
        kept[6, p : p + 1, :] = jnp.where(top, h1[HALF : HALF + 1], h1[HALF - 1 : HALF])
        given[6, p : p + 1, :] = jnp.where(top, h1[HALF - 1 : HALF], h1[HALF : HALF + 1])
        kept[6, 2 + p : 3 + p, :] = jnp.where(top, zero, qy[HALF - 1 : HALF])
        given[6, 2 + p : 3 + p, :] = jnp.where(top, qy[HALF - 1 : HALF], zero)


def second_kernel(own, far, terrain, mine, next_slab, o0, o1, o2, o3, rows, packed):
    z, y, c = place()
    top = c == 0
    slab = lax.axis_index("rows")
    bed, fric = terrain[0], terrain[1]
    bed_in, fric_in = terrain[2, 0:1, :], terrain[2, 1:2, :]
    row = lax.broadcasted_iota(jnp.int32, (HALF, COLS), 0)
    first, last = row == 0, row == HALF - 1
    at_edge = jnp.where(top, 0, HALF - 1)
    lower_edge = jnp.where(top, -1, HALF - 1)
    grid_end = jnp.where(slab == 7, lower_edge, -1)

    def rows_of(n, a, b):
        rows[n] = jnp.zeros((HALF, COLS), F32)
        rows[n, 0:2, :] = a
        rows[n, 2:4, :] = b
        return rows[n]

    in_h = rows_of(0, own[6, 0:2, :], far[6, 0:2, :])
    in_q = rows_of(1, own[6, 2:4, :], far[6, 2:4, :])
    out_h0 = rows_of(2, next_slab[8:10, :], next_slab[0:2, :])
    out_h1 = rows_of(3, next_slab[10:12, :], next_slab[2:4, :])
    out_q = rows_of(4, next_slab[12:14, :], next_slab[4:6, :])
    my_h = rows_of(5, mine[0:2, :], mine[8:10, :])
    my_q = rows_of(6, mine[4:6, :], mine[12:14, :])
    bed_out, fric_out = next_slab[6:7, :], next_slab[7:8, :]
    bed_mine = jnp.where(top, bed[:1], bed[HALF - 1 :])
    eta_mine, eta_out = bed_mine + my_h, bed_out + out_h0
    q1 = flux(
        jnp.where(top, out_q, my_q),
        jnp.where(top, eta_out, eta_mine),
        jnp.where(top, eta_mine, eta_out),
        jnp.maximum(bed_mine, bed_out),
        jnp.where(top, fric_out, fric[HALF - 1 :]),
    )
    q1 = jnp.where(jnp.where(top, slab, 7 - slab) == 0, 0.0, q1)
    out_h = out_h1 + jnp.where(top, -RATIO, RATIO) * q1
    bed_up, fric_up = jnp.where(top, bed_out, bed_in), jnp.where(top, fric_out, fric_in)
    bed_dn = jnp.where(top, bed_in, bed_out)
    eta_up = bed_up + jnp.where(top, out_h, in_h)
    eta_dn = bed_dn + jnp.where(top, in_h, out_h)
    q_up = jnp.where(top, q1, in_q)
    levels = []
    rows[7] = jnp.zeros((HALF, COLS), F32)
    for p in range(4):
        ref, n = (own, 3 * p) if p < 2 else (far, 3 * p - 6)
        q = q1[p : p + 1]
        h1 = ref[n] + jnp.where(row == at_edge, jnp.where(top, RATIO, -RATIO) * q, 0.0)
        qy1 = jnp.where(row == lower_edge, q, ref[n + 2])
        rows[7, p : p + 1, :] = bed[:1] + h1[:1]
        levels.append((h1, ref[n + 1], qy1))
    q2 = flux(q_up, eta_up, rows[7], jnp.maximum(bed_up, bed[:1]), fric_up)
    q2 = jnp.where(2 * slab + c == 0, 0.0, q2)
    bed_x = jnp.maximum(bed, right_of(bed))
    bed_y = jnp.maximum(bed, jnp.where(last, bed_dn, below(bed)))
    fields = []
    for p, (h1, qx, qy) in enumerate(levels):
        eta = bed + h1
        qx = x_faces(qx, eta, bed_x, fric)
        qy = flux(qy, eta, jnp.where(last, eta_dn[p : p + 1], below(eta)), bed_y, fric)
        qy = jnp.where(row == grid_end, 0.0, qy)
        over = jnp.where(first, q2[p : p + 1], above(qy))
        fields.append((h1 + RATIO * ((left_of(qx) - qx) + (over - qy)), qx, qy))
    low, even = masks()
    for f in range(3):
        for t in range(NT):
            a = [fields[p][f][:, 128 * t : 128 * t + 128] for p in range(4)]
            b0, b2 = jnp.where(low, a[0], pltpu.roll(a[2], 4, 0)), jnp.where(low, pltpu.roll(a[0], 4, 0), a[2])
            b1, b3 = jnp.where(low, a[1], pltpu.roll(a[3], 4, 0)), jnp.where(low, pltpu.roll(a[1], 4, 0), a[3])
            pair = [
                jnp.where(even, b0, pltpu.roll(b1, 2, 0)),
                jnp.where(even, pltpu.roll(b0, 6, 0), b1),
                jnp.where(even, b2, pltpu.roll(b3, 2, 0)),
                jnp.where(even, pltpu.roll(b2, 6, 0), b3),
            ]
            for d in range(4):
                n = AT[(d, f, t)]
                packed[n // PER, n % PER] = pair[d]
    names = own[6, 4:5, 0:128] + far[6, 4:5, 0:128]
    for k, out in enumerate((o0, o1, o2, o3)):
        for j in range(4):
            out[PER * j : PER * j + PER] = packed[chunk_at(z, y, c, k, j)]
        out[4 * PER] = jnp.zeros((8, 128), F32)
        out[4 * PER, 0:1, :] = names


def masks():
    sub = lax.broadcasted_iota(jnp.int32, (8, 128), 0)
    return sub < 4, (sub & 2) == 0


def select_kernel(anc, a0, a1, a2, a3, o0, o1, o2, o3, cross, held):
    z, y, c = place()
    for j, a in enumerate((a0, a1, a2, a3)):
        held[4 * PER * j : 4 * PER * j + 4 * PER] = a[: 4 * PER]
    for s in range(2):
        core = c ^ s
        for k, out in enumerate((o0, o1, o2, o3)):
            for j in range(4):
                at = chunk_at(z, y, core, k, j)
                dest = ((at >> 2) << 3) | ((at & 3) << 1) | core
                for u in range(2):
                    name = anc[2 * dest + u]
                    dz = step_of(STEP_Z, (name >> 4) ^ z)
                    dy = step_of(STEP_Y, ((name >> 2) & 3) ^ y)
                    base = jnp.where(c == 0, dy * 4 + dz, dz * 4 + dy) * PER
                    v = pl.multiple_of((((name >> 1) & 1) ^ c) * 4 + (name & 1) * 2, 2)
                    got = held[pl.ds(base, PER), pl.ds(v, 2), :]
                    if s == 0:
                        out[PER * j : PER * j + PER, 2 * u : 2 * u + 2, :] = got
                    else:
                        n = PER * (4 * k + j)
                        cross[n : n + PER, 2 * u : 2 * u + 2, :] = got


def last_kernel(f0, f1, f2, f3, ho, xo, yo, packed):
    z, y, c = place()
    even = (lax.broadcasted_iota(jnp.int32, (8, 128), 0) & 2) == 0
    for j, ref in enumerate((f0, f1, f2, f3)):
        for k in range(4):
            for s in range(2):
                at = s * 16 * PER + chunk_at(z, y, c, k, j) * PER
                packed[pl.ds(at, PER)] = ref[PER * (2 * k + s) : PER * (2 * k + s) + PER]
    for s in range(2):
        rows = pl.ds(pl.multiple_of((c ^ s) * HALF, HALF), HALF)
        for f, out in enumerate((ho, xo, yo)):
            for t in range(NT):
                cols = slice(128 * t, 128 * t + 128)
                pair = [packed[s * 16 * PER + AT[(d, f, t)]] for d in range(4)]
                b0 = jnp.concatenate([pair[0], pair[2]], axis=0)
                b1 = jnp.concatenate([pair[1], pair[3]], axis=0)
                out[0, rows, cols] = jnp.where(even, b0, pltpu.roll(b1, 2, 0))
                out[1, rows, cols] = jnp.where(even, pltpu.roll(b0, 6, 0), b1)


def tiles(n):
    return jax.ShapeDtypeStruct((n, 8, 128), F32)


def params():
    return pltpu.CompilerParams(vmem_limit_bytes=32 * 1024 * 1024)


def outer_step(v, k):
    pairs = [(i, i ^ (STEP_Z[k] << 3 if i % 2 == 0 else STEP_Y[k] << 1)) for i in range(32)]
    return v if k == 0 else lax.ppermute(v, "dom", pairs)


def inner_step(v, k):
    pairs = [(i, i ^ (STEP_Y[k] << 1 if i % 2 == 0 else STEP_Z[k] << 3)) for i in range(32)]
    return v if k == 0 else lax.ppermute(v, "dom", pairs)


def other_core(v):
    return lax.ppermute(v, "dom", [(i, i ^ 1) for i in range(32)])


def next_slab(v):
    low = [((2 * chip + 1) * 8 + r, 2 * chip * 8 + r + 1) for chip in range(16) for r in range(7)]
    return lax.ppermute(v, ("dom", "rows"), low + [(b, a) for a, b in low])


def regroup(parts, count):
    return [jnp.concatenate([p[count * j : count * j + count] for p in parts]) for j in range(4)]


def shards(depth, x_flow, y_flow, elevation, roughness, wet, ancestors):
    state = jax.ShapeDtypeStruct((2, ROWS, COLS), F32)
    strip = jax.ShapeDtypeStruct((HALF, COLS), F32)
    halves = jax.ShapeDtypeStruct((7, HALF, COLS), F32)
    ground = jax.ShapeDtypeStruct((3, HALF, COLS), F32)
    args = (depth, x_flow, y_flow, wet, elevation, roughness, ancestors)
    keep, give, kept, given, terrain = pl.pallas_call(
        first_kernel,
        out_shape=[strip, strip, halves, halves, ground],
        in_specs=[HBM] * 7,
        out_specs=[VMEM] * 5,
        scratch_shapes=[pltpu.VMEM(v.shape, v.dtype) for v in args[:6]]
        + [pltpu.SMEM((2,), jnp.int32), pltpu.SemaphoreType.DMA((7,))],
        compiler_params=params(),
    )(*[pltpu.with_memory_space_constraint(v, pltpu.HBM) for v in args])
    mine = jnp.concatenate([keep, other_core(give)])
    far = other_core(given)
    arrived = next_slab(mine)
    parts = pl.pallas_call(
        second_kernel,
        out_shape=[tiles(4 * PER + 1)] * 4,
        in_specs=[VMEM] * 5,
        out_specs=[VMEM] * 4,
        scratch_shapes=[pltpu.VMEM((8, HALF, COLS), F32), pltpu.VMEM((16, PER, 8, 128), F32)],
        compiler_params=params(),
    )(kept, far, terrain, mine, arrived)
    parts = [outer_step(v, k) for k, v in enumerate(parts)]
    names = (parts[0][4 * PER] + parts[1][4 * PER]) + (parts[2][4 * PER] + parts[3][4 * PER])
    parts = [jnp.concatenate([v, names[None]]) for v in regroup(parts, PER)]
    parts = [inner_step(v, k) for k, v in enumerate(parts)]
    names = sum(v[4 * PER, 0, :64] for v in parts).astype(jnp.int32)
    four = lambda n: jax.ShapeDtypeStruct((n, 4, 128), F32)
    *parts, cross = pl.pallas_call(
        select_kernel,
        out_shape=[four(4 * PER)] * 4 + [four(16 * PER)],
        in_specs=[SMEM] + [VMEM] * 4,
        out_specs=[VMEM] * 5,
        scratch_shapes=[pltpu.VMEM((16 * PER, 8, 128), F32)],
        compiler_params=params(),
    )(names, *parts)
    cross = other_core(cross)
    parts = [
        jnp.concatenate(
            [w for j in range(4) for w in (v[PER * j : PER * j + PER], cross[PER * (4 * k + j) : PER * (4 * k + j) + PER])]
        )
        for k, v in enumerate(parts)
    ]
    parts = [outer_step(v, k) for k, v in enumerate(parts)]
    parts = [inner_step(v, k) for k, v in enumerate(regroup(parts, 2 * PER))]
    return tuple(
        pl.pallas_call(
            last_kernel,
            out_shape=[state] * 3,
            in_specs=[VMEM] * 4,
            out_specs=[VMEM] * 3,
            scratch_shapes=[pltpu.VMEM((2 * 16 * PER, 4, 128), F32)],
            compiler_params=params(),
        )(*parts)
    )


def solution(mesh):
    wide = P("dom", "rows", None)
    in_specs = (wide, wide, wide, P("rows", None), P("rows", None), wide, P("dom"))
    return jax.shard_map(shards, mesh=mesh, in_specs=in_specs, out_specs=(wide, wide, wide), check_vma=False)
```

```python
import jax
import jax.numpy as jnp
from jax import lax
from jax.experimental import pallas as pl
from jax.experimental.pallas import tpu as pltpu
from jax.sharding import PartitionSpec as P

GDT = 9.81 * 1.0
SPACING = 10.0
RATIO = 1.0 / 10.0
MIN_DEPTH = 0.05
MANNING = (0.02, 0.025, 0.03, 0.035, 0.045, 0.06, 0.08, 0.1)
ROWS, COLS = 16, 1536
NT = COLS // 128
F32 = jnp.float32

PER = 9
STEP_Z = (0, 2, 3, 1)
STEP_Y = (0, 2, 1, 3)
ITEMS = [(q, f, 3 * z + c) for z in range(4) for q in range(4) for f in range(3) for c in range(3)]
VMEM = pl.BlockSpec(memory_space=pltpu.VMEM)
SMEM = pl.BlockSpec(memory_space=pltpu.SMEM)
HBM = pl.BlockSpec(memory_space=pltpu.HBM)


def place():
    dom = lax.axis_index("dom")
    return dom >> 3, (dom >> 1) & 3, dom & 1


def flux(q, eta_a, eta_b, bed, fric):
    he = jnp.maximum(jnp.maximum(eta_a, eta_b) - bed, MIN_DEPTH)
    numer = q - (GDT / SPACING) * he * (eta_b - eta_a)
    denom = 1.0 + fric * jnp.abs(q) * jnp.exp2((-7.0 / 3.0) * jnp.log2(he))
    return numer / denom


def friction(rough):
    total = jnp.zeros(rough.shape, F32)
    for klass, n in enumerate(MANNING):
        total = jnp.where(rough == klass, F32(GDT * (n * n)), total)
    return total


def row_iota():
    return lax.broadcasted_iota(jnp.int32, (ROWS, COLS), 0)


def right_of(v):
    return pltpu.roll(v, COLS - 1, 1)


def left_of(v):
    return pltpu.roll(v, 1, 1)


def below(v):
    return pltpu.roll(v, ROWS - 1, 0)


def above(v):
    return pltpu.roll(v, 1, 0)


def last_col():
    return lax.broadcasted_iota(jnp.int32, (ROWS, COLS), 1) == COLS - 1


def x_faces(q, eta, bed_x, fric):
    return jnp.where(last_col(), 0.0, flux(q, eta, right_of(eta), bed_x, fric))


def chunk_at(z, y, c, outer, inner):
    return jnp.where(
        c == 0,
        (z ^ STEP_Z[outer]) * 4 + (y ^ STEP_Y[inner]),
        (z ^ STEP_Z[inner]) * 4 + (y ^ STEP_Y[outer]),
    )


def step_of(steps, distance):
    found = jnp.int32(0)
    for k in range(1, 4):
        found = jnp.where(distance == steps[k], k, found)
    return found


def first_kernel(
    depth_in, xf_in, yf_in, wet_in, elev_in, rough_in, anc_in, keep, give, up, down, h1o, x1o, y1o, frico, bedo, names,
    depth, xf, yf, wet, elev, rough, anc, sems,
):
    pairs = zip((elev_in, rough_in, depth_in, wet_in, xf_in, yf_in, anc_in), (elev, rough, depth, wet, xf, yf, anc))
    copies = [pltpu.make_async_copy(src, dst, sems.at[n]) for n, (src, dst) in enumerate(pairs)]
    for copy in copies:
        copy.start()
    for copy in copies:
        copy.wait()
    _, _, c = place()
    bed = elev[...]
    bedo[...] = bed
    fric = friction(rough[...])
    frico[...] = fric
    bed_x = jnp.maximum(bed, right_of(bed))
    bed_y = jnp.maximum(bed, below(bed))
    last_row = row_iota() == ROWS - 1
    down[6:7, :] = bed[ROWS - 1 :]
    down[7:8, :] = fric[ROWS - 1 :]
    up[...] = jnp.zeros_like(up)
    up[4:5, :] = bed[:1]
    for p in range(2):
        h0 = depth[p] * wet[p].astype(F32)
        qx, qy = xf[p], yf[p]
        down[3 * p : 3 * p + 1, :] = h0[ROWS - 1 :]
        down[3 * p + 1 : 3 * p + 2, :] = qy[ROWS - 1 :]
        up[2 * p : 2 * p + 1, :] = h0[:1]
        eta = bed + h0
        qx = x_faces(qx, eta, bed_x, fric)
        qy = jnp.where(last_row, 0.0, flux(qy, eta, below(eta), bed_y, fric))
        h1 = h0 + RATIO * ((left_of(qx) - qx) + (above(qy) - qy))
        down[3 * p + 2 : 3 * p + 3, :] = h1[ROWS - 1 :]
        up[2 * p + 1 : 2 * p + 2, :] = h1[:1]
        h1o[p] = h1
        x1o[p] = qx
        y1o[p] = qy
    sub = lax.broadcasted_iota(jnp.int32, (8, 128), 0)
    lane = lax.broadcasted_iota(jnp.int32, (8, 128), 1)
    at = 2 * lax.axis_index("dom")
    mine = jnp.where(lane == at, anc[0].astype(F32), 0.0) + jnp.where(lane == at + 1, anc[1].astype(F32), 0.0)
    names[0] = jnp.where(sub == 0, mine, 0.0)
    keep[...] = jnp.where(c == 0, down[...], up[...])
    give[...] = jnp.where(c == 0, up[...], down[...])


def pack_kernel(h1, x1, y1, names, got, o0, o1, o2, o3, packed):
    z, y, c = place()
    low = lax.broadcasted_iota(jnp.int32, (8, 128), 0) < 4
    fields = (h1, x1, y1)
    for n, (q, f, col) in enumerate(ITEMS):
        r, s = q // 2, q % 2
        a = fields[f][0, 8 * r : 8 * r + 8, 128 * col : 128 * col + 128]
        b = fields[f][1, 8 * r : 8 * r + 8, 128 * col : 128 * col + 128]
        tile = jnp.where(low, a, pltpu.roll(b, 4, 0)) if s == 0 else jnp.where(low, pltpu.roll(a, 4, 0), b)
        packed[n // PER, n % PER] = tile
    for k, out in enumerate((o0, o1, o2, o3)):
        for j in range(4):
            out[PER * j : PER * j + PER] = packed[chunk_at(z, y, c, k, j)]
        out[4 * PER] = names[0]


def edge_kernel(fric, bed, own_up, own_down, mine, theirs, strips, beyond, rows, sq, sa, sb, sz, sf):
    _, _, c = place()
    slab = lax.axis_index("rows")
    down = jnp.where(c == 0, mine[...], theirs[...])
    up = jnp.where(c == 0, theirs[...], mine[...])
    bed_up, fric_up, bed_dn = down[6:7], down[7:8], up[4:5]
    beyond[...] = jnp.zeros((8, COLS), F32)
    beyond[0:1, :] = bed_up
    beyond[1:2, :] = fric_up
    beyond[2:3, :] = bed_dn
    for s in (sq, sa, sb, sz, sf):
        s[...] = jnp.zeros((8, COLS), F32)
    first, last = bed[0:1, :], bed[ROWS - 1 : ROWS, :]
    for p in range(2):
        t, b = 2 * p, 2 * p + 1
        sq[t : t + 1, :] = down[3 * p + 1 : 3 * p + 2]
        sa[t : t + 1, :] = bed_up + down[3 * p : 3 * p + 1]
        sb[t : t + 1, :] = first + own_up[2 * p : 2 * p + 1, :]
        sz[t : t + 1, :] = jnp.maximum(bed_up, first)
        sf[t : t + 1, :] = fric_up
        sq[b : b + 1, :] = own_down[3 * p + 1 : 3 * p + 2, :]
        sa[b : b + 1, :] = last + own_down[3 * p : 3 * p + 1, :]
        sb[b : b + 1, :] = bed_dn + up[2 * p : 2 * p + 1]
        sz[b : b + 1, :] = jnp.maximum(last, bed_dn)
        sf[b : b + 1, :] = fric[ROWS - 1 : ROWS, :]
    edge = lax.broadcasted_iota(jnp.int32, (8, COLS), 0) & 1
    dead = edge == jnp.where(slab == 0, 0, jnp.where(slab == 7, 1, 2))
    q1 = jnp.where(dead, 0.0, flux(sq[...], sa[...], sb[...], sz[...], sf[...]))
    for p in range(2):
        q_top, q_bot = q1[2 * p : 2 * p + 1], q1[2 * p + 1 : 2 * p + 2]
        rows[4 * p : 4 * p + 1, :] = q_top
        rows[4 * p + 1 : 4 * p + 2, :] = down[3 * p + 2 : 3 * p + 3] - RATIO * q_top
        rows[4 * p + 2 : 4 * p + 3, :] = q_bot
        rows[4 * p + 3 : 4 * p + 4, :] = up[2 * p + 1 : 2 * p + 2] + RATIO * q_bot
    for t in range(NT):
        strips[t] = rows[:, 128 * t : 128 * t + 128]


def source_of(name, z, y):
    dz, dy = step_of(STEP_Z, (name >> 4) ^ z), step_of(STEP_Y, ((name >> 2) & 3) ^ y)
    return dz, dy, (name >> 1) & 1, name & 1


def select_kernel(anc, m0, m1, m2, m3, t0, t1, t2, t3, o0, o1, o2, o3, e0, e1, e2, e3, held, strips):
    z, y, c = place()
    for n, refs in enumerate(((m0, m1, m2, m3), (t0, t1, t2, t3))):
        for j, ref in enumerate(refs):
            held[n, 4 * PER * j : 4 * PER * j + 4 * PER] = ref[: 4 * PER]
            strips[4 * n + j] = ref[4 * PER + 1 : 4 * PER + 1 + NT]
    low = lax.broadcasted_iota(jnp.int32, (PER, 8, 128), 1) < 4
    low_strip = lax.broadcasted_iota(jnp.int32, (NT, 8, 128), 1) < 4

    def strip(dest, outer):
        halves = []
        for p in range(2):
            dz, dy, _, slot = source_of(anc[2 * dest + p], z, y)
            at = jnp.where(c == 0, dy, dz) if outer else 4 + jnp.where(c == 0, dz, dy)
            got = strips[at]
            halves.append(jnp.where(slot == p, got, pltpu.roll(got, 4, 1)))
        return jnp.where(low_strip, halves[0], halves[1])

    for k, (out, extra) in enumerate(zip((o0, o1, o2, o3), (e0, e1, e2, e3))):
        for j in range(4):
            at = chunk_at(z, y, c, k, j)
            dest = ((at >> 2) << 3) | ((at & 3) << 1) | c
            halves = []
            for p in range(2):
                dz, dy, sc, slot = source_of(anc[2 * dest + p], z, y)
                base = jnp.where(sc == 0, dy * 4 + dz, dz * 4 + dy) * PER
                got = held[sc ^ c, pl.ds(base, PER)]
                halves.append(jnp.where(slot == p, got, pltpu.roll(got, 4, 1)))
            out[PER * j : PER * j + PER] = jnp.where(low, halves[0], halves[1])
            if j == 0:
                out[4 * PER : 4 * PER + NT] = strip(dest, True)
            if k == 0:
                (e0, e1, e2, e3)[j][...] = strip(dest, False)


def last_kernel(
    anc, f0, f1, f2, f3, g0, g1, g2, g3, fric_in, bed_in, beyond, ho, xo, yo, packed, strips, rows, state, side
):
    z, y, c = place()
    slab = lax.axis_index("rows")
    for j, ref in enumerate((f0, f1, f2, f3)):
        for k in range(4):
            packed[chunk_at(z, y, c, k, j)] = ref[PER * k : PER * k + PER]
        strips[4 + j] = ref[4 * PER : 4 * PER + NT]
    for k, ref in enumerate((g0, g1, g2, g3)):
        strips[k] = ref[4 * PER : 4 * PER + NT]
    low = lax.broadcasted_iota(jnp.int32, (8, 128), 0) < 4
    at = []
    for p in range(2):
        dz, dy, sc, _ = source_of(anc[p], z, y)
        at.append(jnp.where(sc == c, jnp.where(c == 0, dz, dy), 4 + jnp.where(c == 0, dy, dz)))
    for t in range(NT):
        rows[:, 128 * t : 128 * t + 128] = jnp.where(low, strips[at[0], t], strips[at[1], t])
    where = {item: (n // PER, n % PER) for n, item in enumerate(ITEMS)}
    for f in range(3):
        for r in range(2):
            for col in range(NT):
                upper = packed[where[(2 * r, f, col)]]
                lower = packed[where[(2 * r + 1, f, col)]]
                part = (slice(8 * r, 8 * r + 8), slice(128 * col, 128 * col + 128))
                state[(f,) + part] = jnp.where(low, upper, pltpu.roll(lower, 4, 0))
                state[(3 + f,) + part] = jnp.where(low, pltpu.roll(upper, 4, 0), lower)
    bed, fric = bed_in[...], fric_in[...]
    bed_up, fric_up, bed_dn = beyond[0:1, :], beyond[1:2, :], beyond[2:3, :]
    row = row_iota()
    first_row, last_row = row == 0, row == ROWS - 1
    bed_x = jnp.maximum(bed, right_of(bed))
    bed_y = jnp.maximum(bed, jnp.where(last_row, bed_dn, below(bed)))
    side[...] = jnp.zeros((3, 8, COLS), F32)
    levels = []
    for p in range(2):
        q_top, q_bot = rows[4 * p : 4 * p + 1, :], rows[4 * p + 2 : 4 * p + 3, :]
        h1 = state[3 * p] + RATIO * jnp.where(first_row, q_top, jnp.where(last_row, -q_bot, 0.0))
        side[0, p : p + 1, :] = q_top
        side[1, p : p + 1, :] = bed_up + rows[4 * p + 1 : 4 * p + 2, :]
        side[2, p : p + 1, :] = bed[:1] + h1[:1]
        levels.append((h1, jnp.where(last_row, q_bot, state[3 * p + 2]), bed_dn + rows[4 * p + 3 : 4 * p + 4, :]))
    q2 = flux(side[0], side[1], side[2], jnp.maximum(bed_up, bed[:1]), fric_up)
    q2 = jnp.where(slab == 0, 0.0, q2)
    grid_end = jnp.where(slab == 7, ROWS - 1, -1)
    for p, (h1, qy1, eta_dn) in enumerate(levels):
        eta = bed + h1
        qx = x_faces(state[3 * p + 1], eta, bed_x, fric)
        qy = flux(qy1, eta, jnp.where(last_row, eta_dn, below(eta)), bed_y, fric)
        qy = jnp.where(row == grid_end, 0.0, qy)
        over = jnp.where(first_row, q2[p : p + 1], above(qy))
        ho[p] = h1 + RATIO * ((left_of(qx) - qx) + (over - qy))
        xo[p] = qx
        yo[p] = qy


def tiles(n):
    return jax.ShapeDtypeStruct((n, 8, 128), F32)


def params():
    return pltpu.CompilerParams(vmem_limit_bytes=32 * 1024 * 1024)


def outer_step(v, k):
    return v if k == 0 else lax.ppermute(v, "dom", [(i, i ^ (STEP_Z[k] << 3 if i % 2 == 0 else STEP_Y[k] << 1)) for i in range(32)])


def inner_step(v, k):
    return v if k == 0 else lax.ppermute(v, "dom", [(i, i ^ (STEP_Y[k] << 1 if i % 2 == 0 else STEP_Z[k] << 3)) for i in range(32)])


def other_core(v):
    return lax.ppermute(v, "dom", [(i, i ^ 1) for i in range(32)])


def to_slabs(v):
    pairs = [(d * 8 + r, d * 8 + r + (1 if d % 2 == 0 else -1)) for d in range(32) for r in range(8)]
    return lax.ppermute(v, ("dom", "rows"), [(a, b) for a, b in pairs if a // 8 == b // 8 and b >= 0])


def regroup(parts, count=PER):
    return [jnp.concatenate([p[count * j : count * j + count] for p in parts]) for j in range(4)]


def shards(depth, x_flow, y_flow, elevation, roughness, wet, ancestors):
    state = jax.ShapeDtypeStruct((2, ROWS, COLS), F32)
    strip = jax.ShapeDtypeStruct((8, COLS), F32)
    plane = jax.ShapeDtypeStruct((ROWS, COLS), F32)
    vm = lambda s: pltpu.VMEM(s.shape, s.dtype)
    args = (depth, x_flow, y_flow, wet, elevation, roughness, ancestors)
    keep, give, up, down, h1, x1, y1, fric, bed, names = pl.pallas_call(
        first_kernel,
        out_shape=[strip] * 4 + [state] * 3 + [plane] * 2 + [tiles(1)],
        in_specs=[HBM] * 7,
        out_specs=[VMEM] * 10,
        scratch_shapes=[pltpu.VMEM(v.shape, v.dtype) for v in args[:6]]
        + [pltpu.SMEM((2,), jnp.int32), pltpu.SemaphoreType.DMA((7,))],
        compiler_params=params(),
    )(*[pltpu.with_memory_space_constraint(v, pltpu.HBM) for v in args])
    got = other_core(give)
    arrived = to_slabs(jnp.concatenate([keep, got]))
    theirs = other_core(arrived[8:])
    parts = pl.pallas_call(
        pack_kernel,
        out_shape=[tiles(4 * PER + 1)] * 4,
        in_specs=[VMEM] * 5,
        out_specs=[VMEM] * 4,
        scratch_shapes=[pltpu.VMEM((16, PER, 8, 128), F32)],
        compiler_params=params(),
    )(h1, x1, y1, names, got)
    parts = [outer_step(v, k) for k, v in enumerate(parts)]
    strips, beyond = pl.pallas_call(
        edge_kernel,
        out_shape=[tiles(NT), strip],
        in_specs=[VMEM] * 6,
        out_specs=[VMEM] * 2,
        scratch_shapes=[vm(strip)] * 6,
        compiler_params=params(),
    )(fric, bed, up, down, arrived[:8], theirs)
    names = (parts[0][4 * PER] + parts[1][4 * PER]) + (parts[2][4 * PER] + parts[3][4 * PER])
    parts = [jnp.concatenate([v, names[None], strips]) for v in regroup(parts)]
    parts = [inner_step(v, k) for k, v in enumerate(parts)]
    others = [other_core(v) for v in parts]
    names = sum(v[4 * PER, 0, :64] for v in parts + others).astype(jnp.int32)
    out = pl.pallas_call(
        select_kernel,
        out_shape=[tiles(4 * PER + NT)] * 4 + [tiles(NT)] * 4,
        in_specs=[SMEM] + [VMEM] * 8,
        out_specs=[VMEM] * 8,
        scratch_shapes=[pltpu.VMEM((2, 16 * PER, 8, 128), F32), pltpu.VMEM((8, NT, 8, 128), F32)],
        compiler_params=params(),
    )(names, *parts, *others)
    first = [outer_step(v, k) for k, v in enumerate(out[:4])]
    second = [jnp.concatenate([v, w]) for v, w in zip(regroup(first), out[4:])]
    second = [inner_step(v, k) for k, v in enumerate(second)]
    return tuple(
        pl.pallas_call(
            last_kernel,
            out_shape=[state] * 3,
            in_specs=[SMEM] + [VMEM] * 11,
            out_specs=[VMEM] * 3,
            scratch_shapes=[
                pltpu.VMEM((16, PER, 8, 128), F32),
                pltpu.VMEM((8, NT, 8, 128), F32),
                vm(strip),
                pltpu.VMEM((6, ROWS, COLS), F32),
                pltpu.VMEM((3, 8, COLS), F32),
            ],
            compiler_params=params(),
        )(ancestors, *second, *first, fric, bed, beyond)
    )


def solution(mesh):
    wide = P("dom", "rows", None)
    in_specs = (wide, wide, wide, P("rows", None), P("rows", None), wide, P("dom"))
    return jax.shard_map(shards, mesh=mesh, in_specs=in_specs, out_specs=(wide, wide, wide), check_vma=False)
```

```python
import jax
import jax.numpy as jnp
from jax import lax
from jax.experimental import pallas as pl
from jax.experimental.pallas import tpu as pltpu
from jax.sharding import PartitionSpec as P

GDT = 9.81 * 1.0
SPACING = 10.0
RATIO = 1.0 / 10.0
MIN_DEPTH = 0.05
MANNING = (0.02, 0.025, 0.03, 0.035, 0.045, 0.06, 0.08, 0.1)
ROWS, COLS, HALF = 16, 1536, 8
NT = COLS // 128
F32 = jnp.float32

PER = 9
ITEMS = [(d, f, 3 * z + t) for z in range(4) for d in range(4) for f in range(3) for t in range(3)]
AT = {item: n for n, item in enumerate(ITEMS)}
STEP_Z = (0, 2, 3, 1)
STEP_Y = (0, 2, 1, 3)
VMEM = pl.BlockSpec(memory_space=pltpu.VMEM)
SMEM = pl.BlockSpec(memory_space=pltpu.SMEM)
HBM = pl.BlockSpec(memory_space=pltpu.HBM)


def place():
    dom = lax.axis_index("dom")
    return dom >> 3, (dom >> 1) & 3, dom & 1


def flux(q, eta_a, eta_b, bed, fric):
    he = jnp.maximum(jnp.maximum(eta_a, eta_b) - bed, MIN_DEPTH)
    numer = q - (GDT / SPACING) * he * (eta_b - eta_a)
    denom = 1.0 + fric * jnp.abs(q) * jnp.exp2((-7.0 / 3.0) * jnp.log2(he))
    return numer / denom


def friction(rough):
    total = jnp.zeros(rough.shape, F32)
    for klass, n in enumerate(MANNING):
        total = jnp.where(rough == klass, F32(GDT * (n * n)), total)
    return total


def right_of(v):
    return pltpu.roll(v, COLS - 1, 1)


def left_of(v):
    return pltpu.roll(v, 1, 1)


def below(v):
    return pltpu.roll(v, v.shape[0] - 1, 0)


def above(v):
    return pltpu.roll(v, 1, 0)


def x_faces(q, eta, bed_x, fric):
    last = lax.broadcasted_iota(jnp.int32, q.shape, 1) == COLS - 1
    return jnp.where(last, 0.0, flux(q, eta, right_of(eta), bed_x, fric))


def chunk_at(z, y, c, outer, inner):
    return jnp.where(
        c == 0,
        (z ^ STEP_Z[outer]) * 4 + (y ^ STEP_Y[inner]),
        (z ^ STEP_Z[inner]) * 4 + (y ^ STEP_Y[outer]),
    )


def step_of(steps, distance):
    found = jnp.int32(0)
    for k in range(1, 4):
        found = jnp.where(distance == steps[k], k, found)
    return found


def first_kernel(
    depth_in, xf_in, yf_in, wet_in, elev_in, rough_in, anc_in, keep, give, kept, given, terrain,
    depth, xf, yf, wet, elev, rough, anc, sems,
):
    pairs = zip(
        (elev_in, rough_in, depth_in, wet_in, xf_in, yf_in, anc_in), (elev, rough, depth, wet, xf, yf, anc)
    )
    copies = [pltpu.make_async_copy(src, dst, sems.at[n]) for n, (src, dst) in enumerate(pairs)]
    for copy in copies:
        copy.start()
    for copy in copies:
        copy.wait()
    _, _, c = place()
    top = c == 0
    bed = elev[...]
    fric = friction(rough[...])
    bed_x = jnp.maximum(bed, right_of(bed))
    bed_y = jnp.maximum(bed, below(bed))
    end = ROWS - 1
    last_row = lax.broadcasted_iota(jnp.int32, (ROWS, COLS), 0) == end
    terrain[0] = jnp.where(top, bed[:HALF], bed[HALF:])
    terrain[1] = jnp.where(top, fric[:HALF], fric[HALF:])
    terrain[2] = jnp.zeros((HALF, COLS), F32)
    terrain[2, 0:1, :] = jnp.where(top, bed[HALF : HALF + 1], bed[HALF - 1 : HALF])
    terrain[2, 1:2, :] = jnp.where(top, fric[HALF : HALF + 1], fric[HALF - 1 : HALF])
    lane = lax.broadcasted_iota(jnp.int32, (1, COLS), 1)
    at = 2 * lax.axis_index("dom")
    names = jnp.where(lane == at, anc[0].astype(F32), 0.0) + jnp.where(lane == at + 1, anc[1].astype(F32), 0.0)
    kept[6] = jnp.zeros((HALF, COLS), F32)
    given[6] = jnp.zeros((HALF, COLS), F32)
    kept[6, 4:5, :] = names
    given[6, 4:5, :] = names

    def edge(row, upper, lower):
        keep[row : row + 1, :] = jnp.where(top, upper, lower)
        give[row : row + 1, :] = jnp.where(top, lower, upper)

    zero = jnp.zeros((1, COLS), F32)
    edge(6, bed[:1], bed[end:])
    edge(7, fric[:1], fric[end:])
    for p in range(2):
        h0 = depth[p] * wet[p].astype(F32)
        qx, qy = xf[p], yf[p]
        edge(p, h0[:1], h0[end:])
        edge(4 + p, zero, qy[end:])
        eta = bed + h0
        qx = x_faces(qx, eta, bed_x, fric)
        qy = jnp.where(last_row, 0.0, flux(qy, eta, below(eta), bed_y, fric))
        h1 = h0 + RATIO * ((left_of(qx) - qx) + (above(qy) - qy))
        edge(2 + p, h1[:1], h1[end:])
        for f, v in enumerate((h1, qx, qy)):
            kept[3 * p + f] = jnp.where(top, v[:HALF], v[HALF:])
            given[3 * p + f] = jnp.where(top, v[HALF:], v[:HALF])
        kept[6, p : p + 1, :] = jnp.where(top, h1[HALF : HALF + 1], h1[HALF - 1 : HALF])
        given[6, p : p + 1, :] = jnp.where(top, h1[HALF - 1 : HALF], h1[HALF : HALF + 1])
        kept[6, 2 + p : 3 + p, :] = jnp.where(top, zero, qy[HALF - 1 : HALF])
        given[6, 2 + p : 3 + p, :] = jnp.where(top, qy[HALF - 1 : HALF], zero)


def second_kernel(own, far, terrain, mine, next_slab, o0, o1, o2, o3, rows, packed):
    z, y, c = place()
    top = c == 0
    slab = lax.axis_index("rows")
    bed, fric = terrain[0], terrain[1]
    bed_in, fric_in = terrain[2, 0:1, :], terrain[2, 1:2, :]
    row = lax.broadcasted_iota(jnp.int32, (HALF, COLS), 0)
    first, last = row == 0, row == HALF - 1
    at_edge = jnp.where(top, 0, HALF - 1)
    lower_edge = jnp.where(top, -1, HALF - 1)
    grid_end = jnp.where(slab == 7, lower_edge, -1)

    def rows_of(n, a, b):
        rows[n] = jnp.zeros((HALF, COLS), F32)
        rows[n, 0:2, :] = a
        rows[n, 2:4, :] = b
        return rows[n]

    in_h = rows_of(0, own[6, 0:2, :], far[6, 0:2, :])
    in_q = rows_of(1, own[6, 2:4, :], far[6, 2:4, :])
    out_h0 = rows_of(2, next_slab[8:10, :], next_slab[0:2, :])
    out_h1 = rows_of(3, next_slab[10:12, :], next_slab[2:4, :])
    out_q = rows_of(4, next_slab[12:14, :], next_slab[4:6, :])
    my_h = rows_of(5, mine[0:2, :], mine[8:10, :])
    my_q = rows_of(6, mine[4:6, :], mine[12:14, :])
    bed_out, fric_out = next_slab[6:7, :], next_slab[7:8, :]
    bed_mine = jnp.where(top, bed[:1], bed[HALF - 1 :])
    eta_mine, eta_out = bed_mine + my_h, bed_out + out_h0
    q1 = flux(
        jnp.where(top, out_q, my_q),
        jnp.where(top, eta_out, eta_mine),
        jnp.where(top, eta_mine, eta_out),
        jnp.maximum(bed_mine, bed_out),
        jnp.where(top, fric_out, fric[HALF - 1 :]),
    )
    q1 = jnp.where(jnp.where(top, slab, 7 - slab) == 0, 0.0, q1)
    out_h = out_h1 + jnp.where(top, -RATIO, RATIO) * q1
    bed_up, fric_up = jnp.where(top, bed_out, bed_in), jnp.where(top, fric_out, fric_in)
    bed_dn = jnp.where(top, bed_in, bed_out)
    eta_up = bed_up + jnp.where(top, out_h, in_h)
    eta_dn = bed_dn + jnp.where(top, in_h, out_h)
    q_up = jnp.where(top, q1, in_q)
    levels = []
    rows[7] = jnp.zeros((HALF, COLS), F32)
    for p in range(4):
        ref, n = (own, 3 * p) if p < 2 else (far, 3 * p - 6)
        q = q1[p : p + 1]
        h1 = ref[n] + jnp.where(row == at_edge, jnp.where(top, RATIO, -RATIO) * q, 0.0)
        qy1 = jnp.where(row == lower_edge, q, ref[n + 2])
        rows[7, p : p + 1, :] = bed[:1] + h1[:1]
        levels.append((h1, ref[n + 1], qy1))
    q2 = flux(q_up, eta_up, rows[7], jnp.maximum(bed_up, bed[:1]), fric_up)
    q2 = jnp.where(2 * slab + c == 0, 0.0, q2)
    bed_x = jnp.maximum(bed, right_of(bed))
    bed_y = jnp.maximum(bed, jnp.where(last, bed_dn, below(bed)))
    fields = []
    for p, (h1, qx, qy) in enumerate(levels):
        eta = bed + h1
        qx = x_faces(qx, eta, bed_x, fric)
        qy = flux(qy, eta, jnp.where(last, eta_dn[p : p + 1], below(eta)), bed_y, fric)
        qy = jnp.where(row == grid_end, 0.0, qy)
        over = jnp.where(first, q2[p : p + 1], above(qy))
        fields.append((h1 + RATIO * ((left_of(qx) - qx) + (over - qy)), qx, qy))
    low, even = masks()
    for f in range(3):
        for t in range(NT):
            a = [fields[p][f][:, 128 * t : 128 * t + 128] for p in range(4)]
            b0, b2 = jnp.where(low, a[0], pltpu.roll(a[2], 4, 0)), jnp.where(low, pltpu.roll(a[0], 4, 0), a[2])
            b1, b3 = jnp.where(low, a[1], pltpu.roll(a[3], 4, 0)), jnp.where(low, pltpu.roll(a[1], 4, 0), a[3])
            pair = [
                jnp.where(even, b0, pltpu.roll(b1, 2, 0)),
                jnp.where(even, pltpu.roll(b0, 6, 0), b1),
                jnp.where(even, b2, pltpu.roll(b3, 2, 0)),
                jnp.where(even, pltpu.roll(b2, 6, 0), b3),
            ]
            for d in range(4):
                n = AT[(d, f, t)]
                packed[n // PER, n % PER] = pair[d]
    names = own[6, 4:5, 0:128] + far[6, 4:5, 0:128]
    for k, out in enumerate((o0, o1, o2, o3)):
        for j in range(4):
            out[PER * j : PER * j + PER] = packed[chunk_at(z, y, c, k, j)]
        out[4 * PER] = jnp.zeros((8, 128), F32)
        out[4 * PER, 0:1, :] = names


def masks():
    sub = lax.broadcasted_iota(jnp.int32, (8, 128), 0)
    return sub < 4, (sub & 2) == 0


def select_kernel(anc, m0, m1, m2, m3, t0, t1, t2, t3, o0, o1, o2, o3, held):
    z, y, c = place()
    for n, refs in enumerate(((m0, m1, m2, m3), (t0, t1, t2, t3))):
        for j, ref in enumerate(refs):
            held[n, 4 * PER * j : 4 * PER * j + 4 * PER] = ref[: 4 * PER]
    for k, out in enumerate((o0, o1, o2, o3)):
        for j in range(4):
            at = chunk_at(z, y, c, k, j)
            dest = ((at >> 2) << 3) | ((at & 3) << 1) | c
            for u in range(2):
                name = anc[2 * dest + u]
                dz = step_of(STEP_Z, (name >> 4) ^ z)
                dy = step_of(STEP_Y, ((name >> 2) & 3) ^ y)
                for n in range(2):
                    core = c ^ n
                    base = jnp.where(core == 0, dy * 4 + dz, dz * 4 + dy) * PER
                    v = pl.multiple_of((((name >> 1) & 1) ^ core) * 4 + (name & 1) * 2, 2)
                    row = 4 * n + 2 * u
                    out[PER * j : PER * j + PER, row : row + 2, :] = held[n, pl.ds(base, PER), pl.ds(v, 2), :]


def last_kernel(f0, f1, f2, f3, ho, xo, yo, packed):
    z, y, c = place()
    low, even = masks()
    for j, ref in enumerate((f0, f1, f2, f3)):
        for k in range(4):
            packed[pl.ds(chunk_at(z, y, c, k, j) * PER, PER)] = ref[PER * k : PER * k + PER]
    for f, out in enumerate((ho, xo, yo)):
        for t in range(NT):
            cols = slice(128 * t, 128 * t + 128)
            pair = [packed[AT[(d, f, t)]] for d in range(4)]
            for n in range(2):
                rows = pl.ds(pl.multiple_of((c ^ n) * HALF, HALF), HALF)
                if n == 0:
                    b0 = jnp.where(low, pair[0], pltpu.roll(pair[2], 4, 0))
                    b1 = jnp.where(low, pair[1], pltpu.roll(pair[3], 4, 0))
                else:
                    b0 = jnp.where(low, pltpu.roll(pair[0], 4, 0), pair[2])
                    b1 = jnp.where(low, pltpu.roll(pair[1], 4, 0), pair[3])
                out[0, rows, cols] = jnp.where(even, b0, pltpu.roll(b1, 2, 0))
                out[1, rows, cols] = jnp.where(even, pltpu.roll(b0, 6, 0), b1)


def tiles(n):
    return jax.ShapeDtypeStruct((n, 8, 128), F32)


def params():
    return pltpu.CompilerParams(vmem_limit_bytes=32 * 1024 * 1024)


def outer_step(v, k):
    pairs = [(i, i ^ (STEP_Z[k] << 3 if i % 2 == 0 else STEP_Y[k] << 1)) for i in range(32)]
    return v if k == 0 else lax.ppermute(v, "dom", pairs)


def inner_step(v, k):
    pairs = [(i, i ^ (STEP_Y[k] << 1 if i % 2 == 0 else STEP_Z[k] << 3)) for i in range(32)]
    return v if k == 0 else lax.ppermute(v, "dom", pairs)


def other_core(v):
    return lax.ppermute(v, "dom", [(i, i ^ 1) for i in range(32)])


def next_slab(v):
    low = [((2 * chip + 1) * 8 + r, 2 * chip * 8 + r + 1) for chip in range(16) for r in range(7)]
    return lax.ppermute(v, ("dom", "rows"), low + [(b, a) for a, b in low])


def regroup(parts, count):
    return [jnp.concatenate([p[count * j : count * j + count] for p in parts]) for j in range(4)]


def shards(depth, x_flow, y_flow, elevation, roughness, wet, ancestors):
    state = jax.ShapeDtypeStruct((2, ROWS, COLS), F32)
    strip = jax.ShapeDtypeStruct((HALF, COLS), F32)
    halves = jax.ShapeDtypeStruct((7, HALF, COLS), F32)
    ground = jax.ShapeDtypeStruct((3, HALF, COLS), F32)
    args = (depth, x_flow, y_flow, wet, elevation, roughness, ancestors)
    keep, give, kept, given, terrain = pl.pallas_call(
        first_kernel,
        out_shape=[strip, strip, halves, halves, ground],
        in_specs=[HBM] * 7,
        out_specs=[VMEM] * 5,
        scratch_shapes=[pltpu.VMEM(v.shape, v.dtype) for v in args[:6]]
        + [pltpu.SMEM((2,), jnp.int32), pltpu.SemaphoreType.DMA((7,))],
        compiler_params=params(),
    )(*[pltpu.with_memory_space_constraint(v, pltpu.HBM) for v in args])
    mine = jnp.concatenate([keep, other_core(give)])
    far = other_core(given)
    arrived = next_slab(mine)
    parts = pl.pallas_call(
        second_kernel,
        out_shape=[tiles(4 * PER + 1)] * 4,
        in_specs=[VMEM] * 5,
        out_specs=[VMEM] * 4,
        scratch_shapes=[pltpu.VMEM((8, HALF, COLS), F32), pltpu.VMEM((16, PER, 8, 128), F32)],
        compiler_params=params(),
    )(kept, far, terrain, mine, arrived)
    parts = [outer_step(v, k) for k, v in enumerate(parts)]
    names = (parts[0][4 * PER] + parts[1][4 * PER]) + (parts[2][4 * PER] + parts[3][4 * PER])
    parts = [jnp.concatenate([v, names[None]]) for v in regroup(parts, PER)]
    parts = [inner_step(v, k) for k, v in enumerate(parts)]
    names = sum(v[4 * PER, 0, :64] for v in parts).astype(jnp.int32)
    others = [other_core(v) for v in parts]
    parts = pl.pallas_call(
        select_kernel,
        out_shape=[tiles(4 * PER)] * 4,
        in_specs=[SMEM] + [VMEM] * 8,
        out_specs=[VMEM] * 4,
        scratch_shapes=[pltpu.VMEM((2, 16 * PER, 8, 128), F32)],
        compiler_params=params(),
    )(names, *parts, *others)
    parts = [outer_step(v, k) for k, v in enumerate(parts)]
    parts = [inner_step(v, k) for k, v in enumerate(regroup(parts, PER))]
    return tuple(
        pl.pallas_call(
            last_kernel,
            out_shape=[state] * 3,
            in_specs=[VMEM] * 4,
            out_specs=[VMEM] * 3,
            scratch_shapes=[pltpu.VMEM((16 * PER, 8, 128), F32)],
            compiler_params=params(),
        )(*parts)
    )


def solution(mesh):
    wide = P("dom", "rows", None)
    in_specs = (wide, wide, wide, P("rows", None), P("rows", None), wide, P("dom"))
    return jax.shard_map(shards, mesh=mesh, in_specs=in_specs, out_specs=(wide, wide, wide), check_vma=False)
```

```python
import jax
import jax.numpy as jnp
from jax import lax
from jax.experimental import pallas as pl
from jax.experimental.pallas import tpu as pltpu
from jax.sharding import PartitionSpec as P

GDT = 9.81 * 1.0
SPACING = 10.0
RATIO = 1.0 / 10.0
MIN_DEPTH = 0.05
MANNING = (0.02, 0.025, 0.03, 0.035, 0.045, 0.06, 0.08, 0.1)
ROWS, COLS, HALF = 16, 1536, 8
NT = COLS // 128
F32 = jnp.float32

PER = 9
ITEMS = [(d, f, 3 * z + t) for z in range(4) for d in range(4) for f in range(3) for t in range(3)]
AT = {item: n for n, item in enumerate(ITEMS)}
STEP_Z = (0, 2, 3, 1)
STEP_Y = (0, 2, 1, 3)
LATE_Z = (0, 2, 1, 3)
VMEM = pl.BlockSpec(memory_space=pltpu.VMEM)
SMEM = pl.BlockSpec(memory_space=pltpu.SMEM)
HBM = pl.BlockSpec(memory_space=pltpu.HBM)


def place():
    dom = lax.axis_index("dom")
    return dom >> 3, (dom >> 1) & 3, dom & 1


def flux(q, eta_a, eta_b, bed, fric):
    he = jnp.maximum(jnp.maximum(eta_a, eta_b) - bed, MIN_DEPTH)
    numer = q - (GDT / SPACING) * he * (eta_b - eta_a)
    denom = 1.0 + fric * jnp.abs(q) * jnp.exp2((-7.0 / 3.0) * jnp.log2(he))
    return numer / denom


def friction(rough):
    total = jnp.zeros(rough.shape, F32)
    for klass, n in enumerate(MANNING):
        total = jnp.where(rough == klass, F32(GDT * (n * n)), total)
    return total


def right_of(v):
    return pltpu.roll(v, COLS - 1, 1)


def left_of(v):
    return pltpu.roll(v, 1, 1)


def below(v):
    return pltpu.roll(v, v.shape[0] - 1, 0)


def above(v):
    return pltpu.roll(v, 1, 0)


def x_faces(q, eta, bed_x, fric):
    last = lax.broadcasted_iota(jnp.int32, q.shape, 1) == COLS - 1
    return jnp.where(last, 0.0, flux(q, eta, right_of(eta), bed_x, fric))


def chunk_at(z, y, c, outer, inner, inner_z=STEP_Z):
    return jnp.where(
        c == 0,
        (z ^ STEP_Z[outer]) * 4 + (y ^ STEP_Y[inner]),
        (z ^ inner_z[inner]) * 4 + (y ^ STEP_Y[outer]),
    )


def step_of(steps, distance):
    found = jnp.int32(0)
    for k in range(1, 4):
        found = jnp.where(distance == steps[k], k, found)
    return found


def first_kernel(
    depth_in, xf_in, yf_in, wet_in, elev_in, rough_in, anc_in, keep, give, kept, given, terrain,
    depth, xf, yf, wet, elev, rough, anc, sems,
):
    pairs = zip(
        (elev_in, rough_in, depth_in, wet_in, xf_in, yf_in, anc_in), (elev, rough, depth, wet, xf, yf, anc)
    )
    copies = [pltpu.make_async_copy(src, dst, sems.at[n]) for n, (src, dst) in enumerate(pairs)]
    for copy in copies:
        copy.start()
    for copy in copies:
        copy.wait()
    _, _, c = place()
    top = c == 0
    bed = elev[...]
    fric = friction(rough[...])
    bed_x = jnp.maximum(bed, right_of(bed))
    bed_y = jnp.maximum(bed, below(bed))
    end = ROWS - 1
    last_row = lax.broadcasted_iota(jnp.int32, (ROWS, COLS), 0) == end
    terrain[0] = jnp.where(top, bed[:HALF], bed[HALF:])
    terrain[1] = jnp.where(top, fric[:HALF], fric[HALF:])
    terrain[2] = jnp.zeros((HALF, COLS), F32)
    terrain[2, 0:1, :] = jnp.where(top, bed[HALF : HALF + 1], bed[HALF - 1 : HALF])
    terrain[2, 1:2, :] = jnp.where(top, fric[HALF : HALF + 1], fric[HALF - 1 : HALF])
    lane = lax.broadcasted_iota(jnp.int32, (1, COLS), 1)
    at = 2 * lax.axis_index("dom")
    names = jnp.where(lane == at, anc[0].astype(F32), 0.0) + jnp.where(lane == at + 1, anc[1].astype(F32), 0.0)
    kept[6] = jnp.zeros((HALF, COLS), F32)
    given[6] = jnp.zeros((HALF, COLS), F32)
    kept[6, 4:5, :] = names
    given[6, 4:5, :] = names

    def edge(row, upper, lower):
        keep[row : row + 1, :] = jnp.where(top, upper, lower)
        give[row : row + 1, :] = jnp.where(top, lower, upper)

    zero = jnp.zeros((1, COLS), F32)
    edge(6, bed[:1], bed[end:])
    edge(7, fric[:1], fric[end:])
    for p in range(2):
        h0 = depth[p] * wet[p].astype(F32)
        qx, qy = xf[p], yf[p]
        edge(p, h0[:1], h0[end:])
        edge(4 + p, zero, qy[end:])
        eta = bed + h0
        qx = x_faces(qx, eta, bed_x, fric)
        qy = jnp.where(last_row, 0.0, flux(qy, eta, below(eta), bed_y, fric))
        h1 = h0 + RATIO * ((left_of(qx) - qx) + (above(qy) - qy))
        edge(2 + p, h1[:1], h1[end:])
        for f, v in enumerate((h1, qx, qy)):
            kept[3 * p + f] = jnp.where(top, v[:HALF], v[HALF:])
            given[3 * p + f] = jnp.where(top, v[HALF:], v[:HALF])
        kept[6, p : p + 1, :] = jnp.where(top, h1[HALF : HALF + 1], h1[HALF - 1 : HALF])
        given[6, p : p + 1, :] = jnp.where(top, h1[HALF - 1 : HALF], h1[HALF : HALF + 1])
        kept[6, 2 + p : 3 + p, :] = jnp.where(top, zero, qy[HALF - 1 : HALF])
        given[6, 2 + p : 3 + p, :] = jnp.where(top, qy[HALF - 1 : HALF], zero)


def second_kernel(own, far, terrain, mine, next_slab, o0, o1, o2, o3, rows, packed):
    z, y, c = place()
    top = c == 0
    slab = lax.axis_index("rows")
    bed, fric = terrain[0], terrain[1]
    bed_in, fric_in = terrain[2, 0:1, :], terrain[2, 1:2, :]
    row = lax.broadcasted_iota(jnp.int32, (HALF, COLS), 0)
    first, last = row == 0, row == HALF - 1
    at_edge = jnp.where(top, 0, HALF - 1)
    lower_edge = jnp.where(top, -1, HALF - 1)
    grid_end = jnp.where(slab == 7, lower_edge, -1)

    def rows_of(n, a, b):
        rows[n] = jnp.zeros((HALF, COLS), F32)
        rows[n, 0:2, :] = a
        rows[n, 2:4, :] = b
        return rows[n]

    in_h = rows_of(0, own[6, 0:2, :], far[6, 0:2, :])
    in_q = rows_of(1, own[6, 2:4, :], far[6, 2:4, :])
    out_h0 = rows_of(2, next_slab[8:10, :], next_slab[0:2, :])
    out_h1 = rows_of(3, next_slab[10:12, :], next_slab[2:4, :])
    out_q = rows_of(4, next_slab[12:14, :], next_slab[4:6, :])
    my_h = rows_of(5, mine[0:2, :], mine[8:10, :])
    my_q = rows_of(6, mine[4:6, :], mine[12:14, :])
    bed_out, fric_out = next_slab[6:7, :], next_slab[7:8, :]
    bed_mine = jnp.where(top, bed[:1], bed[HALF - 1 :])
    eta_mine, eta_out = bed_mine + my_h, bed_out + out_h0
    q1 = flux(
        jnp.where(top, out_q, my_q),
        jnp.where(top, eta_out, eta_mine),
        jnp.where(top, eta_mine, eta_out),
        jnp.maximum(bed_mine, bed_out),
        jnp.where(top, fric_out, fric[HALF - 1 :]),
    )
    q1 = jnp.where(jnp.where(top, slab, 7 - slab) == 0, 0.0, q1)
    out_h = out_h1 + jnp.where(top, -RATIO, RATIO) * q1
    bed_up, fric_up = jnp.where(top, bed_out, bed_in), jnp.where(top, fric_out, fric_in)
    bed_dn = jnp.where(top, bed_in, bed_out)
    eta_up = bed_up + jnp.where(top, out_h, in_h)
    eta_dn = bed_dn + jnp.where(top, in_h, out_h)
    q_up = jnp.where(top, q1, in_q)
    levels = []
    rows[7] = jnp.zeros((HALF, COLS), F32)
    for p in range(4):
        ref, n = (own, 3 * p) if p < 2 else (far, 3 * p - 6)
        q = q1[p : p + 1]
        h1 = ref[n] + jnp.where(row == at_edge, jnp.where(top, RATIO, -RATIO) * q, 0.0)
        qy1 = jnp.where(row == lower_edge, q, ref[n + 2])
        rows[7, p : p + 1, :] = bed[:1] + h1[:1]
        levels.append((h1, ref[n + 1], qy1))
    q2 = flux(q_up, eta_up, rows[7], jnp.maximum(bed_up, bed[:1]), fric_up)
    q2 = jnp.where(2 * slab + c == 0, 0.0, q2)
    bed_x = jnp.maximum(bed, right_of(bed))
    bed_y = jnp.maximum(bed, jnp.where(last, bed_dn, below(bed)))
    fields = []
    for p, (h1, qx, qy) in enumerate(levels):
        eta = bed + h1
        qx = x_faces(qx, eta, bed_x, fric)
        qy = flux(qy, eta, jnp.where(last, eta_dn[p : p + 1], below(eta)), bed_y, fric)
        qy = jnp.where(row == grid_end, 0.0, qy)
        over = jnp.where(first, q2[p : p + 1], above(qy))
        fields.append((h1 + RATIO * ((left_of(qx) - qx) + (over - qy)), qx, qy))
    low, even = masks()
    for f in range(3):
        for t in range(NT):
            a = [fields[p][f][:, 128 * t : 128 * t + 128] for p in range(4)]
            b0, b2 = jnp.where(low, a[0], pltpu.roll(a[2], 4, 0)), jnp.where(low, pltpu.roll(a[0], 4, 0), a[2])
            b1, b3 = jnp.where(low, a[1], pltpu.roll(a[3], 4, 0)), jnp.where(low, pltpu.roll(a[1], 4, 0), a[3])
            pair = [
                jnp.where(even, b0, pltpu.roll(b1, 2, 0)),
                jnp.where(even, pltpu.roll(b0, 6, 0), b1),
                jnp.where(even, b2, pltpu.roll(b3, 2, 0)),
                jnp.where(even, pltpu.roll(b2, 6, 0), b3),
            ]
            for d in range(4):
                n = AT[(d, f, t)]
                packed[n // PER, n % PER] = pair[d]
    names = own[6, 4:5, 0:128] + far[6, 4:5, 0:128]
    for k, out in enumerate((o0, o1, o2, o3)):
        for j in range(4):
            out[PER * j : PER * j + PER] = packed[chunk_at(z, y, c, k, j, LATE_Z)]
        out[4 * PER] = jnp.zeros((8, 128), F32)
        out[4 * PER, 0:1, :] = names


def masks():
    sub = lax.broadcasted_iota(jnp.int32, (8, 128), 0)
    return sub < 4, (sub & 2) == 0


def select_kernel(anc, m0, m1, m2, m3, t0, t1, t2, t3, o0, o1, o2, o3, held):
    z, y, c = place()
    for n, refs in enumerate(((m0, m1, m2, m3), (t0, t1, t2, t3))):
        for j, ref in enumerate(refs):
            held[n, 4 * PER * j : 4 * PER * j + 4 * PER] = ref[: 4 * PER]
    for k, out in enumerate((o0, o1, o2, o3)):
        for j in range(4):
            at = chunk_at(z, y, c, k, j)
            dest = ((at >> 2) << 3) | ((at & 3) << 1) | c
            for u in range(2):
                name = anc[2 * dest + u]
                dz, late_dz = (step_of(steps, (name >> 4) ^ z) for steps in (STEP_Z, LATE_Z))
                dy = step_of(STEP_Y, ((name >> 2) & 3) ^ y)
                for n in range(2):
                    core = c ^ n
                    base = jnp.where(core == 0, dy * 4 + dz, late_dz * 4 + dy) * PER
                    v = pl.multiple_of((((name >> 1) & 1) ^ core) * 4 + (name & 1) * 2, 2)
                    row = 4 * n + 2 * u
                    out[PER * j : PER * j + PER, row : row + 2, :] = held[n, pl.ds(base, PER), pl.ds(v, 2), :]


def last_kernel(f0, f1, f2, f3, ho, xo, yo, packed):
    z, y, c = place()
    low, even = masks()
    for j, ref in enumerate((f0, f1, f2, f3)):
        for k in range(4):
            packed[pl.ds(chunk_at(z, y, c, k, j) * PER, PER)] = ref[PER * k : PER * k + PER]
    for f, out in enumerate((ho, xo, yo)):
        for t in range(NT):
            cols = slice(128 * t, 128 * t + 128)
            pair = [packed[AT[(d, f, t)]] for d in range(4)]
            for n in range(2):
                rows = pl.ds(pl.multiple_of((c ^ n) * HALF, HALF), HALF)
                if n == 0:
                    b0 = jnp.where(low, pair[0], pltpu.roll(pair[2], 4, 0))
                    b1 = jnp.where(low, pair[1], pltpu.roll(pair[3], 4, 0))
                else:
                    b0 = jnp.where(low, pltpu.roll(pair[0], 4, 0), pair[2])
                    b1 = jnp.where(low, pltpu.roll(pair[1], 4, 0), pair[3])
                out[0, rows, cols] = jnp.where(even, b0, pltpu.roll(b1, 2, 0))
                out[1, rows, cols] = jnp.where(even, pltpu.roll(b0, 6, 0), b1)


def tiles(n):
    return jax.ShapeDtypeStruct((n, 8, 128), F32)


def params():
    return pltpu.CompilerParams(vmem_limit_bytes=32 * 1024 * 1024)


def outer_step(v, k):
    pairs = [(i, i ^ (STEP_Z[k] << 3 if i % 2 == 0 else STEP_Y[k] << 1)) for i in range(32)]
    return v if k == 0 else lax.ppermute(v, "dom", pairs)


def inner_step(v, k, inner_z=STEP_Z):
    pairs = [(i, i ^ (STEP_Y[k] << 1 if i % 2 == 0 else inner_z[k] << 3)) for i in range(32)]
    return v if k == 0 else lax.ppermute(v, "dom", pairs)


def other_core(v):
    return lax.ppermute(v, "dom", [(i, i ^ 1) for i in range(32)])


def next_slab(v):
    low = [((2 * chip + 1) * 8 + r, 2 * chip * 8 + (r + 1) % 8) for chip in range(16) for r in range(8)]
    return lax.ppermute(v, ("dom", "rows"), low + [(b, a) for a, b in low])


def regroup(parts, count):
    return [jnp.concatenate([p[count * j : count * j + count] for p in parts]) for j in range(4)]


def shards(depth, x_flow, y_flow, elevation, roughness, wet, ancestors):
    state = jax.ShapeDtypeStruct((2, ROWS, COLS), F32)
    strip = jax.ShapeDtypeStruct((HALF, COLS), F32)
    halves = jax.ShapeDtypeStruct((7, HALF, COLS), F32)
    ground = jax.ShapeDtypeStruct((3, HALF, COLS), F32)
    args = (depth, x_flow, y_flow, wet, elevation, roughness, ancestors)
    keep, give, kept, given, terrain = pl.pallas_call(
        first_kernel,
        out_shape=[strip, strip, halves, halves, ground],
        in_specs=[HBM] * 7,
        out_specs=[VMEM] * 5,
        scratch_shapes=[pltpu.VMEM(v.shape, v.dtype) for v in args[:6]]
        + [pltpu.SMEM((2,), jnp.int32), pltpu.SemaphoreType.DMA((7,))],
        compiler_params=params(),
    )(*[pltpu.with_memory_space_constraint(v, pltpu.HBM) for v in args])
    mine = jnp.concatenate([keep, other_core(give)])
    far = other_core(given)
    arrived = next_slab(mine)
    parts = pl.pallas_call(
        second_kernel,
        out_shape=[tiles(4 * PER + 1)] * 4,
        in_specs=[VMEM] * 5,
        out_specs=[VMEM] * 4,
        scratch_shapes=[pltpu.VMEM((8, HALF, COLS), F32), pltpu.VMEM((16, PER, 8, 128), F32)],
        compiler_params=params(),
    )(kept, far, terrain, mine, arrived)
    parts = [outer_step(v, k) for k, v in enumerate(parts)]
    names = (parts[0][4 * PER] + parts[1][4 * PER]) + (parts[2][4 * PER] + parts[3][4 * PER])
    parts = [jnp.concatenate([v, names[None]]) for v in regroup(parts, PER)]
    parts = [inner_step(v, k, LATE_Z) for k, v in enumerate(parts)]
    names = sum(v[4 * PER, 0, :64] for v in parts).astype(jnp.int32)
    others = [other_core(v) for v in parts]
    parts = pl.pallas_call(
        select_kernel,
        out_shape=[tiles(4 * PER)] * 4,
        in_specs=[SMEM] + [VMEM] * 8,
        out_specs=[VMEM] * 4,
        scratch_shapes=[pltpu.VMEM((2, 16 * PER, 8, 128), F32)],
        compiler_params=params(),
    )(names, *parts, *others)
    parts = [outer_step(v, k) for k, v in enumerate(parts)]
    parts = [inner_step(v, k) for k, v in enumerate(regroup(parts, PER))]
    return tuple(
        pl.pallas_call(
            last_kernel,
            out_shape=[state] * 3,
            in_specs=[VMEM] * 4,
            out_specs=[VMEM] * 3,
            scratch_shapes=[pltpu.VMEM((16 * PER, 8, 128), F32)],
            compiler_params=params(),
        )(*parts)
    )


def solution(mesh):
    wide = P("dom", "rows", None)
    in_specs = (wide, wide, wide, P("rows", None), P("rows", None), wide, P("dom"))
    return jax.shard_map(shards, mesh=mesh, in_specs=in_specs, out_specs=(wide, wide, wide), check_vma=False)
```

```python
import jax
import jax.numpy as jnp
from jax import lax
from jax.experimental import pallas as pl
from jax.experimental.pallas import tpu as pltpu
from jax.sharding import PartitionSpec as P

GDT = 9.81 * 1.0
SPACING = 10.0
RATIO = 1.0 / 10.0
MIN_DEPTH = 0.05
MANNING = (0.02, 0.025, 0.03, 0.035, 0.045, 0.06, 0.08, 0.1)
ROWS, COLS, HALF = 16, 1536, 8
NT = COLS // 128
F32 = jnp.float32

PER = 9
ITEMS = [(d, f, 3 * z + t) for z in range(4) for d in range(4) for f in range(3) for t in range(3)]
AT = {item: n for n, item in enumerate(ITEMS)}
STEP_Z = (0, 2, 3, 1)
STEP_Y = (0, 2, 1, 3)
LATE_Z = (0, 2, 1, 3)
EARLY_Y = (0, 1, 3, 2)
VMEM = pl.BlockSpec(memory_space=pltpu.VMEM)
SMEM = pl.BlockSpec(memory_space=pltpu.SMEM)
HBM = pl.BlockSpec(memory_space=pltpu.HBM)


def place():
    dom = lax.axis_index("dom")
    return dom >> 3, (dom >> 1) & 3, dom & 1


def flux(q, eta_a, eta_b, bed, fric):
    he = jnp.maximum(jnp.maximum(eta_a, eta_b) - bed, MIN_DEPTH)
    numer = q - (GDT / SPACING) * he * (eta_b - eta_a)
    denom = 1.0 + fric * jnp.abs(q) * jnp.exp2((-7.0 / 3.0) * jnp.log2(he))
    return numer / denom


def friction(rough):
    total = jnp.zeros(rough.shape, F32)
    for klass, n in enumerate(MANNING):
        total = jnp.where(rough == klass, F32(GDT * (n * n)), total)
    return total


def right_of(v):
    return pltpu.roll(v, COLS - 1, 1)


def left_of(v):
    return pltpu.roll(v, 1, 1)


def below(v):
    return pltpu.roll(v, v.shape[0] - 1, 0)


def above(v):
    return pltpu.roll(v, 1, 0)


def x_faces(q, eta, bed_x, fric):
    last = lax.broadcasted_iota(jnp.int32, q.shape, 1) == COLS - 1
    return jnp.where(last, 0.0, flux(q, eta, right_of(eta), bed_x, fric))


def role_of(core):
    return core ^ (lax.axis_index("rows") & 1) ^ 1


def chunk_at(z, y, role, outer, inner, inner_z=STEP_Z):
    return jnp.where(
        role == 0,
        (z ^ STEP_Z[outer]) * 4 + (y ^ STEP_Y[inner]),
        (z ^ inner_z[inner]) * 4 + (y ^ EARLY_Y[outer]),
    )


def step_of(steps, distance):
    found = jnp.int32(0)
    for k in range(1, 4):
        found = jnp.where(distance == steps[k], k, found)
    return found


def first_kernel(
    depth_in, xf_in, yf_in, wet_in, elev_in, rough_in, anc_in, keep, give, kept, given, terrain,
    depth, xf, yf, wet, elev, rough, anc, sems,
):
    pairs = zip(
        (elev_in, rough_in, depth_in, wet_in, xf_in, yf_in, anc_in), (elev, rough, depth, wet, xf, yf, anc)
    )
    copies = [pltpu.make_async_copy(src, dst, sems.at[n]) for n, (src, dst) in enumerate(pairs)]
    for copy in copies:
        copy.start()
    for copy in copies:
        copy.wait()
    _, _, c = place()
    top = c == 0
    bed = elev[...]
    fric = friction(rough[...])
    bed_x = jnp.maximum(bed, right_of(bed))
    bed_y = jnp.maximum(bed, below(bed))
    end = ROWS - 1
    last_row = lax.broadcasted_iota(jnp.int32, (ROWS, COLS), 0) == end
    terrain[0] = jnp.where(top, bed[:HALF], bed[HALF:])
    terrain[1] = jnp.where(top, fric[:HALF], fric[HALF:])
    terrain[2] = jnp.zeros((HALF, COLS), F32)
    terrain[2, 0:1, :] = jnp.where(top, bed[HALF : HALF + 1], bed[HALF - 1 : HALF])
    terrain[2, 1:2, :] = jnp.where(top, fric[HALF : HALF + 1], fric[HALF - 1 : HALF])
    lane = lax.broadcasted_iota(jnp.int32, (1, COLS), 1)
    at = 2 * lax.axis_index("dom")
    names = jnp.where(lane == at, anc[0].astype(F32), 0.0) + jnp.where(lane == at + 1, anc[1].astype(F32), 0.0)
    kept[6] = jnp.zeros((HALF, COLS), F32)
    given[6] = jnp.zeros((HALF, COLS), F32)
    kept[6, 4:5, :] = names
    given[6, 4:5, :] = names

    def edge(row, upper, lower):
        keep[row : row + 1, :] = jnp.where(top, upper, lower)
        give[row : row + 1, :] = jnp.where(top, lower, upper)

    zero = jnp.zeros((1, COLS), F32)
    edge(6, bed[:1], bed[end:])
    edge(7, fric[:1], fric[end:])
    for p in range(2):
        h0 = depth[p] * wet[p].astype(F32)
        qx, qy = xf[p], yf[p]
        edge(p, h0[:1], h0[end:])
        edge(4 + p, zero, qy[end:])
        eta = bed + h0
        qx = x_faces(qx, eta, bed_x, fric)
        qy = jnp.where(last_row, 0.0, flux(qy, eta, below(eta), bed_y, fric))
        h1 = h0 + RATIO * ((left_of(qx) - qx) + (above(qy) - qy))
        edge(2 + p, h1[:1], h1[end:])
        for f, v in enumerate((h1, qx, qy)):
            kept[3 * p + f] = jnp.where(top, v[:HALF], v[HALF:])
            given[3 * p + f] = jnp.where(top, v[HALF:], v[:HALF])
        kept[6, p : p + 1, :] = jnp.where(top, h1[HALF : HALF + 1], h1[HALF - 1 : HALF])
        given[6, p : p + 1, :] = jnp.where(top, h1[HALF - 1 : HALF], h1[HALF : HALF + 1])
        kept[6, 2 + p : 3 + p, :] = jnp.where(top, zero, qy[HALF - 1 : HALF])
        given[6, 2 + p : 3 + p, :] = jnp.where(top, qy[HALF - 1 : HALF], zero)


def second_kernel(own, far, terrain, mine, next_slab, o0, o1, o2, o3, rows, packed):
    z, y, c = place()
    top = c == 0
    slab = lax.axis_index("rows")
    bed, fric = terrain[0], terrain[1]
    bed_in, fric_in = terrain[2, 0:1, :], terrain[2, 1:2, :]
    row = lax.broadcasted_iota(jnp.int32, (HALF, COLS), 0)
    first, last = row == 0, row == HALF - 1
    at_edge = jnp.where(top, 0, HALF - 1)
    lower_edge = jnp.where(top, -1, HALF - 1)
    grid_end = jnp.where(slab == 7, lower_edge, -1)

    def rows_of(n, a, b):
        rows[n] = jnp.zeros((HALF, COLS), F32)
        rows[n, 0:2, :] = a
        rows[n, 2:4, :] = b
        return rows[n]

    in_h = rows_of(0, own[6, 0:2, :], far[6, 0:2, :])
    in_q = rows_of(1, own[6, 2:4, :], far[6, 2:4, :])
    out_h0 = rows_of(2, next_slab[8:10, :], next_slab[0:2, :])
    out_h1 = rows_of(3, next_slab[10:12, :], next_slab[2:4, :])
    out_q = rows_of(4, next_slab[12:14, :], next_slab[4:6, :])
    my_h = rows_of(5, mine[0:2, :], mine[8:10, :])
    my_q = rows_of(6, mine[4:6, :], mine[12:14, :])
    bed_out, fric_out = next_slab[6:7, :], next_slab[7:8, :]
    bed_mine = jnp.where(top, bed[:1], bed[HALF - 1 :])
    eta_mine, eta_out = bed_mine + my_h, bed_out + out_h0
    q1 = flux(
        jnp.where(top, out_q, my_q),
        jnp.where(top, eta_out, eta_mine),
        jnp.where(top, eta_mine, eta_out),
        jnp.maximum(bed_mine, bed_out),
        jnp.where(top, fric_out, fric[HALF - 1 :]),
    )
    q1 = jnp.where(jnp.where(top, slab, 7 - slab) == 0, 0.0, q1)
    out_h = out_h1 + jnp.where(top, -RATIO, RATIO) * q1
    bed_up, fric_up = jnp.where(top, bed_out, bed_in), jnp.where(top, fric_out, fric_in)
    bed_dn = jnp.where(top, bed_in, bed_out)
    eta_up = bed_up + jnp.where(top, out_h, in_h)
    eta_dn = bed_dn + jnp.where(top, in_h, out_h)
    q_up = jnp.where(top, q1, in_q)
    levels = []
    rows[7] = jnp.zeros((HALF, COLS), F32)
    for p in range(4):
        ref, n = (own, 3 * p) if p < 2 else (far, 3 * p - 6)
        q = q1[p : p + 1]
        h1 = ref[n] + jnp.where(row == at_edge, jnp.where(top, RATIO, -RATIO) * q, 0.0)
        qy1 = jnp.where(row == lower_edge, q, ref[n + 2])
        rows[7, p : p + 1, :] = bed[:1] + h1[:1]
        levels.append((h1, ref[n + 1], qy1))
    q2 = flux(q_up, eta_up, rows[7], jnp.maximum(bed_up, bed[:1]), fric_up)
    q2 = jnp.where(2 * slab + c == 0, 0.0, q2)
    bed_x = jnp.maximum(bed, right_of(bed))
    bed_y = jnp.maximum(bed, jnp.where(last, bed_dn, below(bed)))
    fields = []
    for p, (h1, qx, qy) in enumerate(levels):
        eta = bed + h1
        qx = x_faces(qx, eta, bed_x, fric)
        qy = flux(qy, eta, jnp.where(last, eta_dn[p : p + 1], below(eta)), bed_y, fric)
        qy = jnp.where(row == grid_end, 0.0, qy)
        over = jnp.where(first, q2[p : p + 1], above(qy))
        fields.append((h1 + RATIO * ((left_of(qx) - qx) + (over - qy)), qx, qy))
    low, even = masks()
    for f in range(3):
        for t in range(NT):
            a = [fields[p][f][:, 128 * t : 128 * t + 128] for p in range(4)]
            b0, b2 = jnp.where(low, a[0], pltpu.roll(a[2], 4, 0)), jnp.where(low, pltpu.roll(a[0], 4, 0), a[2])
            b1, b3 = jnp.where(low, a[1], pltpu.roll(a[3], 4, 0)), jnp.where(low, pltpu.roll(a[1], 4, 0), a[3])
            pair = [
                jnp.where(even, b0, pltpu.roll(b1, 2, 0)),
                jnp.where(even, pltpu.roll(b0, 6, 0), b1),
                jnp.where(even, b2, pltpu.roll(b3, 2, 0)),
                jnp.where(even, pltpu.roll(b2, 6, 0), b3),
            ]
            for d in range(4):
                n = AT[(d, f, t)]
                packed[n // PER, n % PER] = pair[d]
    names = own[6, 4:5, 0:128] + far[6, 4:5, 0:128]
    for k, out in enumerate((o0, o1, o2, o3)):
        for j in range(4):
            out[PER * j : PER * j + PER] = packed[chunk_at(z, y, role_of(c), k, j, LATE_Z)]
        out[4 * PER] = jnp.zeros((8, 128), F32)
        out[4 * PER, 0:1, :] = names


def masks():
    sub = lax.broadcasted_iota(jnp.int32, (8, 128), 0)
    return sub < 4, (sub & 2) == 0


def select_kernel(anc, m0, m1, m2, m3, t0, t1, t2, t3, o0, o1, o2, o3, held):
    z, y, c = place()
    for n, refs in enumerate(((m0, m1, m2, m3), (t0, t1, t2, t3))):
        for j, ref in enumerate(refs):
            held[n, 4 * PER * j : 4 * PER * j + 4 * PER] = ref[: 4 * PER]
    for k, out in enumerate((o0, o1, o2, o3)):
        for j in range(4):
            at = chunk_at(z, y, role_of(c), k, j)
            dest = ((at >> 2) << 3) | ((at & 3) << 1) | c
            for u in range(2):
                name = anc[2 * dest + u]
                dz, late_dz = (step_of(steps, (name >> 4) ^ z) for steps in (STEP_Z, LATE_Z))
                dy, early_dy = (step_of(steps, ((name >> 2) & 3) ^ y) for steps in (STEP_Y, EARLY_Y))
                for n in range(2):
                    core = c ^ n
                    base = jnp.where(role_of(core) == 0, dy * 4 + dz, late_dz * 4 + early_dy) * PER
                    v = pl.multiple_of((((name >> 1) & 1) ^ core) * 4 + (name & 1) * 2, 2)
                    row = 4 * n + 2 * u
                    out[PER * j : PER * j + PER, row : row + 2, :] = held[n, pl.ds(base, PER), pl.ds(v, 2), :]


def last_kernel(f0, f1, f2, f3, ho, xo, yo, packed):
    z, y, c = place()
    low, even = masks()
    for j, ref in enumerate((f0, f1, f2, f3)):
        for k in range(4):
            packed[pl.ds(chunk_at(z, y, role_of(c), k, j) * PER, PER)] = ref[PER * k : PER * k + PER]
    for f, out in enumerate((ho, xo, yo)):
        for t in range(NT):
            cols = slice(128 * t, 128 * t + 128)
            pair = [packed[AT[(d, f, t)]] for d in range(4)]
            for n in range(2):
                rows = pl.ds(pl.multiple_of((c ^ n) * HALF, HALF), HALF)
                if n == 0:
                    b0 = jnp.where(low, pair[0], pltpu.roll(pair[2], 4, 0))
                    b1 = jnp.where(low, pair[1], pltpu.roll(pair[3], 4, 0))
                else:
                    b0 = jnp.where(low, pltpu.roll(pair[0], 4, 0), pair[2])
                    b1 = jnp.where(low, pltpu.roll(pair[1], 4, 0), pair[3])
                out[0, rows, cols] = jnp.where(even, b0, pltpu.roll(b1, 2, 0))
                out[1, rows, cols] = jnp.where(even, pltpu.roll(b0, 6, 0), b1)


def tiles(n):
    return jax.ShapeDtypeStruct((n, 8, 128), F32)


def params():
    return pltpu.CompilerParams(vmem_limit_bytes=32 * 1024 * 1024)


def swap(v, by_role):
    pairs = [(8 * d + r, 8 * (d ^ by_role[(d ^ r ^ 1) & 1]) + r) for d in range(32) for r in range(8)]
    return lax.ppermute(v, ("dom", "rows"), pairs)


def outer_step(v, k):
    return v if k == 0 else swap(v, (STEP_Z[k] << 3, EARLY_Y[k] << 1))


def inner_step(v, k, inner_z=STEP_Z):
    return v if k == 0 else swap(v, (STEP_Y[k] << 1, inner_z[k] << 3))


def other_core(v):
    return lax.ppermute(v, "dom", [(i, i ^ 1) for i in range(32)])


def next_slab(v):
    low = [((2 * chip + 1) * 8 + r, 2 * chip * 8 + (r + 1) % 8) for chip in range(16) for r in range(8)]
    return lax.ppermute(v, ("dom", "rows"), low + [(b, a) for a, b in low])


def regroup(parts, count):
    return [jnp.concatenate([p[count * j : count * j + count] for p in parts]) for j in range(4)]


def shards(depth, x_flow, y_flow, elevation, roughness, wet, ancestors):
    state = jax.ShapeDtypeStruct((2, ROWS, COLS), F32)
    strip = jax.ShapeDtypeStruct((HALF, COLS), F32)
    halves = jax.ShapeDtypeStruct((7, HALF, COLS), F32)
    ground = jax.ShapeDtypeStruct((3, HALF, COLS), F32)
    args = (depth, x_flow, y_flow, wet, elevation, roughness, ancestors)
    keep, give, kept, given, terrain = pl.pallas_call(
        first_kernel,
        out_shape=[strip, strip, halves, halves, ground],
        in_specs=[HBM] * 7,
        out_specs=[VMEM] * 5,
        scratch_shapes=[pltpu.VMEM(v.shape, v.dtype) for v in args[:6]]
        + [pltpu.SMEM((2,), jnp.int32), pltpu.SemaphoreType.DMA((7,))],
        compiler_params=params(),
    )(*[pltpu.with_memory_space_constraint(v, pltpu.HBM) for v in args])
    mine = jnp.concatenate([keep, other_core(give)])
    far = other_core(given)
    arrived = next_slab(mine)
    parts = pl.pallas_call(
        second_kernel,
        out_shape=[tiles(4 * PER + 1)] * 4,
        in_specs=[VMEM] * 5,
        out_specs=[VMEM] * 4,
        scratch_shapes=[pltpu.VMEM((8, HALF, COLS), F32), pltpu.VMEM((16, PER, 8, 128), F32)],
        compiler_params=params(),
    )(kept, far, terrain, mine, arrived)
    parts = [outer_step(v, k) for k, v in enumerate(parts)]
    names = (parts[0][4 * PER] + parts[1][4 * PER]) + (parts[2][4 * PER] + parts[3][4 * PER])
    parts = [jnp.concatenate([v, names[None]]) for v in regroup(parts, PER)]
    parts = [inner_step(v, k, LATE_Z) for k, v in enumerate(parts)]
    names = sum(v[4 * PER, 0, :64] for v in parts).astype(jnp.int32)
    others = [other_core(v) for v in parts]
    parts = pl.pallas_call(
        select_kernel,
        out_shape=[tiles(4 * PER)] * 4,
        in_specs=[SMEM] + [VMEM] * 8,
        out_specs=[VMEM] * 4,
        scratch_shapes=[pltpu.VMEM((2, 16 * PER, 8, 128), F32)],
        compiler_params=params(),
    )(names, *parts, *others)
    parts = [outer_step(v, k) for k, v in enumerate(parts)]
    parts = [inner_step(v, k) for k, v in enumerate(regroup(parts, PER))]
    return tuple(
        pl.pallas_call(
            last_kernel,
            out_shape=[state] * 3,
            in_specs=[VMEM] * 4,
            out_specs=[VMEM] * 3,
            scratch_shapes=[pltpu.VMEM((16 * PER, 8, 128), F32)],
            compiler_params=params(),
        )(*parts)
    )


def solution(mesh):
    wide = P("dom", "rows", None)
    in_specs = (wide, wide, wide, P("rows", None), P("rows", None), wide, P("dom"))
    return jax.shard_map(shards, mesh=mesh, in_specs=in_specs, out_specs=(wide, wide, wide), check_vma=False)
```

```python
import jax
import jax.numpy as jnp
from jax import lax
from jax.experimental import pallas as pl
from jax.experimental.pallas import tpu as pltpu
from jax.sharding import PartitionSpec as P

GDT = 9.81 * 1.0
SPACING = 10.0
RATIO = 1.0 / 10.0
MIN_DEPTH = 0.05
MANNING = (0.02, 0.025, 0.03, 0.035, 0.045, 0.06, 0.08, 0.1)
ROWS, COLS, HALF = 16, 1536, 8
NT = COLS // 128
F32 = jnp.float32

PER = 9
ITEMS = [(d, f, 3 * z + t) for z in range(4) for d in range(4) for f in range(3) for t in range(3)]
AT = {item: n for n, item in enumerate(ITEMS)}
STEP_Z = (0, 2, 3, 1)
STEP_Y = (0, 2, 1, 3)
LATE_Z = (0, 2, 1, 3)
EARLY_Y = (0, 2, 1, 3)
VMEM = pl.BlockSpec(memory_space=pltpu.VMEM)
SMEM = pl.BlockSpec(memory_space=pltpu.SMEM)
HBM = pl.BlockSpec(memory_space=pltpu.HBM)


def place():
    dom = lax.axis_index("dom")
    return dom >> 3, (dom >> 1) & 3, dom & 1


def flux(q, eta_a, eta_b, bed, fric):
    he = jnp.maximum(jnp.maximum(eta_a, eta_b) - bed, MIN_DEPTH)
    numer = q - (GDT / SPACING) * he * (eta_b - eta_a)
    denom = 1.0 + fric * jnp.abs(q) * jnp.exp2((-7.0 / 3.0) * jnp.log2(he))
    return numer / denom


def friction(rough):
    total = jnp.zeros(rough.shape, F32)
    for klass, n in enumerate(MANNING):
        total = jnp.where(rough == klass, F32(GDT * (n * n)), total)
    return total


def right_of(v):
    return pltpu.roll(v, COLS - 1, 1)


def left_of(v):
    return pltpu.roll(v, 1, 1)


def below(v):
    return pltpu.roll(v, v.shape[0] - 1, 0)


def above(v):
    return pltpu.roll(v, 1, 0)


def x_faces(q, eta, bed_x, fric):
    last = lax.broadcasted_iota(jnp.int32, q.shape, 1) == COLS - 1
    return jnp.where(last, 0.0, flux(q, eta, right_of(eta), bed_x, fric))


def role_of(core):
    return core ^ (lax.axis_index("rows") & 1) ^ 1


def chunk_at(z, y, role, outer, inner, inner_z=STEP_Z):
    return jnp.where(
        role == 0,
        (z ^ STEP_Z[outer]) * 4 + (y ^ STEP_Y[inner]),
        (z ^ inner_z[inner]) * 4 + (y ^ EARLY_Y[outer]),
    )


def step_of(steps, distance):
    found = jnp.int32(0)
    for k in range(1, 4):
        found = jnp.where(distance == steps[k], k, found)
    return found


def first_kernel(
    depth_in, xf_in, yf_in, wet_in, elev_in, rough_in, anc_in, keep, give, kept, given, terrain,
    depth, xf, yf, wet, elev, rough, anc, sems,
):
    pairs = zip(
        (elev_in, rough_in, depth_in, wet_in, xf_in, yf_in, anc_in), (elev, rough, depth, wet, xf, yf, anc)
    )
    copies = [pltpu.make_async_copy(src, dst, sems.at[n]) for n, (src, dst) in enumerate(pairs)]
    for copy in copies:
        copy.start()
    for copy in copies:
        copy.wait()
    _, _, c = place()
    top = c == 0
    bed = elev[...]
    fric = friction(rough[...])
    bed_x = jnp.maximum(bed, right_of(bed))
    bed_y = jnp.maximum(bed, below(bed))
    end = ROWS - 1
    last_row = lax.broadcasted_iota(jnp.int32, (ROWS, COLS), 0) == end
    terrain[0] = jnp.where(top, bed[:HALF], bed[HALF:])
    terrain[1] = jnp.where(top, fric[:HALF], fric[HALF:])
    terrain[2] = jnp.zeros((HALF, COLS), F32)
    terrain[2, 0:1, :] = jnp.where(top, bed[HALF : HALF + 1], bed[HALF - 1 : HALF])
    terrain[2, 1:2, :] = jnp.where(top, fric[HALF : HALF + 1], fric[HALF - 1 : HALF])
    lane = lax.broadcasted_iota(jnp.int32, (1, COLS), 1)
    at = 2 * lax.axis_index("dom")
    names = jnp.where(lane == at, anc[0].astype(F32), 0.0) + jnp.where(lane == at + 1, anc[1].astype(F32), 0.0)
    kept[6] = jnp.zeros((HALF, COLS), F32)
    given[6] = jnp.zeros((HALF, COLS), F32)
    kept[6, 4:5, :] = names
    given[6, 4:5, :] = names

    def edge(row, upper, lower):
        keep[row : row + 1, :] = jnp.where(top, upper, lower)
        give[row : row + 1, :] = jnp.where(top, lower, upper)

    zero = jnp.zeros((1, COLS), F32)
    edge(6, bed[:1], bed[end:])
    edge(7, fric[:1], fric[end:])
    for p in range(2):
        h0 = depth[p] * wet[p].astype(F32)
        qx, qy = xf[p], yf[p]
        edge(p, h0[:1], h0[end:])
        edge(4 + p, zero, qy[end:])
        eta = bed + h0
        qx = x_faces(qx, eta, bed_x, fric)
        qy = jnp.where(last_row, 0.0, flux(qy, eta, below(eta), bed_y, fric))
        h1 = h0 + RATIO * ((left_of(qx) - qx) + (above(qy) - qy))
        edge(2 + p, h1[:1], h1[end:])
        for f, v in enumerate((h1, qx, qy)):
            kept[3 * p + f] = jnp.where(top, v[:HALF], v[HALF:])
            given[3 * p + f] = jnp.where(top, v[HALF:], v[:HALF])
        kept[6, p : p + 1, :] = jnp.where(top, h1[HALF : HALF + 1], h1[HALF - 1 : HALF])
        given[6, p : p + 1, :] = jnp.where(top, h1[HALF - 1 : HALF], h1[HALF : HALF + 1])
        kept[6, 2 + p : 3 + p, :] = jnp.where(top, zero, qy[HALF - 1 : HALF])
        given[6, 2 + p : 3 + p, :] = jnp.where(top, qy[HALF - 1 : HALF], zero)


def second_kernel(own, far, terrain, mine, next_slab, o0, o1, o2, o3, rows, packed):
    z, y, c = place()
    top = c == 0
    slab = lax.axis_index("rows")
    bed, fric = terrain[0], terrain[1]
    bed_in, fric_in = terrain[2, 0:1, :], terrain[2, 1:2, :]
    row = lax.broadcasted_iota(jnp.int32, (HALF, COLS), 0)
    first, last = row == 0, row == HALF - 1
    at_edge = jnp.where(top, 0, HALF - 1)
    lower_edge = jnp.where(top, -1, HALF - 1)
    grid_end = jnp.where(slab == 7, lower_edge, -1)

    def rows_of(n, a, b):
        rows[n] = jnp.zeros((HALF, COLS), F32)
        rows[n, 0:2, :] = a
        rows[n, 2:4, :] = b
        return rows[n]

    in_h = rows_of(0, own[6, 0:2, :], far[6, 0:2, :])
    in_q = rows_of(1, own[6, 2:4, :], far[6, 2:4, :])
    out_h0 = rows_of(2, next_slab[8:10, :], next_slab[0:2, :])
    out_h1 = rows_of(3, next_slab[10:12, :], next_slab[2:4, :])
    out_q = rows_of(4, next_slab[12:14, :], next_slab[4:6, :])
    my_h = rows_of(5, mine[0:2, :], mine[8:10, :])
    my_q = rows_of(6, mine[4:6, :], mine[12:14, :])
    bed_out, fric_out = next_slab[6:7, :], next_slab[7:8, :]
    bed_mine = jnp.where(top, bed[:1], bed[HALF - 1 :])
    eta_mine, eta_out = bed_mine + my_h, bed_out + out_h0
    q1 = flux(
        jnp.where(top, out_q, my_q),
        jnp.where(top, eta_out, eta_mine),
        jnp.where(top, eta_mine, eta_out),
        jnp.maximum(bed_mine, bed_out),
        jnp.where(top, fric_out, fric[HALF - 1 :]),
    )
    q1 = jnp.where(jnp.where(top, slab, 7 - slab) == 0, 0.0, q1)
    out_h = out_h1 + jnp.where(top, -RATIO, RATIO) * q1
    bed_up, fric_up = jnp.where(top, bed_out, bed_in), jnp.where(top, fric_out, fric_in)
    bed_dn = jnp.where(top, bed_in, bed_out)
    eta_up = bed_up + jnp.where(top, out_h, in_h)
    eta_dn = bed_dn + jnp.where(top, in_h, out_h)
    q_up = jnp.where(top, q1, in_q)
    levels = []
    rows[7] = jnp.zeros((HALF, COLS), F32)
    for p in range(4):
        ref, n = (own, 3 * p) if p < 2 else (far, 3 * p - 6)
        q = q1[p : p + 1]
        h1 = ref[n] + jnp.where(row == at_edge, jnp.where(top, RATIO, -RATIO) * q, 0.0)
        qy1 = jnp.where(row == lower_edge, q, ref[n + 2])
        rows[7, p : p + 1, :] = bed[:1] + h1[:1]
        levels.append((h1, ref[n + 1], qy1))
    q2 = flux(q_up, eta_up, rows[7], jnp.maximum(bed_up, bed[:1]), fric_up)
    q2 = jnp.where(2 * slab + c == 0, 0.0, q2)
    bed_x = jnp.maximum(bed, right_of(bed))
    bed_y = jnp.maximum(bed, jnp.where(last, bed_dn, below(bed)))
    fields = []
    for p, (h1, qx, qy) in enumerate(levels):
        eta = bed + h1
        qx = x_faces(qx, eta, bed_x, fric)
        qy = flux(qy, eta, jnp.where(last, eta_dn[p : p + 1], below(eta)), bed_y, fric)
        qy = jnp.where(row == grid_end, 0.0, qy)
        over = jnp.where(first, q2[p : p + 1], above(qy))
        fields.append((h1 + RATIO * ((left_of(qx) - qx) + (over - qy)), qx, qy))
    low, even = masks()
    for f in range(3):
        for t in range(NT):
            a = [fields[p][f][:, 128 * t : 128 * t + 128] for p in range(4)]
            b0, b2 = jnp.where(low, a[0], pltpu.roll(a[2], 4, 0)), jnp.where(low, pltpu.roll(a[0], 4, 0), a[2])
            b1, b3 = jnp.where(low, a[1], pltpu.roll(a[3], 4, 0)), jnp.where(low, pltpu.roll(a[1], 4, 0), a[3])
            pair = [
                jnp.where(even, b0, pltpu.roll(b1, 2, 0)),
                jnp.where(even, pltpu.roll(b0, 6, 0), b1),
                jnp.where(even, b2, pltpu.roll(b3, 2, 0)),
                jnp.where(even, pltpu.roll(b2, 6, 0), b3),
            ]
            for d in range(4):
                n = AT[(d, f, t)]
                packed[n // PER, n % PER] = pair[d]
    names = own[6, 4:5, 0:128] + far[6, 4:5, 0:128]
    for k, out in enumerate((o0, o1, o2, o3)):
        for j in range(4):
            out[PER * j : PER * j + PER] = packed[chunk_at(z, y, role_of(c), k, j, LATE_Z)]
        out[4 * PER] = jnp.zeros((8, 128), F32)
        out[4 * PER, 0:1, :] = names


def masks():
    sub = lax.broadcasted_iota(jnp.int32, (8, 128), 0)
    return sub < 4, (sub & 2) == 0


def select_kernel(anc, m0, m1, m2, m3, t0, t1, t2, t3, o0, o1, o2, o3, held):
    z, y, c = place()
    for n, refs in enumerate(((m0, m1, m2, m3), (t0, t1, t2, t3))):
        for j, ref in enumerate(refs):
            held[n, 4 * PER * j : 4 * PER * j + 4 * PER] = ref[: 4 * PER]
    for k, out in enumerate((o0, o1, o2, o3)):
        for j in range(4):
            at = chunk_at(z, y, role_of(c), k, j)
            dest = ((at >> 2) << 3) | ((at & 3) << 1) | c
            for u in range(2):
                name = anc[2 * dest + u]
                dz, late_dz = (step_of(steps, (name >> 4) ^ z) for steps in (STEP_Z, LATE_Z))
                dy, early_dy = (step_of(steps, ((name >> 2) & 3) ^ y) for steps in (STEP_Y, EARLY_Y))
                for n in range(2):
                    core = c ^ n
                    base = jnp.where(role_of(core) == 0, dy * 4 + dz, late_dz * 4 + early_dy) * PER
                    v = pl.multiple_of((((name >> 1) & 1) ^ core) * 4 + (name & 1) * 2, 2)
                    row = 4 * n + 2 * u
                    out[PER * j : PER * j + PER, row : row + 2, :] = held[n, pl.ds(base, PER), pl.ds(v, 2), :]


def last_kernel(f0, f1, f2, f3, ho, xo, yo, packed):
    z, y, c = place()
    low, even = masks()
    for j, ref in enumerate((f0, f1, f2, f3)):
        for k in range(4):
            packed[pl.ds(chunk_at(z, y, role_of(c), k, j) * PER, PER)] = ref[PER * k : PER * k + PER]
    for f, out in enumerate((ho, xo, yo)):
        for t in range(NT):
            cols = slice(128 * t, 128 * t + 128)
            pair = [packed[AT[(d, f, t)]] for d in range(4)]
            for n in range(2):
                rows = pl.ds(pl.multiple_of((c ^ n) * HALF, HALF), HALF)
                if n == 0:
                    b0 = jnp.where(low, pair[0], pltpu.roll(pair[2], 4, 0))
                    b1 = jnp.where(low, pair[1], pltpu.roll(pair[3], 4, 0))
                else:
                    b0 = jnp.where(low, pltpu.roll(pair[0], 4, 0), pair[2])
                    b1 = jnp.where(low, pltpu.roll(pair[1], 4, 0), pair[3])
                out[0, rows, cols] = jnp.where(even, b0, pltpu.roll(b1, 2, 0))
                out[1, rows, cols] = jnp.where(even, pltpu.roll(b0, 6, 0), b1)


def tiles(n):
    return jax.ShapeDtypeStruct((n, 8, 128), F32)


def params():
    return pltpu.CompilerParams(vmem_limit_bytes=32 * 1024 * 1024)


def swap(v, by_role):
    pairs = [(8 * d + r, 8 * (d ^ by_role[(d ^ r ^ 1) & 1]) + r) for d in range(32) for r in range(8)]
    return lax.ppermute(v, ("dom", "rows"), pairs)


def outer_step(v, k):
    return v if k == 0 else swap(v, (STEP_Z[k] << 3, EARLY_Y[k] << 1))


def inner_step(v, k, inner_z=STEP_Z):
    return v if k == 0 else swap(v, (STEP_Y[k] << 1, inner_z[k] << 3))


def other_core(v):
    return lax.ppermute(v, "dom", [(i, i ^ 1) for i in range(32)])


def next_slab(v):
    low = [((2 * chip + 1) * 8 + r, 2 * chip * 8 + (r + 1) % 8) for chip in range(16) for r in range(8)]
    return lax.ppermute(v, ("dom", "rows"), low + [(b, a) for a, b in low])


def regroup(parts, count):
    return [jnp.concatenate([p[count * j : count * j + count] for p in parts]) for j in range(4)]


def shards(depth, x_flow, y_flow, elevation, roughness, wet, ancestors):
    state = jax.ShapeDtypeStruct((2, ROWS, COLS), F32)
    strip = jax.ShapeDtypeStruct((HALF, COLS), F32)
    halves = jax.ShapeDtypeStruct((7, HALF, COLS), F32)
    ground = jax.ShapeDtypeStruct((3, HALF, COLS), F32)
    args = (depth, x_flow, y_flow, wet, elevation, roughness, ancestors)
    keep, give, kept, given, terrain = pl.pallas_call(
        first_kernel,
        out_shape=[strip, strip, halves, halves, ground],
        in_specs=[HBM] * 7,
        out_specs=[VMEM] * 5,
        scratch_shapes=[pltpu.VMEM(v.shape, v.dtype) for v in args[:6]]
        + [pltpu.SMEM((2,), jnp.int32), pltpu.SemaphoreType.DMA((7,))],
        compiler_params=params(),
    )(*[pltpu.with_memory_space_constraint(v, pltpu.HBM) for v in args])
    mine = jnp.concatenate([keep, other_core(give)])
    far = other_core(given)
    arrived = next_slab(mine)
    parts = pl.pallas_call(
        second_kernel,
        out_shape=[tiles(4 * PER + 1)] * 4,
        in_specs=[VMEM] * 5,
        out_specs=[VMEM] * 4,
        scratch_shapes=[pltpu.VMEM((8, HALF, COLS), F32), pltpu.VMEM((16, PER, 8, 128), F32)],
        compiler_params=params(),
    )(kept, far, terrain, mine, arrived)
    parts = [outer_step(v, k) for k, v in enumerate(parts)]
    names = (parts[0][4 * PER] + parts[1][4 * PER]) + (parts[2][4 * PER] + parts[3][4 * PER])
    parts = [jnp.concatenate([v, names[None]]) for v in regroup(parts, PER)]
    parts = [inner_step(v, k, LATE_Z) for k, v in enumerate(parts)]
    names = sum(v[4 * PER, 0, :64] for v in parts).astype(jnp.int32)
    others = [other_core(v) for v in parts]
    parts = pl.pallas_call(
        select_kernel,
        out_shape=[tiles(4 * PER)] * 4,
        in_specs=[SMEM] + [VMEM] * 8,
        out_specs=[VMEM] * 4,
        scratch_shapes=[pltpu.VMEM((2, 16 * PER, 8, 128), F32)],
        compiler_params=params(),
    )(names, *parts, *others)
    parts = [outer_step(v, k) for k, v in enumerate(parts)]
    parts = [inner_step(v, k) for k, v in enumerate(regroup(parts, PER))]
    return tuple(
        pl.pallas_call(
            last_kernel,
            out_shape=[state] * 3,
            in_specs=[VMEM] * 4,
            out_specs=[VMEM] * 3,
            scratch_shapes=[pltpu.VMEM((16 * PER, 8, 128), F32)],
            compiler_params=params(),
        )(*parts)
    )


def solution(mesh):
    wide = P("dom", "rows", None)
    in_specs = (wide, wide, wide, P("rows", None), P("rows", None), wide, P("dom"))
    return jax.shard_map(shards, mesh=mesh, in_specs=in_specs, out_specs=(wide, wide, wide), check_vma=False)
```

```python
import jax
import jax.numpy as jnp
from jax import lax
from jax.experimental import pallas as pl
from jax.experimental.pallas import tpu as pltpu
from jax.sharding import PartitionSpec as P

GDT = 9.81 * 1.0
SPACING = 10.0
RATIO = 1.0 / 10.0
MIN_DEPTH = 0.05
MANNING = (0.02, 0.025, 0.03, 0.035, 0.045, 0.06, 0.08, 0.1)
ROWS, COLS, HALF = 16, 1536, 8
NT = COLS // 128
F32 = jnp.float32

PER = 9
ITEMS = [(d, f, 3 * z + t) for z in range(4) for d in range(4) for f in range(3) for t in range(3)]
AT = {item: n for n, item in enumerate(ITEMS)}
STEP_Z = (0, 3, 2, 1)
STEP_Y = (0, 2, 1, 3)
LATE_Z = (0, 3, 1, 2)
EARLY_Y = (0, 2, 1, 3)
VMEM = pl.BlockSpec(memory_space=pltpu.VMEM)
SMEM = pl.BlockSpec(memory_space=pltpu.SMEM)
HBM = pl.BlockSpec(memory_space=pltpu.HBM)


def place():
    dom = lax.axis_index("dom")
    return dom >> 3, (dom >> 1) & 3, dom & 1


def flux(q, eta_a, eta_b, bed, fric):
    he = jnp.maximum(jnp.maximum(eta_a, eta_b) - bed, MIN_DEPTH)
    numer = q - (GDT / SPACING) * he * (eta_b - eta_a)
    denom = 1.0 + fric * jnp.abs(q) * jnp.exp2((-7.0 / 3.0) * jnp.log2(he))
    return numer / denom


def friction(rough):
    total = jnp.zeros(rough.shape, F32)
    for klass, n in enumerate(MANNING):
        total = jnp.where(rough == klass, F32(GDT * (n * n)), total)
    return total


def right_of(v):
    return pltpu.roll(v, COLS - 1, 1)


def left_of(v):
    return pltpu.roll(v, 1, 1)


def below(v):
    return pltpu.roll(v, v.shape[0] - 1, 0)


def above(v):
    return pltpu.roll(v, 1, 0)


def x_faces(q, eta, bed_x, fric):
    last = lax.broadcasted_iota(jnp.int32, q.shape, 1) == COLS - 1
    return jnp.where(last, 0.0, flux(q, eta, right_of(eta), bed_x, fric))


def role_of(core):
    return core ^ (lax.axis_index("rows") & 1) ^ 1


def chunk_at(z, y, role, outer, inner, inner_z=STEP_Z):
    return jnp.where(
        role == 0,
        (z ^ STEP_Z[outer]) * 4 + (y ^ STEP_Y[inner]),
        (z ^ inner_z[inner]) * 4 + (y ^ EARLY_Y[outer]),
    )


def step_of(steps, distance):
    found = jnp.int32(0)
    for k in range(1, 4):
        found = jnp.where(distance == steps[k], k, found)
    return found


def first_kernel(
    depth_in, xf_in, yf_in, wet_in, elev_in, rough_in, anc_in, keep, give, kept, given, terrain,
    depth, xf, yf, wet, elev, rough, anc, sems,
):
    pairs = zip(
        (elev_in, rough_in, depth_in, wet_in, xf_in, yf_in, anc_in), (elev, rough, depth, wet, xf, yf, anc)
    )
    copies = [pltpu.make_async_copy(src, dst, sems.at[n]) for n, (src, dst) in enumerate(pairs)]
    for copy in copies:
        copy.start()
    for copy in copies:
        copy.wait()
    _, _, c = place()
    top = c == 0
    bed = elev[...]
    fric = friction(rough[...])
    bed_x = jnp.maximum(bed, right_of(bed))
    bed_y = jnp.maximum(bed, below(bed))
    end = ROWS - 1
    last_row = lax.broadcasted_iota(jnp.int32, (ROWS, COLS), 0) == end
    terrain[0] = jnp.where(top, bed[:HALF], bed[HALF:])
    terrain[1] = jnp.where(top, fric[:HALF], fric[HALF:])
    terrain[2] = jnp.zeros((HALF, COLS), F32)
    terrain[2, 0:1, :] = jnp.where(top, bed[HALF : HALF + 1], bed[HALF - 1 : HALF])
    terrain[2, 1:2, :] = jnp.where(top, fric[HALF : HALF + 1], fric[HALF - 1 : HALF])
    lane = lax.broadcasted_iota(jnp.int32, (1, COLS), 1)
    at = 2 * lax.axis_index("dom")
    names = jnp.where(lane == at, anc[0].astype(F32), 0.0) + jnp.where(lane == at + 1, anc[1].astype(F32), 0.0)
    kept[6] = jnp.zeros((HALF, COLS), F32)
    given[6] = jnp.zeros((HALF, COLS), F32)
    kept[6, 4:5, :] = names
    given[6, 4:5, :] = names

    def edge(row, upper, lower):
        keep[row : row + 1, :] = jnp.where(top, upper, lower)
        give[row : row + 1, :] = jnp.where(top, lower, upper)

    zero = jnp.zeros((1, COLS), F32)
    edge(6, bed[:1], bed[end:])
    edge(7, fric[:1], fric[end:])
    for p in range(2):
        h0 = depth[p] * wet[p].astype(F32)
        qx, qy = xf[p], yf[p]
        edge(p, h0[:1], h0[end:])
        edge(4 + p, zero, qy[end:])
        eta = bed + h0
        qx = x_faces(qx, eta, bed_x, fric)
        qy = jnp.where(last_row, 0.0, flux(qy, eta, below(eta), bed_y, fric))
        h1 = h0 + RATIO * ((left_of(qx) - qx) + (above(qy) - qy))
        edge(2 + p, h1[:1], h1[end:])
        for f, v in enumerate((h1, qx, qy)):
            kept[3 * p + f] = jnp.where(top, v[:HALF], v[HALF:])
            given[3 * p + f] = jnp.where(top, v[HALF:], v[:HALF])
        kept[6, p : p + 1, :] = jnp.where(top, h1[HALF : HALF + 1], h1[HALF - 1 : HALF])
        given[6, p : p + 1, :] = jnp.where(top, h1[HALF - 1 : HALF], h1[HALF : HALF + 1])
        kept[6, 2 + p : 3 + p, :] = jnp.where(top, zero, qy[HALF - 1 : HALF])
        given[6, 2 + p : 3 + p, :] = jnp.where(top, qy[HALF - 1 : HALF], zero)


def second_kernel(own, far, terrain, mine, next_slab, o0, o1, o2, o3, rows, packed):
    z, y, c = place()
    top = c == 0
    slab = lax.axis_index("rows")
    bed, fric = terrain[0], terrain[1]
    bed_in, fric_in = terrain[2, 0:1, :], terrain[2, 1:2, :]
    row = lax.broadcasted_iota(jnp.int32, (HALF, COLS), 0)
    first, last = row == 0, row == HALF - 1
    at_edge = jnp.where(top, 0, HALF - 1)
    lower_edge = jnp.where(top, -1, HALF - 1)
    grid_end = jnp.where(slab == 7, lower_edge, -1)

    def rows_of(n, a, b):
        rows[n] = jnp.zeros((HALF, COLS), F32)
        rows[n, 0:2, :] = a
        rows[n, 2:4, :] = b
        return rows[n]

    in_h = rows_of(0, own[6, 0:2, :], far[6, 0:2, :])
    in_q = rows_of(1, own[6, 2:4, :], far[6, 2:4, :])
    out_h0 = rows_of(2, next_slab[8:10, :], next_slab[0:2, :])
    out_h1 = rows_of(3, next_slab[10:12, :], next_slab[2:4, :])
    out_q = rows_of(4, next_slab[12:14, :], next_slab[4:6, :])
    my_h = rows_of(5, mine[0:2, :], mine[8:10, :])
    my_q = rows_of(6, mine[4:6, :], mine[12:14, :])
    bed_out, fric_out = next_slab[6:7, :], next_slab[7:8, :]
    bed_mine = jnp.where(top, bed[:1], bed[HALF - 1 :])
    eta_mine, eta_out = bed_mine + my_h, bed_out + out_h0
    q1 = flux(
        jnp.where(top, out_q, my_q),
        jnp.where(top, eta_out, eta_mine),
        jnp.where(top, eta_mine, eta_out),
        jnp.maximum(bed_mine, bed_out),
        jnp.where(top, fric_out, fric[HALF - 1 :]),
    )
    q1 = jnp.where(jnp.where(top, slab, 7 - slab) == 0, 0.0, q1)
    out_h = out_h1 + jnp.where(top, -RATIO, RATIO) * q1
    bed_up, fric_up = jnp.where(top, bed_out, bed_in), jnp.where(top, fric_out, fric_in)
    bed_dn = jnp.where(top, bed_in, bed_out)
    eta_up = bed_up + jnp.where(top, out_h, in_h)
    eta_dn = bed_dn + jnp.where(top, in_h, out_h)
    q_up = jnp.where(top, q1, in_q)
    levels = []
    rows[7] = jnp.zeros((HALF, COLS), F32)
    for p in range(4):
        ref, n = (own, 3 * p) if p < 2 else (far, 3 * p - 6)
        q = q1[p : p + 1]
        h1 = ref[n] + jnp.where(row == at_edge, jnp.where(top, RATIO, -RATIO) * q, 0.0)
        qy1 = jnp.where(row == lower_edge, q, ref[n + 2])
        rows[7, p : p + 1, :] = bed[:1] + h1[:1]
        levels.append((h1, ref[n + 1], qy1))
    q2 = flux(q_up, eta_up, rows[7], jnp.maximum(bed_up, bed[:1]), fric_up)
    q2 = jnp.where(2 * slab + c == 0, 0.0, q2)
    bed_x = jnp.maximum(bed, right_of(bed))
    bed_y = jnp.maximum(bed, jnp.where(last, bed_dn, below(bed)))
    fields = []
    for p, (h1, qx, qy) in enumerate(levels):
        eta = bed + h1
        qx = x_faces(qx, eta, bed_x, fric)
        qy = flux(qy, eta, jnp.where(last, eta_dn[p : p + 1], below(eta)), bed_y, fric)
        qy = jnp.where(row == grid_end, 0.0, qy)
        over = jnp.where(first, q2[p : p + 1], above(qy))
        fields.append((h1 + RATIO * ((left_of(qx) - qx) + (over - qy)), qx, qy))
    low, even = masks()
    for f in range(3):
        for t in range(NT):
            a = [fields[p][f][:, 128 * t : 128 * t + 128] for p in range(4)]
            b0, b2 = jnp.where(low, a[0], pltpu.roll(a[2], 4, 0)), jnp.where(low, pltpu.roll(a[0], 4, 0), a[2])
            b1, b3 = jnp.where(low, a[1], pltpu.roll(a[3], 4, 0)), jnp.where(low, pltpu.roll(a[1], 4, 0), a[3])
            pair = [
                jnp.where(even, b0, pltpu.roll(b1, 2, 0)),
                jnp.where(even, pltpu.roll(b0, 6, 0), b1),
                jnp.where(even, b2, pltpu.roll(b3, 2, 0)),
                jnp.where(even, pltpu.roll(b2, 6, 0), b3),
            ]
            for d in range(4):
                n = AT[(d, f, t)]
                packed[n // PER, n % PER] = pair[d]
    names = own[6, 4:5, 0:128] + far[6, 4:5, 0:128]
    for k, out in enumerate((o0, o1, o2, o3)):
        for j in range(4):
            out[PER * j : PER * j + PER] = packed[chunk_at(z, y, role_of(c), k, j, LATE_Z)]
        out[4 * PER] = jnp.zeros((8, 128), F32)
        out[4 * PER, 0:1, :] = names


def masks():
    sub = lax.broadcasted_iota(jnp.int32, (8, 128), 0)
    return sub < 4, (sub & 2) == 0


def select_kernel(anc, m0, m1, m2, m3, t0, t1, t2, t3, o0, o1, o2, o3, held):
    z, y, c = place()
    for n, refs in enumerate(((m0, m1, m2, m3), (t0, t1, t2, t3))):
        for j, ref in enumerate(refs):
            held[n, 4 * PER * j : 4 * PER * j + 4 * PER] = ref[: 4 * PER]
    for k, out in enumerate((o0, o1, o2, o3)):
        for j in range(4):
            at = chunk_at(z, y, role_of(c), k, j)
            dest = ((at >> 2) << 3) | ((at & 3) << 1) | c
            for u in range(2):
                name = anc[2 * dest + u]
                dz, late_dz = (step_of(steps, (name >> 4) ^ z) for steps in (STEP_Z, LATE_Z))
                dy, early_dy = (step_of(steps, ((name >> 2) & 3) ^ y) for steps in (STEP_Y, EARLY_Y))
                for n in range(2):
                    core = c ^ n
                    base = jnp.where(role_of(core) == 0, dy * 4 + dz, late_dz * 4 + early_dy) * PER
                    v = pl.multiple_of((((name >> 1) & 1) ^ core) * 4 + (name & 1) * 2, 2)
                    row = 4 * n + 2 * u
                    out[PER * j : PER * j + PER, row : row + 2, :] = held[n, pl.ds(base, PER), pl.ds(v, 2), :]


def last_kernel(f0, f1, f2, f3, ho, xo, yo, packed):
    z, y, c = place()
    low, even = masks()
    for j, ref in enumerate((f0, f1, f2, f3)):
        for k in range(4):
            packed[pl.ds(chunk_at(z, y, role_of(c), k, j) * PER, PER)] = ref[PER * k : PER * k + PER]
    for f, out in enumerate((ho, xo, yo)):
        for t in range(NT):
            cols = slice(128 * t, 128 * t + 128)
            pair = [packed[AT[(d, f, t)]] for d in range(4)]
            for n in range(2):
                rows = pl.ds(pl.multiple_of((c ^ n) * HALF, HALF), HALF)
                if n == 0:
                    b0 = jnp.where(low, pair[0], pltpu.roll(pair[2], 4, 0))
                    b1 = jnp.where(low, pair[1], pltpu.roll(pair[3], 4, 0))
                else:
                    b0 = jnp.where(low, pltpu.roll(pair[0], 4, 0), pair[2])
                    b1 = jnp.where(low, pltpu.roll(pair[1], 4, 0), pair[3])
                out[0, rows, cols] = jnp.where(even, b0, pltpu.roll(b1, 2, 0))
                out[1, rows, cols] = jnp.where(even, pltpu.roll(b0, 6, 0), b1)


def tiles(n):
    return jax.ShapeDtypeStruct((n, 8, 128), F32)


def params():
    return pltpu.CompilerParams(vmem_limit_bytes=32 * 1024 * 1024)


def swap(v, by_role):
    pairs = [(8 * d + r, 8 * (d ^ by_role[(d ^ r ^ 1) & 1]) + r) for d in range(32) for r in range(8)]
    return lax.ppermute(v, ("dom", "rows"), pairs)


def outer_step(v, k):
    return v if k == 0 else swap(v, (STEP_Z[k] << 3, EARLY_Y[k] << 1))


def inner_step(v, k, inner_z=STEP_Z):
    return v if k == 0 else swap(v, (STEP_Y[k] << 1, inner_z[k] << 3))


def other_core(v):
    return lax.ppermute(v, "dom", [(i, i ^ 1) for i in range(32)])


def next_slab(v):
    low = [((2 * chip + 1) * 8 + r, 2 * chip * 8 + (r + 1) % 8) for chip in range(16) for r in range(8)]
    return lax.ppermute(v, ("dom", "rows"), low + [(b, a) for a, b in low])


def regroup(parts, count):
    return [jnp.concatenate([p[count * j : count * j + count] for p in parts]) for j in range(4)]


def shards(depth, x_flow, y_flow, elevation, roughness, wet, ancestors):
    state = jax.ShapeDtypeStruct((2, ROWS, COLS), F32)
    strip = jax.ShapeDtypeStruct((HALF, COLS), F32)
    halves = jax.ShapeDtypeStruct((7, HALF, COLS), F32)
    ground = jax.ShapeDtypeStruct((3, HALF, COLS), F32)
    args = (depth, x_flow, y_flow, wet, elevation, roughness, ancestors)
    keep, give, kept, given, terrain = pl.pallas_call(
        first_kernel,
        out_shape=[strip, strip, halves, halves, ground],
        in_specs=[HBM] * 7,
        out_specs=[VMEM] * 5,
        scratch_shapes=[pltpu.VMEM(v.shape, v.dtype) for v in args[:6]]
        + [pltpu.SMEM((2,), jnp.int32), pltpu.SemaphoreType.DMA((7,))],
        compiler_params=params(),
    )(*[pltpu.with_memory_space_constraint(v, pltpu.HBM) for v in args])
    mine = jnp.concatenate([keep, other_core(give)])
    far = other_core(given)
    arrived = next_slab(mine)
    parts = pl.pallas_call(
        second_kernel,
        out_shape=[tiles(4 * PER + 1)] * 4,
        in_specs=[VMEM] * 5,
        out_specs=[VMEM] * 4,
        scratch_shapes=[pltpu.VMEM((8, HALF, COLS), F32), pltpu.VMEM((16, PER, 8, 128), F32)],
        compiler_params=params(),
    )(kept, far, terrain, mine, arrived)
    parts = [outer_step(v, k) for k, v in enumerate(parts)]
    names = (parts[0][4 * PER] + parts[1][4 * PER]) + (parts[2][4 * PER] + parts[3][4 * PER])
    parts = [jnp.concatenate([v, names[None]]) for v in regroup(parts, PER)]
    parts = [inner_step(v, k, LATE_Z) for k, v in enumerate(parts)]
    names = sum(v[4 * PER, 0, :64] for v in parts).astype(jnp.int32)
    others = [other_core(v) for v in parts]
    parts = pl.pallas_call(
        select_kernel,
        out_shape=[tiles(4 * PER)] * 4,
        in_specs=[SMEM] + [VMEM] * 8,
        out_specs=[VMEM] * 4,
        scratch_shapes=[pltpu.VMEM((2, 16 * PER, 8, 128), F32)],
        compiler_params=params(),
    )(names, *parts, *others)
    parts = [outer_step(v, k) for k, v in enumerate(parts)]
    parts = [inner_step(v, k) for k, v in enumerate(regroup(parts, PER))]
    return tuple(
        pl.pallas_call(
            last_kernel,
            out_shape=[state] * 3,
            in_specs=[VMEM] * 4,
            out_specs=[VMEM] * 3,
            scratch_shapes=[pltpu.VMEM((16 * PER, 8, 128), F32)],
            compiler_params=params(),
        )(*parts)
    )


def solution(mesh):
    wide = P("dom", "rows", None)
    in_specs = (wide, wide, wide, P("rows", None), P("rows", None), wide, P("dom"))
    return jax.shard_map(shards, mesh=mesh, in_specs=in_specs, out_specs=(wide, wide, wide), check_vma=False)
```

```python
import jax
import jax.numpy as jnp
from jax import lax
from jax.experimental import pallas as pl
from jax.experimental.pallas import tpu as pltpu
from jax.sharding import PartitionSpec as P

GDT = 9.81 * 1.0
SPACING = 10.0
RATIO = 1.0 / 10.0
MIN_DEPTH = 0.05
MANNING = (0.02, 0.025, 0.03, 0.035, 0.045, 0.06, 0.08, 0.1)
ROWS, COLS, HALF = 16, 1536, 8
NT = COLS // 128
F32 = jnp.float32

PER = 9
ITEMS = [(d, f, 3 * z + t) for z in range(4) for d in range(4) for f in range(3) for t in range(3)]
AT = {item: n for n, item in enumerate(ITEMS)}
STEP_Z = (0, 3, 2, 1)
STEP_Y = (0, 2, 1, 3)
LATE_Z = (0, 3, 2, 1)
EARLY_Y = (0, 2, 1, 3)
LAST_Z = (0, 1, 2, 3)
LAST_Y = (0, 1, 3, 2)
VMEM = pl.BlockSpec(memory_space=pltpu.VMEM)
SMEM = pl.BlockSpec(memory_space=pltpu.SMEM)
HBM = pl.BlockSpec(memory_space=pltpu.HBM)


def place():
    dom = lax.axis_index("dom")
    return dom >> 3, (dom >> 1) & 3, dom & 1


def flux(q, eta_a, eta_b, bed, fric):
    he = jnp.maximum(jnp.maximum(eta_a, eta_b) - bed, MIN_DEPTH)
    numer = q - (GDT / SPACING) * he * (eta_b - eta_a)
    denom = 1.0 + fric * jnp.abs(q) * jnp.exp2((-7.0 / 3.0) * jnp.log2(he))
    return numer / denom


def friction(rough):
    total = jnp.zeros(rough.shape, F32)
    for klass, n in enumerate(MANNING):
        total = jnp.where(rough == klass, F32(GDT * (n * n)), total)
    return total


def right_of(v):
    return pltpu.roll(v, COLS - 1, 1)


def left_of(v):
    return pltpu.roll(v, 1, 1)


def below(v):
    return pltpu.roll(v, v.shape[0] - 1, 0)


def above(v):
    return pltpu.roll(v, 1, 0)


def x_faces(q, eta, bed_x, fric):
    last = lax.broadcasted_iota(jnp.int32, q.shape, 1) == COLS - 1
    return jnp.where(last, 0.0, flux(q, eta, right_of(eta), bed_x, fric))


def role_of(core):
    return core ^ (lax.axis_index("rows") & 1) ^ 1


def chunk_at(z, y, role, outer, inner, inner_z=LAST_Z, inner_y=LAST_Y):
    return jnp.where(
        role == 0,
        (z ^ STEP_Z[outer]) * 4 + (y ^ inner_y[inner]),
        (z ^ inner_z[inner]) * 4 + (y ^ EARLY_Y[outer]),
    )


def step_of(steps, distance):
    found = jnp.int32(0)
    for k in range(1, 4):
        found = jnp.where(distance == steps[k], k, found)
    return found


def first_kernel(
    depth_in, xf_in, yf_in, wet_in, elev_in, rough_in, anc_in, keep, give, kept, given, terrain,
    depth, xf, yf, wet, elev, rough, anc, sems,
):
    pairs = zip(
        (elev_in, rough_in, depth_in, wet_in, xf_in, yf_in, anc_in), (elev, rough, depth, wet, xf, yf, anc)
    )
    copies = [pltpu.make_async_copy(src, dst, sems.at[n]) for n, (src, dst) in enumerate(pairs)]
    for copy in copies:
        copy.start()
    for copy in copies:
        copy.wait()
    _, _, c = place()
    top = c == 0
    bed = elev[...]
    fric = friction(rough[...])
    bed_x = jnp.maximum(bed, right_of(bed))
    bed_y = jnp.maximum(bed, below(bed))
    end = ROWS - 1
    last_row = lax.broadcasted_iota(jnp.int32, (ROWS, COLS), 0) == end
    terrain[0] = jnp.where(top, bed[:HALF], bed[HALF:])
    terrain[1] = jnp.where(top, fric[:HALF], fric[HALF:])
    terrain[2] = jnp.zeros((HALF, COLS), F32)
    terrain[2, 0:1, :] = jnp.where(top, bed[HALF : HALF + 1], bed[HALF - 1 : HALF])
    terrain[2, 1:2, :] = jnp.where(top, fric[HALF : HALF + 1], fric[HALF - 1 : HALF])
    lane = lax.broadcasted_iota(jnp.int32, (1, COLS), 1)
    at = 2 * lax.axis_index("dom")
    names = jnp.where(lane == at, anc[0].astype(F32), 0.0) + jnp.where(lane == at + 1, anc[1].astype(F32), 0.0)
    kept[6] = jnp.zeros((HALF, COLS), F32)
    given[6] = jnp.zeros((HALF, COLS), F32)
    kept[6, 4:5, :] = names
    given[6, 4:5, :] = names

    def edge(row, upper, lower):
        keep[row // 2, row % 2 : row % 2 + 1, :] = jnp.where(top, upper, lower)
        give[row // 2, row % 2 : row % 2 + 1, :] = jnp.where(top, lower, upper)

    zero = jnp.zeros((1, COLS), F32)
    edge(6, bed[:1], bed[end:])
    edge(7, fric[:1], fric[end:])
    for p in range(2):
        h0 = depth[p] * wet[p].astype(F32)
        qx, qy = xf[p], yf[p]
        edge(p, h0[:1], h0[end:])
        edge(4 + p, zero, qy[end:])
        eta = bed + h0
        qx = x_faces(qx, eta, bed_x, fric)
        qy = jnp.where(last_row, 0.0, flux(qy, eta, below(eta), bed_y, fric))
        h1 = h0 + RATIO * ((left_of(qx) - qx) + (above(qy) - qy))
        edge(2 + p, h1[:1], h1[end:])
        for f, v in enumerate((h1, qx, qy)):
            kept[3 * p + f] = jnp.where(top, v[:HALF], v[HALF:])
            given[3 * p + f] = jnp.where(top, v[HALF:], v[:HALF])
        kept[6, p : p + 1, :] = jnp.where(top, h1[HALF : HALF + 1], h1[HALF - 1 : HALF])
        given[6, p : p + 1, :] = jnp.where(top, h1[HALF - 1 : HALF], h1[HALF : HALF + 1])
        kept[6, 2 + p : 3 + p, :] = jnp.where(top, zero, qy[HALF - 1 : HALF])
        given[6, 2 + p : 3 + p, :] = jnp.where(top, qy[HALF - 1 : HALF], zero)


def second_kernel(own, far, terrain, mine, next_slab, o0, o1, o2, o3, rows, packed):
    z, y, c = place()
    top = c == 0
    slab = lax.axis_index("rows")
    bed, fric = terrain[0], terrain[1]
    bed_in, fric_in = terrain[2, 0:1, :], terrain[2, 1:2, :]
    row = lax.broadcasted_iota(jnp.int32, (HALF, COLS), 0)
    first, last = row == 0, row == HALF - 1
    at_edge = jnp.where(top, 0, HALF - 1)
    lower_edge = jnp.where(top, -1, HALF - 1)
    grid_end = jnp.where(slab == 7, lower_edge, -1)

    def rows_of(n, a, b):
        rows[n] = jnp.zeros((HALF, COLS), F32)
        rows[n, 0:2, :] = a
        rows[n, 2:4, :] = b
        return rows[n]

    in_h = rows_of(0, own[6, 0:2, :], far[6, 0:2, :])
    in_q = rows_of(1, own[6, 2:4, :], far[6, 2:4, :])
    out_h0 = rows_of(2, next_slab[4], next_slab[0])
    out_h1 = rows_of(3, next_slab[5], next_slab[1])
    out_q = rows_of(4, next_slab[6], next_slab[2])
    my_h = rows_of(5, mine[0], mine[4])
    my_q = rows_of(6, mine[2], mine[6])
    bed_out, fric_out = next_slab[3, 0:1, :], next_slab[3, 1:2, :]
    bed_mine = jnp.where(top, bed[:1], bed[HALF - 1 :])
    eta_mine, eta_out = bed_mine + my_h, bed_out + out_h0
    q1 = flux(
        jnp.where(top, out_q, my_q),
        jnp.where(top, eta_out, eta_mine),
        jnp.where(top, eta_mine, eta_out),
        jnp.maximum(bed_mine, bed_out),
        jnp.where(top, fric_out, fric[HALF - 1 :]),
    )
    q1 = jnp.where(jnp.where(top, slab, 7 - slab) == 0, 0.0, q1)
    out_h = out_h1 + jnp.where(top, -RATIO, RATIO) * q1
    bed_up, fric_up = jnp.where(top, bed_out, bed_in), jnp.where(top, fric_out, fric_in)
    bed_dn = jnp.where(top, bed_in, bed_out)
    eta_up = bed_up + jnp.where(top, out_h, in_h)
    eta_dn = bed_dn + jnp.where(top, in_h, out_h)
    q_up = jnp.where(top, q1, in_q)
    levels = []
    rows[7] = jnp.zeros((HALF, COLS), F32)
    for p in range(4):
        ref, n = (own, 3 * p) if p < 2 else (far, 3 * p - 6)
        q = q1[p : p + 1]
        h1 = ref[n] + jnp.where(row == at_edge, jnp.where(top, RATIO, -RATIO) * q, 0.0)
        qy1 = jnp.where(row == lower_edge, q, ref[n + 2])
        rows[7, p : p + 1, :] = bed[:1] + h1[:1]
        levels.append((h1, ref[n + 1], qy1))
    q2 = flux(q_up, eta_up, rows[7], jnp.maximum(bed_up, bed[:1]), fric_up)
    q2 = jnp.where(2 * slab + c == 0, 0.0, q2)
    bed_x = jnp.maximum(bed, right_of(bed))
    bed_y = jnp.maximum(bed, jnp.where(last, bed_dn, below(bed)))
    fields = []
    for p, (h1, qx, qy) in enumerate(levels):
        eta = bed + h1
        qx = x_faces(qx, eta, bed_x, fric)
        qy = flux(qy, eta, jnp.where(last, eta_dn[p : p + 1], below(eta)), bed_y, fric)
        qy = jnp.where(row == grid_end, 0.0, qy)
        over = jnp.where(first, q2[p : p + 1], above(qy))
        fields.append((h1 + RATIO * ((left_of(qx) - qx) + (over - qy)), qx, qy))
    low, even = masks()
    for f in range(3):
        for t in range(NT):
            a = [fields[p][f][:, 128 * t : 128 * t + 128] for p in range(4)]
            b0, b2 = jnp.where(low, a[0], pltpu.roll(a[2], 4, 0)), jnp.where(low, pltpu.roll(a[0], 4, 0), a[2])
            b1, b3 = jnp.where(low, a[1], pltpu.roll(a[3], 4, 0)), jnp.where(low, pltpu.roll(a[1], 4, 0), a[3])
            pair = [
                jnp.where(even, b0, pltpu.roll(b1, 2, 0)),
                jnp.where(even, pltpu.roll(b0, 6, 0), b1),
                jnp.where(even, b2, pltpu.roll(b3, 2, 0)),
                jnp.where(even, pltpu.roll(b2, 6, 0), b3),
            ]
            for d in range(4):
                n = AT[(d, f, t)]
                packed[n // PER, n % PER] = pair[d]
    names = own[6, 4:5, 0:128] + far[6, 4:5, 0:128]
    for k, out in enumerate((o0, o1, o2, o3)):
        for j in range(4):
            out[PER * j : PER * j + PER] = packed[chunk_at(z, y, role_of(c), k, j, LATE_Z, STEP_Y)]
        out[4 * PER] = jnp.zeros((8, 128), F32)
        out[4 * PER, 0:1, :] = names


def masks():
    sub = lax.broadcasted_iota(jnp.int32, (8, 128), 0)
    return sub < 4, (sub & 2) == 0


def select_kernel(codes, m0, m1, m2, m3, t0, t1, t2, t3, o0, o1, o2, o3, held):
    z, y, c = place()
    for n, refs in enumerate(((m0, m1, m2, m3), (t0, t1, t2, t3))):
        for j, ref in enumerate(refs):
            held[n, 4 * PER * j : 4 * PER * j + 4 * PER] = ref[: 4 * PER]
    for k, out in enumerate((o0, o1, o2, o3)):
        for j in range(4):
            at = chunk_at(z, y, role_of(c), k, j)
            dest = ((at >> 2) << 3) | ((at & 3) << 1) | c
            for u in range(2):
                for n in range(2):
                    code = codes[64 * n + 2 * dest + u]
                    v = pl.multiple_of(code & 6, 2)
                    row = 4 * n + 2 * u
                    out[PER * j : PER * j + PER, row : row + 2, :] = held[n, pl.ds(code >> 3, PER), pl.ds(v, 2), :]


def codes_of(names):
    z, y, c = place()
    dz, late_dz = (step_of(steps, (names >> 4) ^ z) for steps in (STEP_Z, LATE_Z))
    dy, early_dy = (step_of(steps, ((names >> 2) & 3) ^ y) for steps in (STEP_Y, EARLY_Y))
    codes = []
    for n in range(2):
        core = c ^ n
        base = jnp.where(role_of(core) == 0, dy * 4 + dz, late_dz * 4 + early_dy) * PER
        codes.append(base * 8 + (((names >> 1) & 1) ^ core) * 4 + (names & 1) * 2)
    return jnp.concatenate(codes)


def last_kernel(f0, f1, f2, f3, ho, xo, yo, packed):
    z, y, c = place()
    low, even = masks()
    for j, ref in enumerate((f0, f1, f2, f3)):
        for k in range(4):
            packed[pl.ds(chunk_at(z, y, role_of(c), k, j) * PER, PER)] = ref[PER * k : PER * k + PER]
    for f, out in enumerate((ho, xo, yo)):
        for t in range(NT):
            cols = slice(128 * t, 128 * t + 128)
            pair = [packed[AT[(d, f, t)]] for d in range(4)]
            for n in range(2):
                rows = pl.ds(pl.multiple_of((c ^ n) * HALF, HALF), HALF)
                if n == 0:
                    b0 = jnp.where(low, pair[0], pltpu.roll(pair[2], 4, 0))
                    b1 = jnp.where(low, pair[1], pltpu.roll(pair[3], 4, 0))
                else:
                    b0 = jnp.where(low, pltpu.roll(pair[0], 4, 0), pair[2])
                    b1 = jnp.where(low, pltpu.roll(pair[1], 4, 0), pair[3])
                out[0, rows, cols] = jnp.where(even, b0, pltpu.roll(b1, 2, 0))
                out[1, rows, cols] = jnp.where(even, pltpu.roll(b0, 6, 0), b1)


def tiles(n):
    return jax.ShapeDtypeStruct((n, 8, 128), F32)


def params():
    return pltpu.CompilerParams(vmem_limit_bytes=32 * 1024 * 1024)


def swap(v, by_role):
    pairs = [(8 * d + r, 8 * (d ^ by_role[(d ^ r ^ 1) & 1]) + r) for d in range(32) for r in range(8)]
    return lax.ppermute(v, ("dom", "rows"), pairs)


def outer_step(v, k):
    return v if k == 0 else swap(v, (STEP_Z[k] << 3, EARLY_Y[k] << 1))


def inner_step(v, k, inner_z=LAST_Z, inner_y=LAST_Y):
    return v if k == 0 else swap(v, (inner_y[k] << 1, inner_z[k] << 3))


def other_core(v):
    return lax.ppermute(v, "dom", [(i, i ^ 1) for i in range(32)])


def next_slab(v):
    low = [((2 * chip + 1) * 8 + r, 2 * chip * 8 + (r + 1) % 8) for chip in range(16) for r in range(8)]
    return lax.ppermute(v, ("dom", "rows"), low + [(b, a) for a, b in low])


def regroup(parts, count):
    return [jnp.concatenate([p[count * j : count * j + count] for p in parts]) for j in range(4)]


def shards(depth, x_flow, y_flow, elevation, roughness, wet, ancestors):
    state = jax.ShapeDtypeStruct((2, ROWS, COLS), F32)
    strip = jax.ShapeDtypeStruct((4, 2, COLS), F32)
    halves = jax.ShapeDtypeStruct((7, HALF, COLS), F32)
    ground = jax.ShapeDtypeStruct((3, HALF, COLS), F32)
    args = (depth, x_flow, y_flow, wet, elevation, roughness, ancestors)
    keep, give, kept, given, terrain = pl.pallas_call(
        first_kernel,
        out_shape=[strip, strip, halves, halves, ground],
        in_specs=[HBM] * 7,
        out_specs=[VMEM] * 5,
        scratch_shapes=[pltpu.VMEM(v.shape, v.dtype) for v in args[:6]]
        + [pltpu.SMEM((2,), jnp.int32), pltpu.SemaphoreType.DMA((7,))],
        compiler_params=params(),
    )(*[pltpu.with_memory_space_constraint(v, pltpu.HBM) for v in args])
    mine = jnp.concatenate([keep, other_core(give)[:3]])
    far = other_core(given)
    arrived = next_slab(mine)
    parts = pl.pallas_call(
        second_kernel,
        out_shape=[tiles(4 * PER + 1)] * 4,
        in_specs=[VMEM] * 5,
        out_specs=[VMEM] * 4,
        scratch_shapes=[pltpu.VMEM((8, HALF, COLS), F32), pltpu.VMEM((16, PER, 8, 128), F32)],
        compiler_params=params(),
    )(kept, far, terrain, mine, arrived)
    parts = [outer_step(v, k) for k, v in enumerate(parts)]
    names = (parts[0][4 * PER] + parts[1][4 * PER]) + (parts[2][4 * PER] + parts[3][4 * PER])
    parts = [jnp.concatenate([v, names[None]]) for v in regroup(parts, PER)]
    parts = [inner_step(v, k, LATE_Z, STEP_Y) for k, v in enumerate(parts)]
    names = sum(v[4 * PER, 0, :64] for v in parts).astype(jnp.int32)
    others = [other_core(v) for v in parts]
    parts = pl.pallas_call(
        select_kernel,
        out_shape=[tiles(4 * PER)] * 4,
        in_specs=[SMEM] + [VMEM] * 8,
        out_specs=[VMEM] * 4,
        scratch_shapes=[pltpu.VMEM((2, 16 * PER, 8, 128), F32)],
        compiler_params=params(),
    )(codes_of(names), *parts, *others)
    parts = [outer_step(v, k) for k, v in enumerate(parts)]
    parts = [inner_step(v, k) for k, v in enumerate(regroup(parts, PER))]
    return tuple(
        pl.pallas_call(
            last_kernel,
            out_shape=[state] * 3,
            in_specs=[VMEM] * 4,
            out_specs=[VMEM] * 3,
            scratch_shapes=[pltpu.VMEM((16 * PER, 8, 128), F32)],
            compiler_params=params(),
        )(*parts)
    )


def solution(mesh):
    wide = P("dom", "rows", None)
    in_specs = (wide, wide, wide, P("rows", None), P("rows", None), wide, P("dom"))
    return jax.shard_map(shards, mesh=mesh, in_specs=in_specs, out_specs=(wide, wide, wide), check_vma=False)
```

```python
import jax
import jax.numpy as jnp
from jax import lax
from jax.experimental import pallas as pl
from jax.experimental.pallas import tpu as pltpu
from jax.sharding import PartitionSpec as P

GDT = 9.81 * 1.0
SPACING = 10.0
RATIO = 1.0 / 10.0
MIN_DEPTH = 0.05
MANNING = (0.02, 0.025, 0.03, 0.035, 0.045, 0.06, 0.08, 0.1)
ROWS, COLS, HALF = 16, 1536, 8
NT = COLS // 128
F32 = jnp.float32

PER = 9
ITEMS = [(d, f, 3 * z + t) for z in range(4) for d in range(4) for f in range(3) for t in range(3)]
AT = {item: n for n, item in enumerate(ITEMS)}
STEP_Z = (0, 3, 2, 1)
STEP_Y = (0, 2, 1, 3)
LATE_Z = (0, 3, 2, 1)
EARLY_Y = (0, 2, 1, 3)
LAST_Z = (0, 1, 2, 3)
LAST_Y = (0, 1, 3, 2)
VMEM = pl.BlockSpec(memory_space=pltpu.VMEM)
SMEM = pl.BlockSpec(memory_space=pltpu.SMEM)
HBM = pl.BlockSpec(memory_space=pltpu.HBM)


def place():
    dom = lax.axis_index("dom")
    return dom >> 3, (dom >> 1) & 3, dom & 1


def flux(q, eta_a, eta_b, bed, fric):
    he = jnp.maximum(jnp.maximum(eta_a, eta_b) - bed, MIN_DEPTH)
    numer = q - (GDT / SPACING) * he * (eta_b - eta_a)
    denom = 1.0 + fric * jnp.abs(q) * jnp.exp2((-7.0 / 3.0) * jnp.log2(he))
    return numer / denom


def friction(rough):
    total = jnp.zeros(rough.shape, F32)
    for klass, n in enumerate(MANNING):
        total = jnp.where(rough == klass, F32(GDT * (n * n)), total)
    return total


def right_of(v):
    return pltpu.roll(v, COLS - 1, 1)


def left_of(v):
    return pltpu.roll(v, 1, 1)


def below(v):
    return pltpu.roll(v, v.shape[0] - 1, 0)


def above(v):
    return pltpu.roll(v, 1, 0)


def x_faces(q, eta, bed_x, fric):
    last = lax.broadcasted_iota(jnp.int32, q.shape, 1) == COLS - 1
    return jnp.where(last, 0.0, flux(q, eta, right_of(eta), bed_x, fric))


def role_of(core):
    return core ^ (lax.axis_index("rows") & 1) ^ 1


def chunk_at(z, y, role, outer, inner, inner_z=LAST_Z, inner_y=LAST_Y):
    return jnp.where(
        role == 0,
        (z ^ STEP_Z[outer]) * 4 + (y ^ inner_y[inner]),
        (z ^ inner_z[inner]) * 4 + (y ^ EARLY_Y[outer]),
    )


def step_of(steps, distance):
    found = jnp.int32(0)
    for k in range(1, 4):
        found = jnp.where(distance == steps[k], k, found)
    return found


def first_kernel(
    depth_in, xf_in, yf_in, wet_in, elev_in, rough_in, anc_in, keep, give, kept, given, terrain,
    depth, xf, yf, wet, elev, rough, anc, sems,
):
    pairs = [(elev_in, elev), (rough_in, rough), (anc_in, anc)]
    for p in range(2):
        fields = ((depth_in, depth), (wet_in, wet), (xf_in, xf), (yf_in, yf))
        pairs += [(src.at[p], dst.at[p]) for src, dst in fields]
    copies = [pltpu.make_async_copy(src, dst, sems.at[n]) for n, (src, dst) in enumerate(pairs)]
    for copy in copies:
        copy.start()
    for copy in copies[:3]:
        copy.wait()
    _, _, c = place()
    top = c == 0
    bed = elev[...]
    fric = friction(rough[...])
    bed_x = jnp.maximum(bed, right_of(bed))
    bed_y = jnp.maximum(bed, below(bed))
    end = ROWS - 1
    last_row = lax.broadcasted_iota(jnp.int32, (ROWS, COLS), 0) == end
    terrain[0] = jnp.where(top, bed[:HALF], bed[HALF:])
    terrain[1] = jnp.where(top, fric[:HALF], fric[HALF:])
    terrain[2] = jnp.zeros((HALF, COLS), F32)
    terrain[2, 0:1, :] = jnp.where(top, bed[HALF : HALF + 1], bed[HALF - 1 : HALF])
    terrain[2, 1:2, :] = jnp.where(top, fric[HALF : HALF + 1], fric[HALF - 1 : HALF])
    lane = lax.broadcasted_iota(jnp.int32, (1, COLS), 1)
    at = 2 * lax.axis_index("dom")
    names = jnp.where(lane == at, anc[0].astype(F32), 0.0) + jnp.where(lane == at + 1, anc[1].astype(F32), 0.0)
    kept[6] = jnp.zeros((HALF, COLS), F32)
    given[6] = jnp.zeros((HALF, COLS), F32)
    kept[6, 4:5, :] = names
    given[6, 4:5, :] = names

    def edge(row, upper, lower):
        keep[row // 2, row % 2 : row % 2 + 1, :] = jnp.where(top, upper, lower)
        give[row // 2, row % 2 : row % 2 + 1, :] = jnp.where(top, lower, upper)

    zero = jnp.zeros((1, COLS), F32)
    edge(6, bed[:1], bed[end:])
    edge(7, fric[:1], fric[end:])
    for p in range(2):
        for copy in copies[3 + 4 * p : 7 + 4 * p]:
            copy.wait()
        h0 = depth[p] * wet[p].astype(F32)
        qx, qy = xf[p], yf[p]
        edge(p, h0[:1], h0[end:])
        edge(4 + p, zero, qy[end:])
        eta = bed + h0
        qx = x_faces(qx, eta, bed_x, fric)
        qy = jnp.where(last_row, 0.0, flux(qy, eta, below(eta), bed_y, fric))
        h1 = h0 + RATIO * ((left_of(qx) - qx) + (above(qy) - qy))
        edge(2 + p, h1[:1], h1[end:])
        for f, v in enumerate((h1, qx, qy)):
            kept[3 * p + f] = jnp.where(top, v[:HALF], v[HALF:])
            given[3 * p + f] = jnp.where(top, v[HALF:], v[:HALF])
        kept[6, p : p + 1, :] = jnp.where(top, h1[HALF : HALF + 1], h1[HALF - 1 : HALF])
        given[6, p : p + 1, :] = jnp.where(top, h1[HALF - 1 : HALF], h1[HALF : HALF + 1])
        kept[6, 2 + p : 3 + p, :] = jnp.where(top, zero, qy[HALF - 1 : HALF])
        given[6, 2 + p : 3 + p, :] = jnp.where(top, qy[HALF - 1 : HALF], zero)


def second_kernel(own, far, terrain, mine, next_slab, o0, o1, o2, o3, rows, packed):
    z, y, c = place()
    top = c == 0
    slab = lax.axis_index("rows")
    bed, fric = terrain[0], terrain[1]
    bed_in, fric_in = terrain[2, 0:1, :], terrain[2, 1:2, :]
    row = lax.broadcasted_iota(jnp.int32, (HALF, COLS), 0)
    first, last = row == 0, row == HALF - 1
    at_edge = jnp.where(top, 0, HALF - 1)
    lower_edge = jnp.where(top, -1, HALF - 1)
    grid_end = jnp.where(slab == 7, lower_edge, -1)

    def rows_of(n, a, b):
        rows[n] = jnp.zeros((HALF, COLS), F32)
        rows[n, 0:2, :] = a
        rows[n, 2:4, :] = b
        return rows[n]

    in_h = rows_of(0, own[6, 0:2, :], far[6, 0:2, :])
    in_q = rows_of(1, own[6, 2:4, :], far[6, 2:4, :])
    out_h0 = rows_of(2, next_slab[4], next_slab[0])
    out_h1 = rows_of(3, next_slab[5], next_slab[1])
    out_q = rows_of(4, next_slab[6], next_slab[2])
    my_h = rows_of(5, mine[0], mine[4])
    my_q = rows_of(6, mine[2], mine[6])
    bed_out, fric_out = next_slab[3, 0:1, :], next_slab[3, 1:2, :]
    bed_mine = jnp.where(top, bed[:1], bed[HALF - 1 :])
    eta_mine, eta_out = bed_mine + my_h, bed_out + out_h0
    q1 = flux(
        jnp.where(top, out_q, my_q),
        jnp.where(top, eta_out, eta_mine),
        jnp.where(top, eta_mine, eta_out),
        jnp.maximum(bed_mine, bed_out),
        jnp.where(top, fric_out, fric[HALF - 1 :]),
    )
    q1 = jnp.where(jnp.where(top, slab, 7 - slab) == 0, 0.0, q1)
    out_h = out_h1 + jnp.where(top, -RATIO, RATIO) * q1
    bed_up, fric_up = jnp.where(top, bed_out, bed_in), jnp.where(top, fric_out, fric_in)
    bed_dn = jnp.where(top, bed_in, bed_out)
    eta_up = bed_up + jnp.where(top, out_h, in_h)
    eta_dn = bed_dn + jnp.where(top, in_h, out_h)
    q_up = jnp.where(top, q1, in_q)
    levels = []
    rows[7] = jnp.zeros((HALF, COLS), F32)
    for p in range(4):
        ref, n = (own, 3 * p) if p < 2 else (far, 3 * p - 6)
        q = q1[p : p + 1]
        h1 = ref[n] + jnp.where(row == at_edge, jnp.where(top, RATIO, -RATIO) * q, 0.0)
        qy1 = jnp.where(row == lower_edge, q, ref[n + 2])
        rows[7, p : p + 1, :] = bed[:1] + h1[:1]
        levels.append((h1, ref[n + 1], qy1))
    q2 = flux(q_up, eta_up, rows[7], jnp.maximum(bed_up, bed[:1]), fric_up)
    q2 = jnp.where(2 * slab + c == 0, 0.0, q2)
    bed_x = jnp.maximum(bed, right_of(bed))
    bed_y = jnp.maximum(bed, jnp.where(last, bed_dn, below(bed)))
    fields = []
    for p, (h1, qx, qy) in enumerate(levels):
        eta = bed + h1
        qx = x_faces(qx, eta, bed_x, fric)
        qy = flux(qy, eta, jnp.where(last, eta_dn[p : p + 1], below(eta)), bed_y, fric)
        qy = jnp.where(row == grid_end, 0.0, qy)
        over = jnp.where(first, q2[p : p + 1], above(qy))
        fields.append((h1 + RATIO * ((left_of(qx) - qx) + (over - qy)), qx, qy))
    low, even = masks()
    for f in range(3):
        for t in range(NT):
            a = [fields[p][f][:, 128 * t : 128 * t + 128] for p in range(4)]
            b0, b2 = jnp.where(low, a[0], pltpu.roll(a[2], 4, 0)), jnp.where(low, pltpu.roll(a[0], 4, 0), a[2])
            b1, b3 = jnp.where(low, a[1], pltpu.roll(a[3], 4, 0)), jnp.where(low, pltpu.roll(a[1], 4, 0), a[3])
            pair = [
                jnp.where(even, b0, pltpu.roll(b1, 2, 0)),
                jnp.where(even, pltpu.roll(b0, 6, 0), b1),
                jnp.where(even, b2, pltpu.roll(b3, 2, 0)),
                jnp.where(even, pltpu.roll(b2, 6, 0), b3),
            ]
            for d in range(4):
                n = AT[(d, f, t)]
                packed[n // PER, n % PER] = pair[d]
    names = own[6, 4:5, 0:128] + far[6, 4:5, 0:128]
    for k, out in enumerate((o0, o1, o2, o3)):
        for j in range(4):
            out[PER * j : PER * j + PER] = packed[chunk_at(z, y, role_of(c), k, j, LATE_Z, STEP_Y)]
        out[4 * PER] = jnp.zeros((8, 128), F32)
        out[4 * PER, 0:1, :] = names


def masks():
    sub = lax.broadcasted_iota(jnp.int32, (8, 128), 0)
    return sub < 4, (sub & 2) == 0


def select_kernel(codes, m0, m1, m2, m3, t0, t1, t2, t3, o0, o1, o2, o3, held):
    z, y, c = place()
    for n, refs in enumerate(((m0, m1, m2, m3), (t0, t1, t2, t3))):
        for j, ref in enumerate(refs):
            held[n, 4 * PER * j : 4 * PER * j + 4 * PER] = ref[: 4 * PER]
    for k, out in enumerate((o0, o1, o2, o3)):
        for j in range(4):
            at = chunk_at(z, y, role_of(c), k, j)
            dest = ((at >> 2) << 3) | ((at & 3) << 1) | c
            for u in range(2):
                for n in range(2):
                    code = codes[64 * n + 2 * dest + u]
                    v = pl.multiple_of(code & 6, 2)
                    row = 4 * n + 2 * u
                    out[PER * j : PER * j + PER, row : row + 2, :] = held[n, pl.ds(code >> 3, PER), pl.ds(v, 2), :]


def codes_of(names):
    z, y, c = place()
    dz, late_dz = (step_of(steps, (names >> 4) ^ z) for steps in (STEP_Z, LATE_Z))
    dy, early_dy = (step_of(steps, ((names >> 2) & 3) ^ y) for steps in (STEP_Y, EARLY_Y))
    codes = []
    for n in range(2):
        core = c ^ n
        base = jnp.where(role_of(core) == 0, dy * 4 + dz, late_dz * 4 + early_dy) * PER
        codes.append(base * 8 + (((names >> 1) & 1) ^ core) * 4 + (names & 1) * 2)
    return jnp.concatenate(codes)


def last_kernel(f0, f1, f2, f3, ho, xo, yo, packed, done, sems):
    z, y, c = place()
    low, even = masks()
    for j, ref in enumerate((f0, f1, f2, f3)):
        for k in range(4):
            packed[pl.ds(chunk_at(z, y, role_of(c), k, j) * PER, PER)] = ref[PER * k : PER * k + PER]
    copies = []
    for f, target in enumerate((ho, xo, yo)):
        out = done.at[f]
        for t in range(NT):
            cols = slice(128 * t, 128 * t + 128)
            pair = [packed[AT[(d, f, t)]] for d in range(4)]
            for n in range(2):
                rows = pl.ds(pl.multiple_of((c ^ n) * HALF, HALF), HALF)
                if n == 0:
                    b0 = jnp.where(low, pair[0], pltpu.roll(pair[2], 4, 0))
                    b1 = jnp.where(low, pair[1], pltpu.roll(pair[3], 4, 0))
                else:
                    b0 = jnp.where(low, pltpu.roll(pair[0], 4, 0), pair[2])
                    b1 = jnp.where(low, pltpu.roll(pair[1], 4, 0), pair[3])
                out[0, rows, cols] = jnp.where(even, b0, pltpu.roll(b1, 2, 0))
                out[1, rows, cols] = jnp.where(even, pltpu.roll(b0, 6, 0), b1)
        copies.append(pltpu.make_async_copy(out, target, sems.at[f]))
        copies[f].start()
    for copy in copies:
        copy.wait()


def tiles(n):
    return jax.ShapeDtypeStruct((n, 8, 128), F32)


def params():
    return pltpu.CompilerParams(vmem_limit_bytes=32 * 1024 * 1024)


def swap(v, by_role):
    pairs = [(8 * d + r, 8 * (d ^ by_role[(d ^ r ^ 1) & 1]) + r) for d in range(32) for r in range(8)]
    return lax.ppermute(v, ("dom", "rows"), pairs)


def outer_step(v, k):
    return v if k == 0 else swap(v, (STEP_Z[k] << 3, EARLY_Y[k] << 1))


def inner_step(v, k, inner_z=LAST_Z, inner_y=LAST_Y):
    return v if k == 0 else swap(v, (inner_y[k] << 1, inner_z[k] << 3))


def other_core(v):
    return lax.ppermute(v, "dom", [(i, i ^ 1) for i in range(32)])


def next_slab(v):
    low = [((2 * chip + 1) * 8 + r, 2 * chip * 8 + (r + 1) % 8) for chip in range(16) for r in range(8)]
    return lax.ppermute(v, ("dom", "rows"), low + [(b, a) for a, b in low])


def regroup(parts, count):
    return [jnp.concatenate([p[count * j : count * j + count] for p in parts]) for j in range(4)]


def shards(depth, x_flow, y_flow, elevation, roughness, wet, ancestors):
    state = jax.ShapeDtypeStruct((2, ROWS, COLS), F32)
    strip = jax.ShapeDtypeStruct((4, 2, COLS), F32)
    halves = jax.ShapeDtypeStruct((7, HALF, COLS), F32)
    ground = jax.ShapeDtypeStruct((3, HALF, COLS), F32)
    args = (depth, x_flow, y_flow, wet, elevation, roughness, ancestors)
    keep, give, kept, given, terrain = pl.pallas_call(
        first_kernel,
        out_shape=[strip, strip, halves, halves, ground],
        in_specs=[HBM] * 7,
        out_specs=[VMEM] * 5,
        scratch_shapes=[pltpu.VMEM(v.shape, v.dtype) for v in args[:6]]
        + [pltpu.SMEM((2,), jnp.int32), pltpu.SemaphoreType.DMA((11,))],
        compiler_params=params(),
    )(*[pltpu.with_memory_space_constraint(v, pltpu.HBM) for v in args])
    mine = jnp.concatenate([keep, other_core(give)[:3]])
    far = other_core(given)
    arrived = next_slab(mine)
    parts = pl.pallas_call(
        second_kernel,
        out_shape=[tiles(4 * PER + 1)] * 4,
        in_specs=[VMEM] * 5,
        out_specs=[VMEM] * 4,
        scratch_shapes=[pltpu.VMEM((8, HALF, COLS), F32), pltpu.VMEM((16, PER, 8, 128), F32)],
        compiler_params=params(),
    )(kept, far, terrain, mine, arrived)
    parts = [outer_step(v, k) for k, v in enumerate(parts)]
    names = (parts[0][4 * PER] + parts[1][4 * PER]) + (parts[2][4 * PER] + parts[3][4 * PER])
    parts = [jnp.concatenate([v, names[None]]) for v in regroup(parts, PER)]
    parts = [inner_step(v, k, LATE_Z, STEP_Y) for k, v in enumerate(parts)]
    names = sum(v[4 * PER, 0, :64] for v in parts).astype(jnp.int32)
    others = [other_core(v) for v in parts]
    parts = pl.pallas_call(
        select_kernel,
        out_shape=[tiles(4 * PER)] * 4,
        in_specs=[SMEM] + [VMEM] * 8,
        out_specs=[VMEM] * 4,
        scratch_shapes=[pltpu.VMEM((2, 16 * PER, 8, 128), F32)],
        compiler_params=params(),
    )(codes_of(names), *parts, *others)
    parts = [outer_step(v, k) for k, v in enumerate(parts)]
    parts = [inner_step(v, k) for k, v in enumerate(regroup(parts, PER))]
    return tuple(
        pl.pallas_call(
            last_kernel,
            out_shape=[state] * 3,
            in_specs=[VMEM] * 4,
            out_specs=[HBM] * 3,
            scratch_shapes=[
                pltpu.VMEM((16 * PER, 8, 128), F32),
                pltpu.VMEM((3, 2, ROWS, COLS), F32),
                pltpu.SemaphoreType.DMA((3,)),
            ],
            compiler_params=params(),
        )(*parts)
    )


def solution(mesh):
    wide = P("dom", "rows", None)
    in_specs = (wide, wide, wide, P("rows", None), P("rows", None), wide, P("dom"))
    return jax.shard_map(shards, mesh=mesh, in_specs=in_specs, out_specs=(wide, wide, wide), check_vma=False)
```

```python
import jax
import jax.numpy as jnp
from jax import lax
from jax.experimental import pallas as pl
from jax.experimental.pallas import tpu as pltpu
from jax.sharding import PartitionSpec as P

GDT = 9.81 * 1.0
SPACING = 10.0
RATIO = 1.0 / 10.0
MIN_DEPTH = 0.05
MANNING = (0.02, 0.025, 0.03, 0.035, 0.045, 0.06, 0.08, 0.1)
ROWS, COLS, HALF = 16, 1536, 8
NT = COLS // 128
F32 = jnp.float32

PER = 9
ITEMS = [(d, f, 3 * z + t) for z in range(4) for d in range(4) for f in range(3) for t in range(3)]
AT = {item: n for n, item in enumerate(ITEMS)}
STEP_Z = (0, 3, 2, 1)
STEP_Y = (0, 2, 1, 3)
LATE_Z = (0, 3, 2, 1)
EARLY_Y = (0, 2, 1, 3)
LAST_Z = (0, 1, 2, 3)
LAST_Y = (0, 1, 3, 2)
VMEM = pl.BlockSpec(memory_space=pltpu.VMEM)
SMEM = pl.BlockSpec(memory_space=pltpu.SMEM)
HBM = pl.BlockSpec(memory_space=pltpu.HBM)


def place():
    dom = lax.axis_index("dom")
    return dom >> 3, (dom >> 1) & 3, dom & 1


def flux(q, eta_a, eta_b, bed, fric):
    he = jnp.maximum(jnp.maximum(eta_a, eta_b) - bed, MIN_DEPTH)
    numer = q - (GDT / SPACING) * he * (eta_b - eta_a)
    denom = 1.0 + fric * jnp.abs(q) * jnp.exp2((-7.0 / 3.0) * jnp.log2(he))
    return numer / denom


def friction(rough):
    total = jnp.zeros(rough.shape, F32)
    for klass, n in enumerate(MANNING):
        total = jnp.where(rough == klass, F32(GDT * (n * n)), total)
    return total


def right_of(v):
    return pltpu.roll(v, COLS - 1, 1)


def left_of(v):
    return pltpu.roll(v, 1, 1)


def below(v):
    return pltpu.roll(v, v.shape[0] - 1, 0)


def above(v):
    return pltpu.roll(v, 1, 0)


def x_faces(q, eta, bed_x, fric):
    last = lax.broadcasted_iota(jnp.int32, q.shape, 1) == COLS - 1
    return jnp.where(last, 0.0, flux(q, eta, right_of(eta), bed_x, fric))


def role_of(core):
    return core ^ (lax.axis_index("rows") & 1) ^ 1


def chunk_at(z, y, role, outer, inner, inner_z=LAST_Z, inner_y=LAST_Y):
    return jnp.where(
        role == 0,
        (z ^ STEP_Z[outer]) * 4 + (y ^ inner_y[inner]),
        (z ^ inner_z[inner]) * 4 + (y ^ EARLY_Y[outer]),
    )


def step_of(steps, distance):
    found = jnp.int32(0)
    for k in range(1, 4):
        found = jnp.where(distance == steps[k], k, found)
    return found


def first_kernel(
    depth_in, xf_in, yf_in, wet_in, elev_in, rough_in, anc_in, keep, give, kept, given, terrain,
    depth, xf, yf, wet, elev, rough, anc, sems,
):
    pairs = [(elev_in, elev), (rough_in, rough), (anc_in, anc)]
    for p in range(2):
        fields = ((depth_in, depth), (wet_in, wet), (xf_in, xf), (yf_in, yf))
        pairs += [(src.at[p], dst.at[p]) for src, dst in fields]
    copies = [pltpu.make_async_copy(src, dst, sems.at[n]) for n, (src, dst) in enumerate(pairs)]
    for copy in copies:
        copy.start()
    for copy in copies[:3]:
        copy.wait()
    _, _, c = place()
    top = c == 0
    bed = elev[...]
    fric = friction(rough[...])
    bed_x = jnp.maximum(bed, right_of(bed))
    bed_y = jnp.maximum(bed, below(bed))
    end = ROWS - 1
    last_row = lax.broadcasted_iota(jnp.int32, (ROWS, COLS), 0) == end
    terrain[0] = jnp.where(top, bed[:HALF], bed[HALF:])
    terrain[1] = jnp.where(top, fric[:HALF], fric[HALF:])
    terrain[2] = jnp.zeros((HALF, COLS), F32)
    terrain[2, 0:1, :] = jnp.where(top, bed[HALF : HALF + 1], bed[HALF - 1 : HALF])
    terrain[2, 1:2, :] = jnp.where(top, fric[HALF : HALF + 1], fric[HALF - 1 : HALF])
    lane = lax.broadcasted_iota(jnp.int32, (1, COLS), 1)
    at = 2 * lax.axis_index("dom")
    names = jnp.where(lane == at, anc[0].astype(F32), 0.0) + jnp.where(lane == at + 1, anc[1].astype(F32), 0.0)
    kept[6] = jnp.zeros((HALF, COLS), F32)
    given[6] = jnp.zeros((HALF, COLS), F32)
    kept[6, 4:5, :] = names
    given[6, 4:5, :] = names

    def edge(row, upper, lower):
        keep[row // 2, row % 2 : row % 2 + 1, :] = jnp.where(top, upper, lower)
        if row < 6:
            give[row // 2, row % 2 : row % 2 + 1, :] = jnp.where(top, lower, upper)

    zero = jnp.zeros((1, COLS), F32)
    edge(6, bed[:1], bed[end:])
    edge(7, fric[:1], fric[end:])
    for p in range(2):
        for copy in copies[3 + 4 * p : 7 + 4 * p]:
            copy.wait()
        h0 = depth[p] * wet[p].astype(F32)
        qx, qy = xf[p], yf[p]
        edge(p, h0[:1], h0[end:])
        edge(4 + p, zero, qy[end:])
        eta = bed + h0
        qx = x_faces(qx, eta, bed_x, fric)
        qy = jnp.where(last_row, 0.0, flux(qy, eta, below(eta), bed_y, fric))
        h1 = h0 + RATIO * ((left_of(qx) - qx) + (above(qy) - qy))
        edge(2 + p, h1[:1], h1[end:])
        for f, v in enumerate((h1, qx, qy)):
            kept[3 * p + f] = jnp.where(top, v[:HALF], v[HALF:])
            given[3 * p + f] = jnp.where(top, v[HALF:], v[:HALF])
        kept[6, p : p + 1, :] = jnp.where(top, h1[HALF : HALF + 1], h1[HALF - 1 : HALF])
        given[6, p : p + 1, :] = jnp.where(top, h1[HALF - 1 : HALF], h1[HALF : HALF + 1])
        kept[6, 2 + p : 3 + p, :] = jnp.where(top, zero, qy[HALF - 1 : HALF])
        given[6, 2 + p : 3 + p, :] = jnp.where(top, qy[HALF - 1 : HALF], zero)


def second_kernel(own, far, terrain, mine, next_slab, o0, o1, o2, o3, rows, packed):
    z, y, c = place()
    top = c == 0
    slab = lax.axis_index("rows")
    bed, fric = terrain[0], terrain[1]
    bed_in, fric_in = terrain[2, 0:1, :], terrain[2, 1:2, :]
    row = lax.broadcasted_iota(jnp.int32, (HALF, COLS), 0)
    first, last = row == 0, row == HALF - 1
    at_edge = jnp.where(top, 0, HALF - 1)
    lower_edge = jnp.where(top, -1, HALF - 1)
    grid_end = jnp.where(slab == 7, lower_edge, -1)

    def rows_of(n, a, b):
        rows[n] = jnp.zeros((HALF, COLS), F32)
        rows[n, 0:2, :] = a
        rows[n, 2:4, :] = b
        return rows[n]

    in_h = rows_of(0, own[6, 0:2, :], far[6, 0:2, :])
    in_q = rows_of(1, own[6, 2:4, :], far[6, 2:4, :])
    out_h0 = rows_of(2, next_slab[4], next_slab[0])
    out_h1 = rows_of(3, next_slab[5], next_slab[1])
    out_q = rows_of(4, next_slab[6], next_slab[2])
    my_h = rows_of(5, mine[0], mine[4])
    my_q = rows_of(6, mine[2], mine[6])
    bed_out, fric_out = next_slab[3, 0:1, :], next_slab[3, 1:2, :]
    bed_mine = jnp.where(top, bed[:1], bed[HALF - 1 :])
    eta_mine, eta_out = bed_mine + my_h, bed_out + out_h0
    q1 = flux(
        jnp.where(top, out_q, my_q),
        jnp.where(top, eta_out, eta_mine),
        jnp.where(top, eta_mine, eta_out),
        jnp.maximum(bed_mine, bed_out),
        jnp.where(top, fric_out, fric[HALF - 1 :]),
    )
    q1 = jnp.where(jnp.where(top, slab, 7 - slab) == 0, 0.0, q1)
    out_h = out_h1 + jnp.where(top, -RATIO, RATIO) * q1
    bed_up, fric_up = jnp.where(top, bed_out, bed_in), jnp.where(top, fric_out, fric_in)
    bed_dn = jnp.where(top, bed_in, bed_out)
    eta_up = bed_up + jnp.where(top, out_h, in_h)
    eta_dn = bed_dn + jnp.where(top, in_h, out_h)
    q_up = jnp.where(top, q1, in_q)
    levels = []
    rows[7] = jnp.zeros((HALF, COLS), F32)
    for p in range(4):
        ref, n = (own, 3 * p) if p < 2 else (far, 3 * p - 6)
        q = q1[p : p + 1]
        h1 = ref[n] + jnp.where(row == at_edge, jnp.where(top, RATIO, -RATIO) * q, 0.0)
        qy1 = jnp.where(row == lower_edge, q, ref[n + 2])
        rows[7, p : p + 1, :] = bed[:1] + h1[:1]
        levels.append((h1, ref[n + 1], qy1))
    q2 = flux(q_up, eta_up, rows[7], jnp.maximum(bed_up, bed[:1]), fric_up)
    q2 = jnp.where(2 * slab + c == 0, 0.0, q2)
    bed_x = jnp.maximum(bed, right_of(bed))
    bed_y = jnp.maximum(bed, jnp.where(last, bed_dn, below(bed)))
    fields = []
    for p, (h1, qx, qy) in enumerate(levels):
        eta = bed + h1
        qx = x_faces(qx, eta, bed_x, fric)
        qy = flux(qy, eta, jnp.where(last, eta_dn[p : p + 1], below(eta)), bed_y, fric)
        qy = jnp.where(row == grid_end, 0.0, qy)
        over = jnp.where(first, q2[p : p + 1], above(qy))
        fields.append((h1 + RATIO * ((left_of(qx) - qx) + (over - qy)), qx, qy))
    low, even = masks()
    for f in range(3):
        for t in range(NT):
            a = [fields[p][f][:, 128 * t : 128 * t + 128] for p in range(4)]
            b0, b2 = jnp.where(low, a[0], pltpu.roll(a[2], 4, 0)), jnp.where(low, pltpu.roll(a[0], 4, 0), a[2])
            b1, b3 = jnp.where(low, a[1], pltpu.roll(a[3], 4, 0)), jnp.where(low, pltpu.roll(a[1], 4, 0), a[3])
            pair = [
                jnp.where(even, b0, pltpu.roll(b1, 2, 0)),
                jnp.where(even, pltpu.roll(b0, 6, 0), b1),
                jnp.where(even, b2, pltpu.roll(b3, 2, 0)),
                jnp.where(even, pltpu.roll(b2, 6, 0), b3),
            ]
            for d in range(4):
                n = AT[(d, f, t)]
                packed[n // PER, n % PER] = pair[d]
    names = own[6, 4:5, 0:128] + far[6, 4:5, 0:128]
    for k, out in enumerate((o0, o1, o2, o3)):
        for j in range(4):
            out[PER * j : PER * j + PER] = packed[chunk_at(z, y, role_of(c), k, j, LATE_Z, STEP_Y)]
        out[4 * PER] = jnp.zeros((8, 128), F32)
        out[4 * PER, 0:1, :] = names


def masks():
    sub = lax.broadcasted_iota(jnp.int32, (8, 128), 0)
    return sub < 4, (sub & 2) == 0


def select_kernel(codes, m0, m1, m2, m3, t0, t1, t2, t3, o0, o1, o2, o3, held):
    z, y, c = place()
    for n, refs in enumerate(((m0, m1, m2, m3), (t0, t1, t2, t3))):
        for j, ref in enumerate(refs):
            held[n, 4 * PER * j : 4 * PER * j + 4 * PER] = ref[: 4 * PER]
    for k, out in enumerate((o0, o1, o2, o3)):
        for j in range(4):
            at = chunk_at(z, y, role_of(c), k, j)
            dest = ((at >> 2) << 3) | ((at & 3) << 1) | c
            for u in range(2):
                for n in range(2):
                    code = codes[64 * n + 2 * dest + u]
                    v = pl.multiple_of(code & 6, 2)
                    row = 4 * n + 2 * u
                    out[PER * j : PER * j + PER, row : row + 2, :] = held[n, pl.ds(code >> 3, PER), pl.ds(v, 2), :]


def codes_of(names):
    z, y, c = place()
    dz, late_dz = (step_of(steps, (names >> 4) ^ z) for steps in (STEP_Z, LATE_Z))
    dy, early_dy = (step_of(steps, ((names >> 2) & 3) ^ y) for steps in (STEP_Y, EARLY_Y))
    codes = []
    for n in range(2):
        core = c ^ n
        base = jnp.where(role_of(core) == 0, dy * 4 + dz, late_dz * 4 + early_dy) * PER
        codes.append(base * 8 + (((names >> 1) & 1) ^ core) * 4 + (names & 1) * 2)
    return jnp.concatenate(codes)


def last_kernel(f0, f1, f2, f3, ho, xo, yo, packed, done, sems):
    z, y, c = place()
    low, even = masks()
    for j, ref in enumerate((f0, f1, f2, f3)):
        for k in range(4):
            packed[pl.ds(chunk_at(z, y, role_of(c), k, j) * PER, PER)] = ref[PER * k : PER * k + PER]
    copies = []
    for f, target in enumerate((ho, xo, yo)):
        out = done.at[f]
        for t in range(NT):
            cols = slice(128 * t, 128 * t + 128)
            pair = [packed[AT[(d, f, t)]] for d in range(4)]
            for n in range(2):
                rows = pl.ds(pl.multiple_of((c ^ n) * HALF, HALF), HALF)
                if n == 0:
                    b0 = jnp.where(low, pair[0], pltpu.roll(pair[2], 4, 0))
                    b1 = jnp.where(low, pair[1], pltpu.roll(pair[3], 4, 0))
                else:
                    b0 = jnp.where(low, pltpu.roll(pair[0], 4, 0), pair[2])
                    b1 = jnp.where(low, pltpu.roll(pair[1], 4, 0), pair[3])
                out[0, rows, cols] = jnp.where(even, b0, pltpu.roll(b1, 2, 0))
                out[1, rows, cols] = jnp.where(even, pltpu.roll(b0, 6, 0), b1)
        copies.append(pltpu.make_async_copy(out, target, sems.at[f]))
        copies[f].start()
    for copy in copies:
        copy.wait()


def tiles(n):
    return jax.ShapeDtypeStruct((n, 8, 128), F32)


def params():
    return pltpu.CompilerParams(vmem_limit_bytes=32 * 1024 * 1024)


def swap(v, by_role):
    pairs = [(8 * d + r, 8 * (d ^ by_role[(d ^ r ^ 1) & 1]) + r) for d in range(32) for r in range(8)]
    return lax.ppermute(v, ("dom", "rows"), pairs)


def outer_step(v, k):
    return v if k == 0 else swap(v, (STEP_Z[k] << 3, EARLY_Y[k] << 1))


def inner_step(v, k, inner_z=LAST_Z, inner_y=LAST_Y):
    return v if k == 0 else swap(v, (inner_y[k] << 1, inner_z[k] << 3))


def other_core(v):
    return lax.ppermute(v, "dom", [(i, i ^ 1) for i in range(32)])


def next_slab(v):
    low = [((2 * chip + 1) * 8 + r, 2 * chip * 8 + (r + 1) % 8) for chip in range(16) for r in range(8)]
    return lax.ppermute(v, ("dom", "rows"), low + [(b, a) for a, b in low])


def regroup(parts, count):
    return [jnp.concatenate([p[count * j : count * j + count] for p in parts]) for j in range(4)]


def shards(depth, x_flow, y_flow, elevation, roughness, wet, ancestors):
    state = jax.ShapeDtypeStruct((2, ROWS, COLS), F32)
    strip = jax.ShapeDtypeStruct((4, 2, COLS), F32)
    halves = jax.ShapeDtypeStruct((7, HALF, COLS), F32)
    ground = jax.ShapeDtypeStruct((3, HALF, COLS), F32)
    args = (depth, x_flow, y_flow, wet, elevation, roughness, ancestors)
    keep, give, kept, given, terrain = pl.pallas_call(
        first_kernel,
        out_shape=[strip, jax.ShapeDtypeStruct((3, 2, COLS), F32), halves, halves, ground],
        in_specs=[HBM] * 7,
        out_specs=[VMEM] * 5,
        scratch_shapes=[pltpu.VMEM(v.shape, v.dtype) for v in args[:6]]
        + [pltpu.SMEM((2,), jnp.int32), pltpu.SemaphoreType.DMA((11,))],
        compiler_params=params(),
    )(*[pltpu.with_memory_space_constraint(v, pltpu.HBM) for v in args])
    mine = jnp.concatenate([keep, other_core(give)])
    far = other_core(given)
    arrived = next_slab(mine)
    parts = pl.pallas_call(
        second_kernel,
        out_shape=[tiles(4 * PER + 1)] * 4,
        in_specs=[VMEM] * 5,
        out_specs=[VMEM] * 4,
        scratch_shapes=[pltpu.VMEM((8, HALF, COLS), F32), pltpu.VMEM((16, PER, 8, 128), F32)],
        compiler_params=params(),
    )(kept, far, terrain, mine, arrived)
    parts = [outer_step(v, k) for k, v in enumerate(parts)]
    names = (parts[0][4 * PER] + parts[1][4 * PER]) + (parts[2][4 * PER] + parts[3][4 * PER])
    parts = [jnp.concatenate([v, names[None]]) for v in regroup(parts, PER)]
    parts = [inner_step(v, k, LATE_Z, STEP_Y) for k, v in enumerate(parts)]
    names = sum(v[4 * PER, 0, :64] for v in parts).astype(jnp.int32)
    others = [other_core(v) for v in parts]
    parts = pl.pallas_call(
        select_kernel,
        out_shape=[tiles(4 * PER)] * 4,
        in_specs=[SMEM] + [VMEM] * 8,
        out_specs=[VMEM] * 4,
        scratch_shapes=[pltpu.VMEM((2, 16 * PER, 8, 128), F32)],
        compiler_params=params(),
    )(codes_of(names), *parts, *others)
    parts = [outer_step(v, k) for k, v in enumerate(parts)]
    parts = [inner_step(v, k) for k, v in enumerate(regroup(parts, PER))]
    return tuple(
        pl.pallas_call(
            last_kernel,
            out_shape=[state] * 3,
            in_specs=[VMEM] * 4,
            out_specs=[HBM] * 3,
            scratch_shapes=[
                pltpu.VMEM((16 * PER, 8, 128), F32),
                pltpu.VMEM((3, 2, ROWS, COLS), F32),
                pltpu.SemaphoreType.DMA((3,)),
            ],
            compiler_params=params(),
        )(*parts)
    )


def solution(mesh):
    wide = P("dom", "rows", None)
    in_specs = (wide, wide, wide, P("rows", None), P("rows", None), wide, P("dom"))
    return jax.shard_map(shards, mesh=mesh, in_specs=in_specs, out_specs=(wide, wide, wide), check_vma=False)
```
